32 devices in a mesh: dp: 8 (over z, core), ctx: 4 (over y, x).
Axes of the slice: x: 2, y: 2, z: 4, core: 2. Of those that a mesh axis runs over, the one named last changes fastest.
Arguments:
- tokens: bfloat16 [8, 512, 2048], P('dp', 'ctx'), may hold values from -6 to 6
- cotangent: bfloat16 [8, 512, 2048], P('dp', 'ctx'), may hold values from -6 to 6
- pair_index: int32 [4], replicated, may hold values from 0 to 3, each once
- norm1_gain: bfloat16 [2048], P('dp'), may hold values from 0.25 to 1.75
- norm1_bias: bfloat16 [2048], P('dp'), may hold values from -1.75 to 1.75
- norm2_gain: bfloat16 [2048], P('dp'), may hold values from 0.25 to 1.75
- norm2_bias: bfloat16 [2048], P('dp'), may hold values from -1.75 to 1.75
- w_qkv: bfloat16 [2048, 6144], P('dp'), may hold values from -0.1875 to 0.1875
- b_qkv: bfloat16 [6144], P('dp'), may hold values from -1.75 to 1.75
- w_out: bfloat16 [2048, 2048], P('dp'), may hold values from -0.375 to 0.375
- b_out: bfloat16 [2048], P('dp'), may hold values from -1.75 to 1.75
- w_up: bfloat16 [2048, 8192], P('dp'), may hold values from -0.125 to 0.125
- b_up: bfloat16 [8192], P('dp'), may hold values from -1.75 to 1.75
- w_down: bfloat16 [8192, 2048], P('dp'), may hold values from -0.0625 to 0.0625
- b_down: bfloat16 [2048], P('dp'), may hold values from -1.75 to 1.75
Outputs:
- output: bfloat16 [8, 512, 2048], P('dp', 'ctx')
- input_grad: bfloat16 [8, 512, 2048], P('dp', 'ctx')
- grad_norm1_gain: float32 [2048], P('dp')
- grad_norm1_bias: float32 [2048], P('dp')
- grad_norm2_gain: float32 [2048], P('dp')
- grad_norm2_bias: float32 [2048], P('dp')
- grad_w_qkv: float32 [2048, 6144], P('dp')
- grad_b_qkv: float32 [6144], P('dp')
- grad_w_out: float32 [2048, 2048], P('dp')
- grad_b_out: float32 [2048], P('dp')
- grad_w_up: float32 [2048, 8192], P('dp')
- grad_b_up: float32 [8192], P('dp')
- grad_w_down: float32 [8192, 2048], P('dp')
- grad_b_down: float32 [2048], P('dp')
The draws below stay inside these ranges and needn't reach their ends.
Inputs may be any that keep to these rules, and one draw needn't show every extreme that they name: A permutation: index c of ctx holds the blocks pair_index[c] and 7 - pair_index[c] of the 8 blocks of 64 tokens of every sequence.
All inputs are finite; a program needn't handle non-finite values.
Results may differ from the reference program's by a relative error of at most 0.018.
Values may be sent and summed in bfloat16 or wider, within the bound.
A program may use at most 512 MiB of HBM per device.

```python
import jax
import jax.numpy as jnp
from jax import lax

D = 2048
FF = 8192
H = 8
DH = 256
ROT = 64
TOK_CTX = 128
SEQS = 8
LEN = 512
N_CTX = 4


def with_spikes(values, own_key, source, target, blocks, factor):
    owner, partner = [(jnp.arange(values.shape[dim]) // (values.shape[dim] // blocks)).reshape([-1 if axis == dim else 1 for axis in range(values.ndim)]) for dim in (source, target)]
    chosen = jax.random.permutation(own_key, blocks)[partner]
    strong = (owner == chosen) | (owner == (partner + blocks // 2) % blocks)
    return jnp.where(strong, factor * values, values)


def shard_levels(rng, dims, split, low, largest):
    loudness, own = 1.0, jax.random.fold_in(rng, 6)
    for position, parts in split:
        steps = jnp.exp(jax.random.uniform(jax.random.fold_in(own, position), (parts,), jnp.float32, low / len(split), largest / len(split)))
        loudness = loudness * jnp.repeat(steps, dims[position] // parts).reshape([-1 if axis == position else 1 for axis in range(len(dims))])
    return loudness


def bell_draw(key, shape, deviation, bound, pieces=(), kind=jnp.bfloat16):
    values = deviation * jax.random.normal(key, shape, jnp.float32)
    if pieces:
        values = values * shard_levels(key, shape, pieces, -0.22, 0.18)
    return jnp.clip(values, -bound, bound).astype(kind)


def heavy_noise(own_key, dims, scale, bound, cuts, heavy, held_as=jnp.bfloat16):
    entries = scale * jax.random.normal(own_key, dims, jnp.float32)
    if cuts:
        entries = entries * shard_levels(own_key, dims, cuts, -0.22, 0.18)
    return jnp.clip(with_spikes(entries, jax.random.fold_in(own_key, 3), *heavy), -bound, bound).astype(held_as)


def setup_inputs(seed: int = 0) -> dict:
    key_list = jax.random.split(jax.random.key(seed), 16)
    return {
        "tokens": heavy_noise(key_list[0], (SEQS, LEN, D), 1.0, 6.0, ((0, 8), (1, 4)), (0, 2, 8, 2.0)),
        "cotangent": heavy_noise(key_list[1], (SEQS, LEN, D), 1.0, 6.0, ((0, 8), (1, 4)), (0, 2, 8, 2.0)),
        "pair_index": jax.random.permutation(key_list[2], N_CTX).astype(jnp.int32),
        "norm1_gain": jnp.clip(1.0 + 0.15 * jax.random.normal(key_list[3], (D,), jnp.float32), 0.25, 1.75).astype(jnp.bfloat16),
        "norm1_bias": bell_draw(key_list[4], (D,), 0.3, 1.75, ((0, 8),)),
        "norm2_gain": jnp.clip(1.0 + 0.15 * jax.random.normal(key_list[5], (D,), jnp.float32), 0.25, 1.75).astype(jnp.bfloat16),
        "norm2_bias": bell_draw(key_list[6], (D,), 0.3, 1.75, ((0, 8),)),
        "w_qkv": bell_draw(key_list[7], (D, 3 * D), (D // 2) ** -0.5, 0.1875, ((0, 8),)),
        "b_qkv": bell_draw(key_list[8], (3 * D,), 0.3, 1.75, ((0, 8),)),
        "w_out": bell_draw(key_list[9], (D, D), (D // 8) ** -0.5, 0.375, ((0, 8),)),
        "b_out": bell_draw(key_list[10], (D,), 0.3, 1.75, ((0, 8),)),
        "w_up": bell_draw(key_list[11], (D, FF), D ** -0.5, 0.125, ((0, 8),)),
        "b_up": bell_draw(key_list[12], (FF,), 0.3, 1.75, ((0, 8),)),
        "w_down": bell_draw(key_list[13], (FF, D), FF ** -0.5, 0.0625, ((0, 8),)),
        "b_down": bell_draw(key_list[14], (D,), 0.3, 1.75, ((0, 8),)),
    }


EPS_NORM = 1e-05
ROPE_BASE = 10000.0
MASK_FILL = -1000000000.0

@jax.custom_vjp
def low(v):
    return lax.optimization_barrier(v.astype(jnp.bfloat16)).astype(jnp.float32)

@jax.custom_vjp
def low_back(v):
    return v

def low_keep(v):
    return (low(v), None)

def low_pass(kept, grad):
    return (grad,)

def back_keep(v):
    return (v, None)

def back_low(kept, grad):
    return (low(grad),)
low.defvjp(low_keep, low_pass)
low_back.defvjp(back_keep, back_low)

def matmul_hi(left, right):
    return jnp.dot(left, right, precision=lax.Precision.HIGHEST, preferred_element_type=jnp.float32)

def layer_norm(values_in, gain_vec, offset):
    centre = values_in - lax.optimization_barrier(jnp.mean(values_in, axis=-1, keepdims=True))
    spread = lax.optimization_barrier(jnp.mean(centre * centre, axis=-1, keepdims=True))
    return centre * lax.rsqrt(spread + EPS_NORM) * gain_vec + offset

def positions(pair_index, tok_count):
    ranks_total = pair_index.shape[0]
    half_len = tok_count // 2
    index_all = jnp.arange(ranks_total * tok_count, dtype=jnp.int32)
    owner_rank = index_all // tok_count
    within = index_all % tok_count
    match_table = owner_rank[:, None] == jnp.arange(ranks_total, dtype=jnp.int32)[None, :]
    first_block = lax.optimization_barrier(jnp.sum(jnp.where(match_table, pair_index[None, :], 0), axis=1)).astype(jnp.int32)
    block_id = jnp.where(within < half_len, first_block, 2 * ranks_total - 1 - first_block)
    return (block_id * half_len + within % half_len).astype(jnp.int32)

def rotary(head_vals, token_place, turn_sign):
    half_rot = ROT // 2
    frequency = ROPE_BASE ** (-2.0 * jnp.arange(half_rot, dtype=jnp.float32) / ROT)
    angles = token_place.astype(jnp.float32)[:, None] * frequency[None, :]
    cosine = jnp.cos(angles)[:, None, :]
    sine_part = turn_sign * jnp.sin(angles)[:, None, :]
    first_half = head_vals[..., :half_rot]
    second = head_vals[..., half_rot:ROT]
    return jnp.concatenate([first_half * cosine - second * sine_part, second * cosine + first_half * sine_part, head_vals[..., ROT:]], axis=-1)

def attention(queries, key_heads, values, token_place):
    seq_len = queries.shape[0]
    block_rows = min(512, seq_len)
    block_count = seq_len // block_rows
    score_scale = DH ** (-0.5)

    def one_block(inputs):
        query_block, query_place = inputs
        scores = jnp.einsum('qhd,khd->hqk', query_block, key_heads, precision=lax.Precision.HIGHEST) * score_scale
        scores = low_back(scores)
        scores = jnp.where(token_place[None, None, :] <= query_place[None, :, None], scores, MASK_FILL)
        row_max = lax.optimization_barrier(jnp.max(scores, axis=-1, keepdims=True))
        exponent = jnp.exp(scores - row_max)
        attn_prob = low(exponent / lax.optimization_barrier(jnp.sum(exponent, axis=-1, keepdims=True)))
        return jnp.einsum('hqk,khd->qhd', attn_prob, values, precision=lax.Precision.HIGHEST)
    blocks = lax.map(jax.checkpoint(one_block), (queries.reshape(block_count, block_rows, H, DH), token_place.reshape(block_count, block_rows)))
    return blocks.reshape(seq_len, H, DH)

def forward(values_in, token_place, params):
    norm1_gain, norm1_bias, norm2_gain, norm2_bias, w_qkv, b_qkv, w_out, b_out, w_up, b_up, w_down, b_down = params
    seq_len = values_in.shape[0]
    normed_attn = low(layer_norm(values_in, norm1_gain, norm1_bias))
    normed_mlp = low(layer_norm(values_in, norm2_gain, norm2_bias))
    projected = low_back(matmul_hi(normed_attn, w_qkv) + b_qkv)
    queries = low(rotary(projected[:, :D].reshape(seq_len, H, DH), token_place, 1.0))
    key_heads = low(rotary(projected[:, D:2 * D].reshape(seq_len, H, DH), token_place, 1.0))
    values = low(projected[:, 2 * D:].reshape(seq_len, H, DH))
    attn_mixed = attention(queries, key_heads, values, token_place).reshape(seq_len, D)
    attn_mixed = low(low_back(attn_mixed))
    attn_branch = matmul_hi(attn_mixed, w_out) + b_out
    hidden_pre = low_back(matmul_hi(normed_mlp, w_up) + b_up)
    hidden = low(jax.nn.gelu(hidden_pre, approximate=False))
    mlp_branch = matmul_hi(hidden, w_down) + b_down
    return values_in + attn_branch + mlp_branch

def reference(tokens, cotangent, pair_index, norm1_gain, norm1_bias, norm2_gain, norm2_bias, w_qkv, b_qkv, w_out, b_out, w_up, b_up, w_down, b_down):
    params = tuple((member.astype(jnp.float32) for member in (norm1_gain, norm1_bias, norm2_gain, norm2_bias, w_qkv, b_qkv, w_out, b_out, w_up, b_up, w_down, b_down)))
    token_place = positions(pair_index, TOK_CTX)

    def one_sequence(totals, inputs):
        seq_tokens, seq_cotangent = inputs
        result, pullback = jax.vjp(lambda values_in, weights: forward(values_in, token_place, weights), seq_tokens.astype(jnp.float32), params)
        grad_in, grad_params = pullback(seq_cotangent.astype(jnp.float32))
        totals = jax.tree.map(lambda summed, addend: summed + addend, totals, grad_params)
        return (totals, (result.astype(jnp.bfloat16), grad_in.astype(jnp.bfloat16)))
    zero_grads = tuple((jnp.zeros_like(member) for member in params))
    totals, (output, input_grad) = lax.scan(one_sequence, zero_grads, (tokens, cotangent))
    return (output, input_grad, totals[0], totals[1], totals[2], totals[3], totals[4], totals[5], totals[6], totals[7], totals[8], totals[9], totals[10], totals[11])
```

```python
import jax
import jax.numpy as jnp
from jax import lax
from jax.experimental import pallas as pl
from jax.experimental.pallas import tpu as pltpu
from jax.sharding import PartitionSpec as P

H = 8
DH = 256
ROT = 64


EPS_NORM = 1e-05
ROPE_BASE = 10000.0
MASK_FILL = -1000000000.0


def shortened(x):

    def short(part):
        return part.astype(jnp.bfloat16) if part.dtype == jnp.float32 else part

    return jax.tree.map(short, x)


def layer_norm(values_in, gain_vec, offset):
    centre = values_in - jnp.mean(values_in, axis=-1, keepdims=True)
    spread = jnp.mean(centre * centre, axis=-1, keepdims=True)
    return centre * lax.rsqrt(spread + EPS_NORM) * gain_vec + offset


def norm_grads(values_in, gain_vec, offset, upstream):
    unused, pullback = jax.vjp(layer_norm, values_in, gain_vec, offset)
    return pullback(upstream)


def positions(pair_index, tok_count):
    ranks_total = pair_index.shape[0]
    half_len = tok_count // 2
    index_all = jnp.arange(ranks_total * tok_count, dtype=jnp.int32)
    owner_rank = index_all // tok_count
    within = index_all % tok_count
    match_table = owner_rank[:, None] == jnp.arange(ranks_total, dtype=jnp.int32)[None, :]
    first_block = jnp.sum(jnp.where(match_table, pair_index[None, :], 0), axis=1)
    block_id = jnp.where(within < half_len, first_block, 2 * ranks_total - 1 - first_block)
    return block_id * half_len + within % half_len


def rotary(head_vals, token_place, turn_sign):
    half_rot = ROT // 2
    frequency = ROPE_BASE ** (-2.0 * jnp.arange(half_rot, dtype=jnp.float32) / ROT)
    angles = token_place.astype(jnp.float32)[:, None] * frequency[None, :]
    cosine = jnp.cos(angles)[:, None, :]
    sine_part = turn_sign * jnp.sin(angles)[:, None, :]
    first_half = head_vals[..., :half_rot]
    second = head_vals[..., half_rot:ROT]
    return jnp.concatenate(
        [
            first_half * cosine - second * sine_part,
            second * cosine + first_half * sine_part,
            head_vals[..., ROT:],
        ],
        axis=-1,
    )


def contract_rows(left, right):
    return lax.dot_general(
        left, right, (((0,), (0,)), ((), ())), preferred_element_type=jnp.float32
    )


def contract_cols(left, right):
    return lax.dot_general(
        left, right, (((1,), (1,)), ((), ())), preferred_element_type=jnp.float32
    )


def plain_local(
    tokens,
    cotangent,
    pair_index,
    norm1_gain,
    norm1_bias,
    norm2_gain,
    norm2_bias,
    w_qkv,
    b_qkv,
    w_out,
    b_out,
    w_up,
    b_up,
    w_down,
    b_down,
):
    seq_dev, tok_count, width = tokens.shape
    row_count = seq_dev * tok_count
    head_shape = (seq_dev, tok_count, H, DH)
    score_scale = DH ** (-0.5)
    device_rank = lax.axis_index("ctx")
    all_place = positions(pair_index, tok_count)
    own_place = lax.dynamic_slice_in_dim(all_place, device_rank * tok_count, tok_count)
    allowed = all_place[None, None, None, :] <= own_place[None, None, :, None]
    gathered = (
        lax.all_gather(norm1_gain, "dp", axis=0, tiled=True),
        lax.all_gather(norm1_bias, "dp", axis=0, tiled=True),
        lax.all_gather(norm2_gain, "dp", axis=0, tiled=True),
        lax.all_gather(norm2_bias, "dp", axis=0, tiled=True),
        lax.all_gather(w_qkv, "dp", axis=0, tiled=True),
        lax.all_gather(b_qkv, "dp", axis=0, tiled=True),
        lax.all_gather(w_out, "dp", axis=0, tiled=True),
        lax.all_gather(b_out, "dp", axis=0, tiled=True),
        lax.all_gather(w_up, "dp", axis=0, tiled=True),
        lax.all_gather(b_up, "dp", axis=0, tiled=True),
        lax.all_gather(w_down, "dp", axis=0, tiled=True),
        lax.all_gather(b_down, "dp", axis=0, tiled=True),
    )
    (
        attn_gain,
        attn_shift,
        mlp_gain,
        mlp_shift,
        qkv_weight,
        qkv_bias,
        out_weight,
        out_bias,
        up_weight,
        up_bias,
        down_weight,
        down_bias,
    ) = gathered
    token_rows = tokens.reshape(row_count, width).astype(jnp.float32)
    normed_attn = layer_norm(
        token_rows, attn_gain.astype(jnp.float32), attn_shift.astype(jnp.float32)
    ).astype(jnp.bfloat16)
    normed_mlp = layer_norm(
        token_rows, mlp_gain.astype(jnp.float32), mlp_shift.astype(jnp.float32)
    ).astype(jnp.bfloat16)
    projected = jnp.dot(
        normed_attn, qkv_weight, preferred_element_type=jnp.float32
    ) + qkv_bias.astype(jnp.float32)
    queries = rotary(projected[:, :width].reshape(head_shape), own_place, 1.0).astype(jnp.bfloat16)
    key_local = (
        rotary(projected[:, width : 2 * width].reshape(head_shape), own_place, 1.0)
        .astype(jnp.bfloat16)
        .reshape(seq_dev, tok_count, width)
    )
    value_local = projected[:, 2 * width :].astype(jnp.bfloat16).reshape(seq_dev, tok_count, width)
    key_all, value_all = (
        lax.all_gather(key_local, "ctx", axis=1, tiled=True),
        lax.all_gather(value_local, "ctx", axis=1, tiled=True),
    )
    seq_len = key_all.shape[1]
    key_heads = key_all.reshape(seq_dev, seq_len, H, DH)
    value_heads = value_all.reshape(seq_dev, seq_len, H, DH)
    raw_scores = (
        jnp.einsum("sqhd,skhd->shqk", queries, key_heads, preferred_element_type=jnp.float32)
        * score_scale
    )
    raw_scores = jnp.where(allowed, raw_scores, MASK_FILL)
    row_max = jnp.max(raw_scores, axis=-1, keepdims=True)
    exponent = jnp.exp(raw_scores - row_max)
    row_total = jnp.sum(exponent, axis=-1, keepdims=True)
    log_norm = row_max + jnp.log(row_total)
    prob_low = (exponent / row_total).astype(jnp.bfloat16)
    attn_mixed = (
        jnp.einsum("shqk,skhd->sqhd", prob_low, value_heads, preferred_element_type=jnp.float32)
        .reshape(row_count, width)
        .astype(jnp.bfloat16)
    )
    attn_branch = jnp.dot(
        attn_mixed, out_weight, preferred_element_type=jnp.float32
    ) + out_bias.astype(jnp.float32)
    hidden_pre = jnp.dot(
        normed_mlp, up_weight, preferred_element_type=jnp.float32
    ) + up_bias.astype(jnp.float32)
    hidden = jax.nn.gelu(hidden_pre, approximate=False).astype(jnp.bfloat16)
    mlp_branch = jnp.dot(
        hidden, down_weight, preferred_element_type=jnp.float32
    ) + down_bias.astype(jnp.float32)
    output = (token_rows + attn_branch + mlp_branch).astype(jnp.bfloat16).reshape(tokens.shape)
    attn_gain, mlp_gain, qkv_weight, out_weight, up_weight, down_weight = (
        lax.all_gather(norm1_gain, "dp", axis=0, tiled=True),
        lax.all_gather(norm2_gain, "dp", axis=0, tiled=True),
        lax.all_gather(w_qkv, "dp", axis=0, tiled=True),
        lax.all_gather(w_out, "dp", axis=0, tiled=True),
        lax.all_gather(w_up, "dp", axis=0, tiled=True),
        lax.all_gather(w_down, "dp", axis=0, tiled=True),
    )
    grad_rows = cotangent.reshape(row_count, width)
    grad_wide = grad_rows.astype(jnp.float32)
    hidden_grad = contract_cols(grad_rows, down_weight)
    unused, gelu_pull = jax.vjp(
        lambda pre_value: jax.nn.gelu(pre_value, approximate=False), hidden_pre
    )
    pre_grad = gelu_pull(hidden_grad)[0].astype(jnp.bfloat16)
    normed_mlp_grad = contract_cols(pre_grad, up_weight)
    mlp_in_grad, mlp_gain_grad, mlp_shift_grad = norm_grads(
        token_rows, mlp_gain.astype(jnp.float32), mlp_shift.astype(jnp.float32), normed_mlp_grad
    )
    mlp_terms = (
        contract_rows(normed_mlp, pre_grad),
        jnp.sum(pre_grad.astype(jnp.float32), axis=0),
        contract_rows(hidden, grad_rows),
        jnp.sum(grad_wide, axis=0),
        mlp_gain_grad,
        mlp_shift_grad,
    )
    mlp_shares = (
        lax.psum_scatter(
            mlp_terms[0].astype(jnp.bfloat16), "dp", scatter_dimension=0, tiled=True
        ).astype(jnp.float32),
        lax.psum_scatter(
            mlp_terms[1].astype(jnp.bfloat16), "dp", scatter_dimension=0, tiled=True
        ).astype(jnp.float32),
        lax.psum_scatter(
            mlp_terms[2].astype(jnp.bfloat16), "dp", scatter_dimension=0, tiled=True
        ).astype(jnp.float32),
        lax.psum_scatter(
            mlp_terms[3].astype(jnp.bfloat16), "dp", scatter_dimension=0, tiled=True
        ).astype(jnp.float32),
        lax.psum_scatter(
            mlp_terms[4].astype(jnp.bfloat16), "dp", scatter_dimension=0, tiled=True
        ).astype(jnp.float32),
        lax.psum_scatter(
            mlp_terms[5].astype(jnp.bfloat16), "dp", scatter_dimension=0, tiled=True
        ).astype(jnp.float32),
    )
    mixed_grad = contract_cols(grad_rows, out_weight).astype(jnp.bfloat16).reshape(head_shape)
    again_scores = (
        jnp.einsum("sqhd,skhd->shqk", queries, key_heads, preferred_element_type=jnp.float32)
        * score_scale
    )
    again_scores = jnp.where(allowed, again_scores, MASK_FILL)
    attn_prob = jnp.exp(again_scores - log_norm)
    prob_again = attn_prob.astype(jnp.bfloat16)
    prob_grad = jnp.einsum(
        "sqhd,skhd->shqk", mixed_grad, value_heads, preferred_element_type=jnp.float32
    )
    row_dot = jnp.sum(prob_grad * attn_prob, axis=-1, keepdims=True)
    score_grad = (attn_prob * (prob_grad - row_dot)).astype(jnp.bfloat16)
    query_grad = (
        jnp.einsum("shqk,skhd->sqhd", score_grad, key_heads, preferred_element_type=jnp.float32)
        * score_scale
    )
    key_part = (
        jnp.einsum("shqk,sqhd->skhd", score_grad, queries, preferred_element_type=jnp.float32)
        * score_scale
    ).reshape(seq_dev, seq_len, width)
    value_part = jnp.einsum(
        "shqk,sqhd->skhd", prob_again, mixed_grad, preferred_element_type=jnp.float32
    ).reshape(seq_dev, seq_len, width)
    key_grad, value_grad = (
        lax.psum_scatter(
            key_part.astype(jnp.bfloat16), "ctx", scatter_dimension=1, tiled=True
        ).astype(jnp.float32),
        lax.psum_scatter(
            value_part.astype(jnp.bfloat16), "ctx", scatter_dimension=1, tiled=True
        ).astype(jnp.float32),
    )
    query_back = rotary(query_grad, own_place, -1.0).reshape(row_count, width)
    key_back = rotary(key_grad.reshape(head_shape), own_place, -1.0).reshape(row_count, width)
    proj_grad = jnp.concatenate(
        [query_back, key_back, value_grad.reshape(row_count, width)], axis=1
    ).astype(jnp.bfloat16)
    normed_attn_grad = contract_cols(proj_grad, qkv_weight)
    attn_in_grad, attn_gain_grad, attn_shift_grad = norm_grads(
        token_rows, attn_gain.astype(jnp.float32), attn_shift.astype(jnp.float32), normed_attn_grad
    )
    input_grad = (grad_wide + mlp_in_grad + attn_in_grad).astype(jnp.bfloat16).reshape(tokens.shape)
    attn_terms = (
        contract_rows(normed_attn, proj_grad),
        jnp.sum(proj_grad.astype(jnp.float32), axis=0),
        contract_rows(attn_mixed, grad_rows),
        attn_gain_grad,
        attn_shift_grad,
    )
    attn_shares = (
        lax.psum_scatter(
            attn_terms[0].astype(jnp.bfloat16), "dp", scatter_dimension=0, tiled=True
        ).astype(jnp.float32),
        lax.psum_scatter(
            attn_terms[1].astype(jnp.bfloat16), "dp", scatter_dimension=0, tiled=True
        ).astype(jnp.float32),
        lax.psum_scatter(
            attn_terms[2].astype(jnp.bfloat16), "dp", scatter_dimension=0, tiled=True
        ).astype(jnp.float32),
        lax.psum_scatter(
            attn_terms[3].astype(jnp.bfloat16), "dp", scatter_dimension=0, tiled=True
        ).astype(jnp.float32),
        lax.psum_scatter(
            attn_terms[4].astype(jnp.bfloat16), "dp", scatter_dimension=0, tiled=True
        ).astype(jnp.float32),
    )
    summed = jax.tree.map(
        lambda part: part.astype(jnp.float32), lax.psum(shortened(mlp_shares + attn_shares), "ctx")
    )
    (
        up_total,
        up_bias_total,
        down_total,
        bias_total,
        mlp_gain_total,
        mlp_shift_total,
        qkv_total,
        qkv_bias_total,
        out_total,
        attn_gain_total,
        attn_shift_total,
    ) = summed
    return (
        output,
        input_grad,
        attn_gain_total,
        attn_shift_total,
        mlp_gain_total,
        mlp_shift_total,
        qkv_total,
        qkv_bias_total,
        out_total,
        bias_total,
        up_total,
        up_bias_total,
        down_total,
        bias_total,
    )


PLANES = 4


def hop_line(part, step, first):
    planes = [z for z in range(PLANES) if 0 <= z + step < PLANES]
    planes = [z for z in planes if (z if step > 0 else PLANES - 1 - z) >= first]
    pairs = [(2 * z + k, 2 * (z + step) + k) for z in planes for k in range(2)]
    return lax.ppermute(part, "dp", pairs)


def hop_plane(part, shift):
    pairs = [(2 * z + k, 2 * ((z + shift) % PLANES) + k) for z in range(PLANES) for k in range(2)]
    return lax.ppermute(part, "dp", pairs)


def hop_core(part):
    return lax.ppermute(part, "dp", [(d, d ^ 1) for d in range(2 * PLANES)])


def hop_ctx(part, flip):
    return lax.ppermute(part, "ctx", [(c, c ^ flip) for c in range(4)])


def pick(stacked, index):
    return lax.dynamic_index_in_dim(stacked, index, 0, keepdims=False)


def in_order(bit, mine, other):
    return jnp.stack([jnp.where(bit == 0, mine, other), jnp.where(bit == 0, other, mine)])


def line_scatter(blocks, z):
    def block(index):
        return pick(blocks, jnp.clip(index, 0, PLANES - 1)).astype(jnp.float32)

    total = block(z)
    for step in (1, -1):
        flow = None
        for ahead in (3, 2, 1):
            own = block(z + step * ahead)
            flow = own if flow is None else own + flow.astype(jnp.float32)
            planes = [p for p in range(PLANES) if 0 <= p + step * ahead < PLANES]
            pairs = [(2 * p + k, 2 * (p + step) + k) for p in planes for k in range(2)]
            flow = lax.ppermute(flow.astype(jnp.bfloat16), "dp", pairs)
        total = total + flow.astype(jnp.float32)
    return total


def core_sum(parts, k):
    low = parts.astype(jnp.bfloat16)
    return pick(low, k).astype(jnp.float32) + hop_core(pick(low, 1 - k)).astype(jnp.float32)


def hop_pair(part):
    pairs = []
    for z in range(PLANES):
        for x in range(2):
            one, two = (2 * z) * 4 + 2 + x, (2 * z + 1) * 4 + x
            pairs += [(one, two), (two, one)]
    return lax.ppermute(part, ("dp", "ctx"), pairs)


def dp_exchange(parts, z, core):
    split = parts.reshape((PLANES, 2) + parts.shape[1:])
    got = [pick(split, z)]
    for shift in range(1, PLANES):
        got.append(hop_plane(pick(split, (z + shift) % PLANES), shift))
    stacked = jnp.stack([got[0], got[3], got[2], got[1]])
    lined = jnp.concatenate([stacked, stacked])
    lined = lax.dynamic_slice_in_dim(lined, (PLANES - z) % PLANES, PLANES)
    mine = lax.dynamic_index_in_dim(lined, core, 1, keepdims=False)
    away = lax.dynamic_index_in_dim(lined, 1 - core, 1, keepdims=False)
    both = in_order(core, mine, hop_core(away))
    return jnp.swapaxes(both, 0, 1).reshape(parts.shape)


MESH_ID = pl.DeviceIdType.MESH


def gather_kernel(
    x_in,
    g_in,
    up_in,
    qkv_in,
    small_in,
    x_out,
    g_out,
    up_out,
    qkv_out,
    small_out,
    line_send,
    line_recv,
    side_send,
    side_recv,
    pair_send,
    core_send,
    core_recv,
    w_send,
    w_recv,
    wx_send,
    wx_recv,
    wy_send,
    wy_recv,
    wc_send,
    wc_recv,
    small_send,
    small_recv,
    local_sem,
):
    dp = lax.axis_index("dp")
    rank = lax.axis_index("ctx")
    z, k = dp // 2, dp % 2
    y, x = rank // 2, rank % 2
    core_to = (2 * z + 1 - k, rank)
    x_to = (dp, 2 * y + 1 - x)
    y_to = (dp, 2 * (1 - y) + x)
    pair_to = (2 * z + 1 - k, 2 * (1 - y) + x)
    ff_part = up_out.shape[2]
    dh = qkv_out.shape[2] // 3

    barrier = pltpu.get_barrier_semaphore()
    for target in (core_to, x_to, y_to, pair_to):
        pl.semaphore_signal(barrier, inc=1, device_id=target, device_id_type=MESH_ID)
    for shift in range(1, PLANES):
        for c in range(2):
            target = (2 * lax.rem(z + shift, PLANES) + c, rank)
            pl.semaphore_signal(barrier, inc=1, device_id=target, device_id_type=MESH_ID)
    pl.semaphore_wait(barrier, 4 + 2 * (PLANES - 1))

    def remote(src, dst, send, recv, target):
        return pltpu.make_async_remote_copy(
            src_ref=src,
            dst_ref=dst,
            send_sem=send,
            recv_sem=recv,
            device_id=target,
            device_id_type=MESH_ID,
        )

    arrays = ((g_in, g_out), (x_in, x_out))
    mine = 2 * k + x
    theirs = 2 * k + 1 - x
    sends = []

    def start(copy, when=None):
        if when is None:
            copy.start()
        else:
            pl.when(when)(copy.start)
        sends.append((when, copy))

    same = k == y
    for a, (src, dst) in enumerate(arrays):
        pair = remote(src, dst.at[z, 2 * y + x], pair_send.at[a], line_recv.at[a, z], pair_to)
        local = pltpu.make_async_copy(src, dst.at[z, mine], local_sem.at[a])
        pl.when(jnp.logical_not(same))(pair.start)
        pl.when(same)(local.start)

    small_local = pltpu.make_async_copy(small_in, small_out.at[dp], local_sem.at[2])
    small_local.start()
    small_copies = []
    for n, (shift, c) in enumerate([(s, c) for s in range(PLANES) for c in range(2)][1:]):
        target = (2 * lax.rem(z + shift, PLANES) + lax.rem(k + c, 2), rank)
        copy = remote(
            small_in, small_out.at[dp], small_send.at[n], small_recv.at[n], target
        )
        copy.start()
        small_copies.append(copy)

    for a, (src, dst) in enumerate(arrays):
        pair = remote(src, dst.at[z, mine], pair_send.at[a], line_recv.at[a, z], pair_to)
        local = pltpu.make_async_copy(src, dst.at[z, mine], local_sem.at[a])
        pl.when(jnp.logical_not(same))(pair.wait_recv)
        pl.when(same)(local.wait)

    quarter = up_in.shape[0] // 4
    half = up_in.shape[0] // 2
    own_copies = []
    core_copies = []

    def up_cols(target):
        return up_in.at[:, pl.ds(pl.multiple_of(target * ff_part, 128), ff_part)]

    def qkv_cols(target, section):
        first = section * qkv_in.shape[1] // 3
        return qkv_in.at[:, pl.ds(pl.multiple_of(first + target * dh, 128), dh)]

    own_copies.append(pltpu.make_async_copy(up_cols(dp), up_out.at[dp], local_sem.at[3]))
    core_copies.append(
        remote(up_cols(2 * z + 1 - k), up_out.at[dp], wc_send.at[0], wc_recv.at[0], core_to)
    )
    for section in range(3):
        columns = pl.ds(section * dh, dh)
        own_copies.append(
            pltpu.make_async_copy(
                qkv_cols(dp, section), qkv_out.at[dp, :, columns], local_sem.at[4 + section]
            )
        )
        core_copies.append(
            remote(
                qkv_cols(2 * z + 1 - k, section),
                qkv_out.at[dp, :, columns],
                wc_send.at[1 + section],
                wc_recv.at[1 + section],
                core_to,
            )
        )
    for copy in own_copies:
        copy.start()

    def carry(a, plane, when, along):
        dst = arrays[a][1]
        block = dst.at[plane, mine]
        if along in (0, 1):
            start(
                remote(block, block, line_send.at[a, 0, plane], line_recv.at[a, plane], (dp + 2, rank)),
                jnp.logical_and(when, z < PLANES - 1),
            )
        if along in (0, -1):
            start(
                remote(block, block, line_send.at[a, 1, plane], line_recv.at[a, plane], (dp - 2, rank)),
                jnp.logical_and(when, z > 0),
            )
        start(remote(block, block, side_send.at[a, plane], side_recv.at[a, plane], x_to), when)
        start(
            remote(block, block, core_send.at[a, 0, plane], core_recv.at[a, 0, plane], core_to), when
        )

    def arrived(a, plane, when):
        block = arrays[a][1].at[plane, mine]
        copy = remote(block, block, line_send.at[a, 0, plane], line_recv.at[a, plane], core_to)
        pl.when(when)(copy.wait_recv)

    def side_on(a, plane, when):
        block = arrays[a][1].at[plane, theirs]
        copy = remote(block, block, side_send.at[a, plane], side_recv.at[a, plane], core_to)
        pl.when(when)(copy.wait_recv)
        start(
            remote(block, block, core_send.at[a, 1, plane], core_recv.at[a, 1, plane], core_to), when
        )

    always = z >= 0
    for a in range(2):
        carry(a, z, always, 0)

    w_copies = []
    up_rows = pl.ds(pl.multiple_of(rank * quarter, 16), quarter)
    qkv_rows = pl.ds(pl.multiple_of(y * half, 16), half)
    for shift in range(1, PLANES):
        plane = lax.rem(z + shift, PLANES)
        for c in range(2):
            target = (2 * plane + c, rank)
            columns = pl.ds(pl.multiple_of(target[0] * ff_part, 128), ff_part)
            w_copies.append(
                remote(
                    up_in.at[up_rows, columns],
                    up_out.at[dp, up_rows],
                    w_send.at[shift - 1, c, 0],
                    w_recv.at[shift - 1, k, 0],
                    target,
                )
            )
            for section in range(3):
                first = section * qkv_in.shape[1] // 3
                columns = pl.ds(pl.multiple_of(first + target[0] * dh, 128), dh)
                w_copies.append(
                    remote(
                        qkv_in.at[qkv_rows, columns],
                        qkv_out.at[dp, qkv_rows, pl.ds(section * dh, dh)],
                        w_send.at[shift - 1, c, 1 + section],
                        w_recv.at[shift - 1, k, 1 + section],
                        target,
                    )
                )
    for copy in w_copies:
        copy.start()
    for copy in core_copies:
        copy.start()

    def w_arrive(shift, c, part):
        source = 2 * lax.rem(z - shift + PLANES, PLANES) + c
        if part == 0:
            dst = up_out.at[source, up_rows]
        else:
            dst = qkv_out.at[source, qkv_rows, pl.ds((part - 1) * dh, dh)]
        remote(dst, dst, w_send.at[shift - 1, c, part], w_recv.at[shift - 1, c, part], core_to).wait_recv()

    def x_rows(flip):
        other = 2 * y + (1 - x if flip else x)
        return pl.ds(pl.multiple_of(other * quarter, 16), quarter)

    def pair_of(shift):
        return pl.ds(2 * lax.rem(z - shift + PLANES, PLANES), 2)

    def share_weights(shift):
        for c in range(2):
            for part in range(4):
                w_arrive(shift, c, part)
        block = up_out.at[pair_of(shift), up_rows]
        start(remote(block, block, wx_send.at[shift - 1], wx_recv.at[shift - 1], x_to))
        start(remote(block, block, wy_send.at[shift - 1, 0], wy_recv.at[shift - 1, 0], y_to))
        block = qkv_out.at[pair_of(shift), qkv_rows]
        start(remote(block, block, wy_send.at[shift - 1, 2], wy_recv.at[shift - 1, 2], y_to))

    def share_side_weights(shift):
        block = up_out.at[pair_of(shift), x_rows(True)]
        remote(block, block, wx_send.at[shift - 1], wx_recv.at[shift - 1], x_to).wait_recv()
        start(remote(block, block, wy_send.at[shift - 1, 1], wy_recv.at[shift - 1, 1], y_to))

    for step in range(1, PLANES):
        for a in range(2):
            for along in (1, -1):
                plane = z - along * step
                there = jnp.logical_and(plane >= 0, plane < PLANES)
                plane = lax.rem(plane + PLANES, PLANES)
                arrived(a, plane, there)
                carry(a, plane, there, along)
        if step == 1:
            for a in range(2):
                side_on(a, z, always)
        else:
            for a in range(2):
                for along in (1, -1):
                    plane = z - along * (step - 1)
                    there = jnp.logical_and(plane >= 0, plane < PLANES)
                    side_on(a, lax.rem(plane + PLANES, PLANES), there)
        if step > 1:
            share_weights(step - 1)
        if step > 2:
            share_side_weights(step - 2)
    for a in range(2):
        for along in (1, -1):
            plane = z - along * (PLANES - 1)
            there = jnp.logical_and(plane >= 0, plane < PLANES)
            side_on(a, lax.rem(plane + PLANES, PLANES), there)
    share_weights(3)
    share_side_weights(2)
    share_side_weights(3)

    for shift in range(1, PLANES):
        other_y = 2 * (1 - y)
        for n, other in enumerate((other_y + x, other_y + 1 - x)):
            block = up_out.at[pair_of(shift), pl.ds(pl.multiple_of(other * quarter, 16), quarter)]
            remote(block, block, wy_send.at[shift - 1, n], wy_recv.at[shift - 1, n], y_to).wait_recv()
        block = qkv_out.at[pair_of(shift), pl.ds(pl.multiple_of((1 - y) * half, 16), half)]
        remote(block, block, wy_send.at[shift - 1, 2], wy_recv.at[shift - 1, 2], y_to).wait_recv()
    for a in range(2):
        for plane in range(PLANES):
            for n, side in enumerate((x, 1 - x)):
                block = arrays[a][1].at[plane, 2 * (1 - k) + side]
                remote(
                    block, block, core_send.at[a, n, plane], core_recv.at[a, n, plane], core_to
                ).wait_recv()
    for n, (shift, c) in enumerate([(s, c) for s in range(PLANES) for c in range(2)][1:]):
        source = 2 * lax.rem(z - shift + PLANES, PLANES) + lax.rem(k + c, 2)
        remote(
            small_in, small_out.at[source], small_send.at[n], small_recv.at[n], core_to
        ).wait_recv()
    for copy in core_copies:
        copy.wait()
    for copy in own_copies:
        copy.wait()
    small_local.wait()
    for copy in small_copies + w_copies:
        copy.wait_send()
    for a, (src, dst) in enumerate(arrays):
        pair = remote(src, dst.at[z, 2 * y + x], pair_send.at[a], line_recv.at[a, z], pair_to)
        pl.when(jnp.logical_not(same))(pair.wait_send)
    for when, copy in sends:
        if when is None:
            copy.wait_send()
        else:
            pl.when(when)(copy.wait_send)


def gather_all(tokens, cotangent, w_up, w_qkv, small):
    rows, width = tokens.shape
    n_dp = 2 * PLANES
    bf16 = jnp.bfloat16
    dma = pltpu.SemaphoreType.DMA
    hbm = pl.BlockSpec(memory_space=pl.ANY)
    block = jax.ShapeDtypeStruct((PLANES, 4, rows, width), bf16)
    return pl.pallas_call(
        gather_kernel,
        out_shape=(
            block,
            block,
            jax.ShapeDtypeStruct((n_dp, w_up.shape[0], w_up.shape[1] // n_dp), bf16),
            jax.ShapeDtypeStruct((n_dp, w_qkv.shape[0], w_qkv.shape[1] // n_dp), bf16),
            jax.ShapeDtypeStruct((n_dp,) + small.shape, bf16),
        ),
        in_specs=[hbm] * 5,
        out_specs=(hbm,) * 5,
        scratch_shapes=[
            dma((2, 2, PLANES)),
            dma((2, PLANES)),
            dma((2, PLANES)),
            dma((2, PLANES)),
            dma((2,)),
            dma((2, 2, PLANES)),
            dma((2, 2, PLANES)),
            dma((3, 2, 4)),
            dma((3, 2, 4)),
            dma((3,)),
            dma((3,)),
            dma((3, 3)),
            dma((3, 3)),
            dma((4,)),
            dma((4,)),
            dma((7,)),
            dma((7,)),
            dma((7,)),
        ],
        compiler_params=pltpu.CompilerParams(collective_id=1, has_side_effects=True),
    )(tokens, cotangent, w_up, w_qkv, small)


def dot_nn(left, right):
    return jnp.dot(left, right, preferred_element_type=jnp.float32)


def half_turn(head, cosine, sine):
    first = head[:, :128]
    lane = lax.broadcasted_iota(jnp.int32, first.shape, 1)
    swapped = jnp.where(
        lane < ROT // 2, pltpu.roll(first, 128 - ROT // 2, 1), pltpu.roll(first, ROT // 2, 1)
    )
    return jnp.concatenate([first * cosine + swapped * sine, head[:, 128:]], axis=1)


def block_kernel(
    x_hbm,
    g_hbm,
    up,
    down,
    qkv,
    out_w,
    gains,
    up_bias,
    qkv_bias,
    cosine,
    sine,
    place_q,
    place_k,
    out_hbm,
    back_hbm,
    down_hbm,
    up_hbm,
    outw_hbm,
    qkv_hbm,
    vec,
    xb,
    gb,
    nm,
    na,
    nmh,
    nah,
    hid,
    prg,
    q,
    k,
    v,
    mg,
    mix,
    proj,
    mean_s,
    inv_s,
    kacc,
    vacc,
    acc_down,
    acc_up,
    acc_out,
    acc_qkv,
    stage,
    load_sem,
    store_sem,
):
    f32, bf16 = jnp.float32, jnp.bfloat16
    x = lax.axis_index("ctx") % 2
    seqs, length, width = x_hbm.shape
    ff = up.shape[1]
    row_tile = 64
    quarter = length // 4
    scale = DH ** (-0.5)

    def ds(start, size):
        return pl.ds(pl.multiple_of(start, size), size)

    def load(s, slot):
        return (
            pltpu.make_async_copy(x_hbm.at[s], xb.at[slot], load_sem.at[0, slot]),
            pltpu.make_async_copy(g_hbm.at[s], gb.at[slot], load_sem.at[1, slot]),
        )

    def stores(s):
        return (
            pltpu.make_async_copy(stage.at[0], out_hbm.at[s], store_sem.at[0]),
            pltpu.make_async_copy(stage.at[1], back_hbm.at[s], store_sem.at[1]),
        )

    for copy in load(0, 0):
        copy.start()
    for ref in (acc_down, acc_up, acc_out, acc_qkv):
        rows = ref.shape[0] // 64

        @pl.loop(0, rows)
        def clear(i, ref=ref):
            ref[ds(i * 64, 64), :] = jnp.zeros((64, ref.shape[1]), f32)

    vec[...] = jnp.zeros_like(vec)

    @pl.loop(0, seqs)
    def sequence(s):
        slot = lax.rem(s, 2)
        for copy in load(s, slot):
            copy.wait()

        @pl.when(s + 1 < seqs)
        def ahead():
            for copy in load(s + 1, 1 - slot):
                copy.start()

        @pl.loop(0, length // row_tile)
        def norm(i):
            r = ds(i * row_tile, row_tile)
            value = xb[slot, r, :].astype(f32)
            mean = jnp.mean(value, axis=1, keepdims=True)
            centre = value - mean
            inv = lax.rsqrt(jnp.mean(centre * centre, axis=1, keepdims=True) + EPS_NORM)
            hat = centre * inv
            mean_s[r, :] = mean
            inv_s[r, :] = inv
            na[r, :] = (hat * gains[0:1, :] + gains[1:2, :]).astype(bf16)
            nm[r, :] = (hat * gains[2:3, :] + gains[3:4, :]).astype(bf16)

        for d in range(width // 256):
            nmh[:, d * 128 : (d + 1) * 128] = nm[:, ds(d * 256 + x * 128, 128)]
            nah[:, d * 128 : (d + 1) * 128] = na[:, ds(d * 256 + x * 128, 128)]

        @pl.loop(0, ff // 256)
        def feed(n):
            c = ds(n * 256, 256)
            pre = dot_nn(nm[...], up[:, c]) + up_bias[:, c]
            hidden_grad = contract_cols(gb[slot], down[c, :])
            cdf = 0.5 * (1.0 + lax.erf(pre * (0.5**0.5)))
            pdf = jnp.exp(-0.5 * pre * pre) * ((2.0 * 3.141592653589793) ** -0.5)
            hid[:, c] = (pre * cdf).astype(bf16)
            prg[:, c] = (hidden_grad * (cdf + pre * pdf)).astype(bf16)

        @pl.loop(0, ff // 512)
        def gdown(m):
            r = ds(m * 256, 256)
            acc_down[r, :] += contract_rows(hid[:, ds(x * (ff // 2) + m * 256, 256)], gb[slot])

        @pl.loop(0, width // 512)
        def gup(m):
            r = ds(m * 256, 256)
            acc_up[r, :] += contract_rows(nmh[:, r], prg[...])

        for n, ref in enumerate((q, k, v)):
            part = dot_nn(na[...], qkv[:, n * DH : (n + 1) * DH]) + qkv_bias[:, n * DH : (n + 1) * DH]
            if n < 2:
                part = half_turn(part, cosine[...], sine[...])
            ref[...] = part.astype(bf16)
        mg[...] = contract_cols(gb[slot], out_w[...]).astype(bf16)
        kacc[...] = jnp.zeros_like(kacc)
        vacc[...] = jnp.zeros_like(vacc)

        @pl.loop(0, 4)
        def attend(i):
            r = ds(i * quarter, quarter)
            scores = contract_cols(q[r, :], k[...]) * scale
            scores = jnp.where(place_k[...] <= place_q[r, :], scores, MASK_FILL)
            exponent = jnp.exp(scores - jnp.max(scores, axis=1, keepdims=True))
            prob = exponent / jnp.sum(exponent, axis=1, keepdims=True)
            low = prob.astype(bf16)
            mix[r, :] = dot_nn(low, v[...]).astype(bf16)
            prob_grad = contract_cols(mg[r, :], v[...])
            row_dot = jnp.sum(prob_grad * prob, axis=1, keepdims=True)
            score_grad = (prob * (prob_grad - row_dot)).astype(bf16)
            query_grad = dot_nn(score_grad, k[...]) * scale
            proj[r, 0:DH] = half_turn(query_grad, cosine[r, :], -sine[r, :]).astype(bf16)
            kacc[...] += contract_rows(score_grad, q[r, :])
            vacc[...] += contract_rows(low, mg[r, :])

        proj[:, DH : 2 * DH] = half_turn(kacc[...] * scale, cosine[...], -sine[...]).astype(bf16)
        proj[:, 2 * DH : 3 * DH] = vacc[...].astype(bf16)
        acc_out[...] += contract_rows(mix[:, ds(x * 128, 128)], gb[slot])

        @pl.loop(0, width // 512)
        def gqkv(m):
            r = ds(m * 256, 256)
            acc_qkv[r, :] += contract_rows(nah[:, r], proj[...])

        one, two = ds(x * quarter, quarter), ds((2 + x) * quarter, quarter)

        def picked(ref):
            return jnp.concatenate([ref[one, :], ref[two, :]], axis=0)

        @pl.when(s > 0)
        def stored():
            for copy in stores(s - 1):
                copy.wait()

        hid_rows, prg_rows = picked(hid), picked(prg)
        mix_rows, proj_rows = picked(mix), picked(proj)
        mean_rows, inv_rows = picked(mean_s), picked(inv_s)

        @pl.loop(0, width // 256)
        def followers(n):
            c = ds(n * 256, 256)
            out = dot_nn(picked(hid), down[:, c]) + dot_nn(picked(mix), out_w[:, c])
            stage[0, 0, :, c] = out[:quarter].astype(bf16)
            stage[0, 1, :, c] = out[quarter:].astype(bf16)
            mlp_back = contract_cols(picked(prg), up[c, :])
            attn_back = contract_cols(picked(proj), qkv[c, :])
            rows = jnp.concatenate([xb[slot, one, c], xb[slot, two, c]], axis=0).astype(f32)
            hat = (rows - picked(mean_s)) * picked(inv_s)
            back = attn_back * gains[0:1, c] + mlp_back * gains[2:3, c]
            stage[1, 0, :, c] = back[:quarter].astype(bf16)
            stage[1, 1, :, c] = back[quarter:].astype(bf16)
            grad = jnp.concatenate([gb[slot, one, c], gb[slot, two, c]], axis=0).astype(f32)
            sums = (attn_back * hat, attn_back, mlp_back * hat, mlp_back, grad)
            for n_sum, term in enumerate(sums):
                vec[n_sum : n_sum + 1, c] += jnp.sum(term, axis=0, keepdims=True)

        vec[5:6, 0 : 3 * DH] += jnp.sum(picked(proj).astype(f32), axis=0, keepdims=True)
        vec[6:7, 0:ff] += jnp.sum(picked(prg).astype(f32), axis=0, keepdims=True)
        for copy in stores(s):
            copy.start()

    for copy in stores(seqs - 1):
        copy.wait()

    copies = []
    for ref, buf, target, rows in (
        (acc_down, xb.at[0], down_hbm, 512),
        (acc_up, xb.at[1], up_hbm, 512),
        (acc_qkv, gb.at[0], qkv_hbm, 512),
        (acc_out, gb.at[1], outw_hbm, 128),
    ):
        cols = ref.shape[1]
        for piece in range(ref.shape[0] // rows):

            @pl.loop(0, rows // 64)
            def rounded(i, ref=ref, buf=buf, piece=piece, rows=rows, cols=cols):
                buf[ds(i * 64, 64), piece * cols : (piece + 1) * cols] = ref[
                    ds(piece * rows + i * 64, 64), :
                ].astype(bf16)

            copy = pltpu.make_async_copy(
                buf.at[0:rows, piece * cols : (piece + 1) * cols],
                target.at[piece * rows : (piece + 1) * rows],
                store_sem.at[2 + len(copies)],
            )
            copy.start()
            copies.append(copy)
    for copy in copies:
        copy.wait()


def block_compute(x_all, g_all, up_cols, w_down, qkv_cols, w_out, gains, up_bias, qkv_bias, place):
    f32, bf16 = jnp.float32, jnp.bfloat16
    seqs, length, width = x_all.shape
    ff = up_cols.shape[1]
    tok = length // 4
    half_rot = ROT // 2
    frequency = ROPE_BASE ** (-2.0 * jnp.arange(half_rot, dtype=f32) / ROT)
    angles = place.astype(f32)[:, None] * frequency[None, :]
    rest = jnp.zeros((length, 128 - ROT), f32)
    cosine = jnp.concatenate([jnp.cos(angles), jnp.cos(angles), rest + 1.0], axis=1)
    sine = jnp.concatenate([-jnp.sin(angles), jnp.sin(angles), rest], axis=1)
    hbm = pl.BlockSpec(memory_space=pl.ANY)
    vmem = pl.BlockSpec(memory_space=pltpu.VMEM)

    def shape(*dims, dtype=bf16):
        return jax.ShapeDtypeStruct(dims, dtype)

    def buf(*dims, dtype=bf16):
        return pltpu.VMEM(dims, dtype)

    return pl.pallas_call(
        block_kernel,
        out_shape=(
            shape(seqs, 2, tok, width),
            shape(seqs, 2, tok, width),
            shape(ff // 2, width),
            shape(width // 2, ff),
            shape(DH // 2, width),
            shape(width // 2, 3 * DH),
            shape(8, width, dtype=f32),
        ),
        in_specs=[hbm, hbm] + [vmem] * 11,
        out_specs=(hbm,) * 6 + (vmem,),
        scratch_shapes=[
            buf(2, length, width),
            buf(2, length, width),
            buf(length, width),
            buf(length, width),
            buf(length, width // 2),
            buf(length, width // 2),
            buf(length, ff),
            buf(length, ff),
            buf(length, DH),
            buf(length, DH),
            buf(length, DH),
            buf(length, DH),
            buf(length, DH),
            buf(length, 3 * DH),
            buf(length, 1, dtype=f32),
            buf(length, 1, dtype=f32),
            buf(length, DH, dtype=f32),
            buf(length, DH, dtype=f32),
            buf(ff // 2, width, dtype=f32),
            buf(width // 2, ff, dtype=f32),
            buf(DH // 2, width, dtype=f32),
            buf(width // 2, 3 * DH, dtype=f32),
            buf(2, 2, tok, width),
            pltpu.SemaphoreType.DMA((2, 2)),
            pltpu.SemaphoreType.DMA((8,)),
        ],
        compiler_params=pltpu.CompilerParams(vmem_limit_bytes=62 * 2**20),
    )(
        x_all,
        g_all,
        up_cols,
        w_down,
        qkv_cols,
        w_out,
        gains,
        up_bias,
        qkv_bias,
        cosine,
        sine,
        place[:, None],
        place[None, :],
    )


def column_local(
    tokens,
    cotangent,
    pair_index,
    norm1_gain,
    norm1_bias,
    norm2_gain,
    norm2_bias,
    w_qkv,
    b_qkv,
    w_out,
    b_out,
    w_up,
    b_up,
    w_down,
    b_down,
):
    bf16, f32 = jnp.bfloat16, jnp.float32
    tok_count, width = tokens.shape[1:]
    n_dp = H
    dp_rank = lax.axis_index("dp")
    rank = lax.axis_index("ctx")
    z, core = dp_rank // 2, dp_rank % 2
    y, x = rank // 2, rank % 2
    part = width // n_dp
    ff_part = w_up.shape[1] // n_dp
    qkv_part = 3 * DH
    seq_len = 4 * tok_count
    place = positions(pair_index, tok_count)

    small = jnp.concatenate(
        [norm1_gain, norm1_bias, norm2_gain, norm2_bias, b_out, b_down, b_qkv]
    ).reshape(-1, part)
    small = jnp.pad(small, ((0, -small.shape[0] % 16), (0, 0)))
    x_all, g_all, up_cols, qkv_cols, small_all = gather_all(
        tokens[0], cotangent[0], w_up, w_qkv, small
    )
    up_cols = up_cols.reshape(width, ff_part)
    qkv_cols = qkv_cols.reshape(width, qkv_part)
    vectors = [small_all[:, i].reshape(width).astype(f32) for i in range(6)]
    gain1, shift1, gain2, shift2, out_bias, down_bias = vectors
    qkv_bias_all = small_all[:, 6:9].reshape(3, H, DH).astype(f32)
    qkv_bias = lax.dynamic_index_in_dim(qkv_bias_all, dp_rank, 1, keepdims=False).reshape(qkv_part)

    gains = jnp.stack([gain1, shift1, gain2, shift2] * 2)
    out_part, back_part, grad_down, grad_up, grad_out, grad_qkv, vec = block_compute(
        x_all.reshape(PLANES, seq_len, width),
        g_all.reshape(PLANES, seq_len, width),
        up_cols,
        w_down,
        qkv_cols,
        w_out,
        gains,
        b_up.astype(f32)[None],
        qkv_bias[None],
        place,
    )

    def to_owner(parts):
        return line_scatter(core_sum(jnp.swapaxes(parts, 0, 1), core), z)

    def home(block):
        low = block.astype(bf16)
        return jnp.where(core == y, low, hop_pair(low)).astype(f32)

    out_sum = home(to_owner(out_part.reshape(PLANES, 2, tok_count, width)))
    own_rows = tokens[0].astype(f32)
    output = (own_rows + out_sum + out_bias + down_bias).astype(bf16)[None]

    own_head = (jnp.arange(n_dp) == dp_rank).astype(f32)[:, None]
    vector_parts = jnp.concatenate(
        [vec[i].reshape(n_dp, part) for i in range(4)]
        + [
            (vec[5, :qkv_part].reshape(3, 1, DH) * own_head[None]).reshape(n_dp, -1),
            vec[4].reshape(n_dp, part) * own_head,
            vec[6, :ff_part][None] * own_head,
        ],
        axis=1,
    )
    vector_len = vector_parts.shape[1]
    vector_rows = jnp.pad(vector_parts, ((0, 0), (0, -vector_len % width)))
    vector_rows = vector_rows.reshape(PLANES, 2, -1, width)
    back_mine = to_owner(jnp.concatenate([back_part, vector_rows], axis=2))
    vector_mine = back_mine[tok_count:].reshape(-1)[:vector_len]
    back_sum = home(back_mine[:tok_count])
    vector_row = vector_mine + hop_ctx(vector_mine, 1)
    vector_total = vector_row + hop_ctx(vector_row, 2)
    own_centre = own_rows - jnp.mean(own_rows, axis=-1, keepdims=True)
    own_inv = lax.rsqrt(jnp.mean(own_centre * own_centre, axis=-1, keepdims=True) + EPS_NORM)
    own_hat = own_centre * own_inv
    norm_back = (
        back_sum
        - jnp.mean(back_sum, axis=-1, keepdims=True)
        - own_hat * jnp.mean(back_sum * own_hat, axis=-1, keepdims=True)
    ) * own_inv
    input_grad = (cotangent[0].astype(f32) + norm_back).astype(bf16)[None]

    def over_y(low):
        return (low.astype(f32) + hop_ctx(low, 2).astype(f32)).astype(bf16)

    def row_total(grad):
        low = over_y(grad)
        return in_order(x, low, hop_ctx(low, 1)).reshape(-1, grad.shape[1]).astype(f32)

    def column_total(grad):
        low = dp_exchange(over_y(grad).reshape(n_dp, part // 2, -1), z, core)
        return in_order(x, low, hop_ctx(low, 1))

    down_total = row_total(grad_down)
    out_total = row_total(grad_out)
    up_total = column_total(grad_up).transpose(0, 2, 1, 3).reshape(part, -1).astype(f32)
    qkv_total = column_total(grad_qkv).reshape(2, n_dp, part // 2, 3, DH)
    qkv_total = qkv_total.transpose(0, 2, 3, 1, 4).reshape(part, -1).astype(f32)

    cuts = [part, 2 * part, 3 * part, 4 * part, 4 * part + b_qkv.shape[0]]
    cuts.append(cuts[-1] + part)
    pieces = jnp.split(vector_total, cuts)
    gain1_total, shift1_total, gain2_total, shift2_total, qkv_bias_total, bias_total, up_bias_total = pieces
    return (
        output,
        input_grad,
        gain1_total,
        shift1_total,
        gain2_total,
        shift2_total,
        qkv_total,
        qkv_bias_total,
        out_total,
        bias_total,
        up_total,
        up_bias_total,
        down_total,
        bias_total,
    )


def solution(mesh):
    local = column_local if mesh.shape["dp"] == H and mesh.shape["ctx"] == 4 else plain_local
    placed = (
        P("dp", "ctx", None),
        P("dp", "ctx", None),
        P(),
        P("dp"),
        P("dp"),
        P("dp"),
        P("dp"),
        P("dp", None),
        P("dp"),
        P("dp", None),
        P("dp"),
        P("dp", None),
        P("dp"),
        P("dp", None),
        P("dp"),
    )
    return jax.shard_map(
        local,
        mesh=mesh,
        in_specs=placed,
        out_specs=(
            P("dp", "ctx", None),
            P("dp", "ctx", None),
            P("dp"),
            P("dp"),
            P("dp"),
            P("dp"),
            P("dp", None),
            P("dp"),
            P("dp", None),
            P("dp"),
            P("dp", None),
            P("dp"),
            P("dp", None),
            P("dp"),
        ),
        check_vma=False,
    )
```

```python
import functools

import jax
import jax.numpy as jnp
from jax import lax
from jax.experimental import pallas as pl
from jax.experimental.pallas import tpu as pltpu
from jax.sharding import PartitionSpec as P

H = 8
DH = 256
ROT = 64


EPS_NORM = 1e-05
ROPE_BASE = 10000.0
MASK_FILL = -1000000000.0


def shortened(x):

    def short(part):
        return part.astype(jnp.bfloat16) if part.dtype == jnp.float32 else part

    return jax.tree.map(short, x)


def layer_norm(values_in, gain_vec, offset):
    centre = values_in - jnp.mean(values_in, axis=-1, keepdims=True)
    spread = jnp.mean(centre * centre, axis=-1, keepdims=True)
    return centre * lax.rsqrt(spread + EPS_NORM) * gain_vec + offset


def norm_grads(values_in, gain_vec, offset, upstream):
    unused, pullback = jax.vjp(layer_norm, values_in, gain_vec, offset)
    return pullback(upstream)


def positions(pair_index, tok_count):
    ranks_total = pair_index.shape[0]
    half_len = tok_count // 2
    index_all = jnp.arange(ranks_total * tok_count, dtype=jnp.int32)
    owner_rank = index_all // tok_count
    within = index_all % tok_count
    match_table = owner_rank[:, None] == jnp.arange(ranks_total, dtype=jnp.int32)[None, :]
    first_block = jnp.sum(jnp.where(match_table, pair_index[None, :], 0), axis=1)
    block_id = jnp.where(within < half_len, first_block, 2 * ranks_total - 1 - first_block)
    return block_id * half_len + within % half_len


def rotary(head_vals, token_place, turn_sign):
    half_rot = ROT // 2
    frequency = ROPE_BASE ** (-2.0 * jnp.arange(half_rot, dtype=jnp.float32) / ROT)
    angles = token_place.astype(jnp.float32)[:, None] * frequency[None, :]
    cosine = jnp.cos(angles)[:, None, :]
    sine_part = turn_sign * jnp.sin(angles)[:, None, :]
    first_half = head_vals[..., :half_rot]
    second = head_vals[..., half_rot:ROT]
    return jnp.concatenate(
        [
            first_half * cosine - second * sine_part,
            second * cosine + first_half * sine_part,
            head_vals[..., ROT:],
        ],
        axis=-1,
    )


def contract_rows(left, right):
    return lax.dot_general(
        left, right, (((0,), (0,)), ((), ())), preferred_element_type=jnp.float32
    )


def contract_cols(left, right):
    return lax.dot_general(
        left, right, (((1,), (1,)), ((), ())), preferred_element_type=jnp.float32
    )


def plain_local(
    tokens,
    cotangent,
    pair_index,
    norm1_gain,
    norm1_bias,
    norm2_gain,
    norm2_bias,
    w_qkv,
    b_qkv,
    w_out,
    b_out,
    w_up,
    b_up,
    w_down,
    b_down,
):
    seq_dev, tok_count, width = tokens.shape
    row_count = seq_dev * tok_count
    head_shape = (seq_dev, tok_count, H, DH)
    score_scale = DH ** (-0.5)
    device_rank = lax.axis_index("ctx")
    all_place = positions(pair_index, tok_count)
    own_place = lax.dynamic_slice_in_dim(all_place, device_rank * tok_count, tok_count)
    allowed = all_place[None, None, None, :] <= own_place[None, None, :, None]
    gathered = (
        lax.all_gather(norm1_gain, "dp", axis=0, tiled=True),
        lax.all_gather(norm1_bias, "dp", axis=0, tiled=True),
        lax.all_gather(norm2_gain, "dp", axis=0, tiled=True),
        lax.all_gather(norm2_bias, "dp", axis=0, tiled=True),
        lax.all_gather(w_qkv, "dp", axis=0, tiled=True),
        lax.all_gather(b_qkv, "dp", axis=0, tiled=True),
        lax.all_gather(w_out, "dp", axis=0, tiled=True),
        lax.all_gather(b_out, "dp", axis=0, tiled=True),
        lax.all_gather(w_up, "dp", axis=0, tiled=True),
        lax.all_gather(b_up, "dp", axis=0, tiled=True),
        lax.all_gather(w_down, "dp", axis=0, tiled=True),
        lax.all_gather(b_down, "dp", axis=0, tiled=True),
    )
    (
        attn_gain,
        attn_shift,
        mlp_gain,
        mlp_shift,
        qkv_weight,
        qkv_bias,
        out_weight,
        out_bias,
        up_weight,
        up_bias,
        down_weight,
        down_bias,
    ) = gathered
    token_rows = tokens.reshape(row_count, width).astype(jnp.float32)
    normed_attn = layer_norm(
        token_rows, attn_gain.astype(jnp.float32), attn_shift.astype(jnp.float32)
    ).astype(jnp.bfloat16)
    normed_mlp = layer_norm(
        token_rows, mlp_gain.astype(jnp.float32), mlp_shift.astype(jnp.float32)
    ).astype(jnp.bfloat16)
    projected = jnp.dot(
        normed_attn, qkv_weight, preferred_element_type=jnp.float32
    ) + qkv_bias.astype(jnp.float32)
    queries = rotary(projected[:, :width].reshape(head_shape), own_place, 1.0).astype(jnp.bfloat16)
    key_local = (
        rotary(projected[:, width : 2 * width].reshape(head_shape), own_place, 1.0)
        .astype(jnp.bfloat16)
        .reshape(seq_dev, tok_count, width)
    )
    value_local = projected[:, 2 * width :].astype(jnp.bfloat16).reshape(seq_dev, tok_count, width)
    key_all, value_all = (
        lax.all_gather(key_local, "ctx", axis=1, tiled=True),
        lax.all_gather(value_local, "ctx", axis=1, tiled=True),
    )
    seq_len = key_all.shape[1]
    key_heads = key_all.reshape(seq_dev, seq_len, H, DH)
    value_heads = value_all.reshape(seq_dev, seq_len, H, DH)
    raw_scores = (
        jnp.einsum("sqhd,skhd->shqk", queries, key_heads, preferred_element_type=jnp.float32)
        * score_scale
    )
    raw_scores = jnp.where(allowed, raw_scores, MASK_FILL)
    row_max = jnp.max(raw_scores, axis=-1, keepdims=True)
    exponent = jnp.exp(raw_scores - row_max)
    row_total = jnp.sum(exponent, axis=-1, keepdims=True)
    log_norm = row_max + jnp.log(row_total)
    prob_low = (exponent / row_total).astype(jnp.bfloat16)
    attn_mixed = (
        jnp.einsum("shqk,skhd->sqhd", prob_low, value_heads, preferred_element_type=jnp.float32)
        .reshape(row_count, width)
        .astype(jnp.bfloat16)
    )
    attn_branch = jnp.dot(
        attn_mixed, out_weight, preferred_element_type=jnp.float32
    ) + out_bias.astype(jnp.float32)
    hidden_pre = jnp.dot(
        normed_mlp, up_weight, preferred_element_type=jnp.float32
    ) + up_bias.astype(jnp.float32)
    hidden = jax.nn.gelu(hidden_pre, approximate=False).astype(jnp.bfloat16)
    mlp_branch = jnp.dot(
        hidden, down_weight, preferred_element_type=jnp.float32
    ) + down_bias.astype(jnp.float32)
    output = (token_rows + attn_branch + mlp_branch).astype(jnp.bfloat16).reshape(tokens.shape)
    attn_gain, mlp_gain, qkv_weight, out_weight, up_weight, down_weight = (
        lax.all_gather(norm1_gain, "dp", axis=0, tiled=True),
        lax.all_gather(norm2_gain, "dp", axis=0, tiled=True),
        lax.all_gather(w_qkv, "dp", axis=0, tiled=True),
        lax.all_gather(w_out, "dp", axis=0, tiled=True),
        lax.all_gather(w_up, "dp", axis=0, tiled=True),
        lax.all_gather(w_down, "dp", axis=0, tiled=True),
    )
    grad_rows = cotangent.reshape(row_count, width)
    grad_wide = grad_rows.astype(jnp.float32)
    hidden_grad = contract_cols(grad_rows, down_weight)
    unused, gelu_pull = jax.vjp(
        lambda pre_value: jax.nn.gelu(pre_value, approximate=False), hidden_pre
    )
    pre_grad = gelu_pull(hidden_grad)[0].astype(jnp.bfloat16)
    normed_mlp_grad = contract_cols(pre_grad, up_weight)
    mlp_in_grad, mlp_gain_grad, mlp_shift_grad = norm_grads(
        token_rows, mlp_gain.astype(jnp.float32), mlp_shift.astype(jnp.float32), normed_mlp_grad
    )
    mlp_terms = (
        contract_rows(normed_mlp, pre_grad),
        jnp.sum(pre_grad.astype(jnp.float32), axis=0),
        contract_rows(hidden, grad_rows),
        jnp.sum(grad_wide, axis=0),
        mlp_gain_grad,
        mlp_shift_grad,
    )
    mlp_shares = (
        lax.psum_scatter(
            mlp_terms[0].astype(jnp.bfloat16), "dp", scatter_dimension=0, tiled=True
        ).astype(jnp.float32),
        lax.psum_scatter(
            mlp_terms[1].astype(jnp.bfloat16), "dp", scatter_dimension=0, tiled=True
        ).astype(jnp.float32),
        lax.psum_scatter(
            mlp_terms[2].astype(jnp.bfloat16), "dp", scatter_dimension=0, tiled=True
        ).astype(jnp.float32),
        lax.psum_scatter(
            mlp_terms[3].astype(jnp.bfloat16), "dp", scatter_dimension=0, tiled=True
        ).astype(jnp.float32),
        lax.psum_scatter(
            mlp_terms[4].astype(jnp.bfloat16), "dp", scatter_dimension=0, tiled=True
        ).astype(jnp.float32),
        lax.psum_scatter(
            mlp_terms[5].astype(jnp.bfloat16), "dp", scatter_dimension=0, tiled=True
        ).astype(jnp.float32),
    )
    mixed_grad = contract_cols(grad_rows, out_weight).astype(jnp.bfloat16).reshape(head_shape)
    again_scores = (
        jnp.einsum("sqhd,skhd->shqk", queries, key_heads, preferred_element_type=jnp.float32)
        * score_scale
    )
    again_scores = jnp.where(allowed, again_scores, MASK_FILL)
    attn_prob = jnp.exp(again_scores - log_norm)
    prob_again = attn_prob.astype(jnp.bfloat16)
    prob_grad = jnp.einsum(
        "sqhd,skhd->shqk", mixed_grad, value_heads, preferred_element_type=jnp.float32
    )
    row_dot = jnp.sum(prob_grad * attn_prob, axis=-1, keepdims=True)
    score_grad = (attn_prob * (prob_grad - row_dot)).astype(jnp.bfloat16)
    query_grad = (
        jnp.einsum("shqk,skhd->sqhd", score_grad, key_heads, preferred_element_type=jnp.float32)
        * score_scale
    )
    key_part = (
        jnp.einsum("shqk,sqhd->skhd", score_grad, queries, preferred_element_type=jnp.float32)
        * score_scale
    ).reshape(seq_dev, seq_len, width)
    value_part = jnp.einsum(
        "shqk,sqhd->skhd", prob_again, mixed_grad, preferred_element_type=jnp.float32
    ).reshape(seq_dev, seq_len, width)
    key_grad, value_grad = (
        lax.psum_scatter(
            key_part.astype(jnp.bfloat16), "ctx", scatter_dimension=1, tiled=True
        ).astype(jnp.float32),
        lax.psum_scatter(
            value_part.astype(jnp.bfloat16), "ctx", scatter_dimension=1, tiled=True
        ).astype(jnp.float32),
    )
    query_back = rotary(query_grad, own_place, -1.0).reshape(row_count, width)
    key_back = rotary(key_grad.reshape(head_shape), own_place, -1.0).reshape(row_count, width)
    proj_grad = jnp.concatenate(
        [query_back, key_back, value_grad.reshape(row_count, width)], axis=1
    ).astype(jnp.bfloat16)
    normed_attn_grad = contract_cols(proj_grad, qkv_weight)
    attn_in_grad, attn_gain_grad, attn_shift_grad = norm_grads(
        token_rows, attn_gain.astype(jnp.float32), attn_shift.astype(jnp.float32), normed_attn_grad
    )
    input_grad = (grad_wide + mlp_in_grad + attn_in_grad).astype(jnp.bfloat16).reshape(tokens.shape)
    attn_terms = (
        contract_rows(normed_attn, proj_grad),
        jnp.sum(proj_grad.astype(jnp.float32), axis=0),
        contract_rows(attn_mixed, grad_rows),
        attn_gain_grad,
        attn_shift_grad,
    )
    attn_shares = (
        lax.psum_scatter(
            attn_terms[0].astype(jnp.bfloat16), "dp", scatter_dimension=0, tiled=True
        ).astype(jnp.float32),
        lax.psum_scatter(
            attn_terms[1].astype(jnp.bfloat16), "dp", scatter_dimension=0, tiled=True
        ).astype(jnp.float32),
        lax.psum_scatter(
            attn_terms[2].astype(jnp.bfloat16), "dp", scatter_dimension=0, tiled=True
        ).astype(jnp.float32),
        lax.psum_scatter(
            attn_terms[3].astype(jnp.bfloat16), "dp", scatter_dimension=0, tiled=True
        ).astype(jnp.float32),
        lax.psum_scatter(
            attn_terms[4].astype(jnp.bfloat16), "dp", scatter_dimension=0, tiled=True
        ).astype(jnp.float32),
    )
    summed = jax.tree.map(
        lambda part: part.astype(jnp.float32), lax.psum(shortened(mlp_shares + attn_shares), "ctx")
    )
    (
        up_total,
        up_bias_total,
        down_total,
        bias_total,
        mlp_gain_total,
        mlp_shift_total,
        qkv_total,
        qkv_bias_total,
        out_total,
        attn_gain_total,
        attn_shift_total,
    ) = summed
    return (
        output,
        input_grad,
        attn_gain_total,
        attn_shift_total,
        mlp_gain_total,
        mlp_shift_total,
        qkv_total,
        qkv_bias_total,
        out_total,
        bias_total,
        up_total,
        up_bias_total,
        down_total,
        bias_total,
    )


PLANES = 4


MESH_ID = pl.DeviceIdType.MESH


def gather_kernel(
    x_in,
    g_in,
    up_in,
    qkv_in,
    small_in,
    x_out,
    g_out,
    up_out,
    qkv_out,
    small_out,
    line_send,
    line_recv,
    side_send,
    side_recv,
    pair_send,
    core_send,
    core_recv,
    w_send,
    w_recv,
    wx_send,
    wx_recv,
    wy_send,
    wy_recv,
    wc_send,
    wc_recv,
    small_send,
    small_recv,
    local_sem,
):
    dp = lax.axis_index("dp")
    rank = lax.axis_index("ctx")
    z, k = dp // 2, dp % 2
    y, x = rank // 2, rank % 2
    core_to = (2 * z + 1 - k, rank)
    x_to = (dp, 2 * y + 1 - x)
    y_to = (dp, 2 * (1 - y) + x)
    pair_to = (2 * z + 1 - k, 2 * (1 - y) + x)
    ff_part = up_out.shape[2]
    dh = qkv_out.shape[2] // 3

    barrier = pltpu.get_barrier_semaphore()
    for target in (core_to, x_to, y_to, pair_to):
        pl.semaphore_signal(barrier, inc=1, device_id=target, device_id_type=MESH_ID)
    for shift in range(1, PLANES):
        for c in range(2):
            target = (2 * lax.rem(z + shift, PLANES) + c, rank)
            pl.semaphore_signal(barrier, inc=1, device_id=target, device_id_type=MESH_ID)
    pl.semaphore_wait(barrier, 4 + 2 * (PLANES - 1))

    def remote(src, dst, send, recv, target):
        return pltpu.make_async_remote_copy(
            src_ref=src,
            dst_ref=dst,
            send_sem=send,
            recv_sem=recv,
            device_id=target,
            device_id_type=MESH_ID,
        )

    arrays = ((g_in, g_out), (x_in, x_out))
    mine = 2 * k + x
    theirs = 2 * k + 1 - x
    sends = []

    def start(copy, when=None):
        if when is None:
            copy.start()
        else:
            pl.when(when)(copy.start)
        sends.append((when, copy))

    same = k == y
    for a, (src, dst) in enumerate(arrays):
        pair = remote(src, dst.at[z, 2 * y + x], pair_send.at[a], line_recv.at[a, z], pair_to)
        local = pltpu.make_async_copy(src, dst.at[z, mine], local_sem.at[a])
        pl.when(jnp.logical_not(same))(pair.start)
        pl.when(same)(local.start)

    small_local = pltpu.make_async_copy(small_in, small_out.at[dp], local_sem.at[2])
    small_local.start()
    small_copies = []
    for n, (shift, c) in enumerate([(s, c) for s in range(PLANES) for c in range(2)][1:]):
        target = (2 * lax.rem(z + shift, PLANES) + lax.rem(k + c, 2), rank)
        copy = remote(
            small_in, small_out.at[dp], small_send.at[n], small_recv.at[n], target
        )
        copy.start()
        small_copies.append(copy)

    def own_arrived(a):
        src, dst = arrays[a]
        pair = remote(src, dst.at[z, mine], pair_send.at[a], line_recv.at[a, z], pair_to)
        local = pltpu.make_async_copy(src, dst.at[z, mine], local_sem.at[a])
        pl.when(jnp.logical_not(same))(pair.wait_recv)
        pl.when(same)(local.wait)

    quarter = up_in.shape[0] // 4
    half = up_in.shape[0] // 2
    own_copies = []
    core_copies = []

    def up_cols(target):
        return up_in.at[:, pl.ds(pl.multiple_of(target * ff_part, 128), ff_part)]

    def qkv_cols(target, section):
        first = section * qkv_in.shape[1] // 3
        return qkv_in.at[:, pl.ds(pl.multiple_of(first + target * dh, 128), dh)]

    own_copies.append(pltpu.make_async_copy(up_cols(dp), up_out.at[dp], local_sem.at[3]))
    core_copies.append(
        remote(up_cols(2 * z + 1 - k), up_out.at[dp], wc_send.at[0], wc_recv.at[0], core_to)
    )
    for section in range(3):
        columns = pl.ds(section * dh, dh)
        own_copies.append(
            pltpu.make_async_copy(
                qkv_cols(dp, section), qkv_out.at[dp, :, columns], local_sem.at[4 + section]
            )
        )
        core_copies.append(
            remote(
                qkv_cols(2 * z + 1 - k, section),
                qkv_out.at[dp, :, columns],
                wc_send.at[1 + section],
                wc_recv.at[1 + section],
                core_to,
            )
        )
    def carry(a, plane, when, along):
        dst = arrays[a][1]
        block = dst.at[plane, mine]
        if along in (0, 1):
            start(
                remote(block, block, line_send.at[a, 0, plane], line_recv.at[a, plane], (dp + 2, rank)),
                jnp.logical_and(when, z < PLANES - 1),
            )
        if along in (0, -1):
            start(
                remote(block, block, line_send.at[a, 1, plane], line_recv.at[a, plane], (dp - 2, rank)),
                jnp.logical_and(when, z > 0),
            )
        start(remote(block, block, side_send.at[a, plane], side_recv.at[a, plane], x_to), when)
        start(
            remote(block, block, core_send.at[a, 0, plane], core_recv.at[a, 0, plane], core_to), when
        )

    def arrived(a, plane, when):
        block = arrays[a][1].at[plane, mine]
        copy = remote(block, block, line_send.at[a, 0, plane], line_recv.at[a, plane], core_to)
        pl.when(when)(copy.wait_recv)

    def side_on(a, plane, when):
        block = arrays[a][1].at[plane, theirs]
        copy = remote(block, block, side_send.at[a, plane], side_recv.at[a, plane], core_to)
        pl.when(when)(copy.wait_recv)
        start(
            remote(block, block, core_send.at[a, 1, plane], core_recv.at[a, 1, plane], core_to), when
        )

    always = z >= 0
    up_copies = []
    qkv_copies = []
    up_rows = pl.ds(pl.multiple_of(rank * quarter, 16), quarter)
    qkv_rows = pl.ds(pl.multiple_of(y * half, 16), half)
    for shift in range(1, PLANES):
        plane = lax.rem(z + shift, PLANES)
        for c in range(2):
            target = (2 * plane + c, rank)
            columns = pl.ds(pl.multiple_of(target[0] * ff_part, 128), ff_part)
            up_copies.append(
                remote(
                    up_in.at[up_rows, columns],
                    up_out.at[dp, up_rows],
                    w_send.at[shift - 1, c, 0],
                    w_recv.at[shift - 1, k, 0],
                    target,
                )
            )
            for section in range(3):
                first = section * qkv_in.shape[1] // 3
                columns = pl.ds(pl.multiple_of(first + target[0] * dh, 128), dh)
                qkv_copies.append(
                    remote(
                        qkv_in.at[qkv_rows, columns],
                        qkv_out.at[dp, qkv_rows, pl.ds(section * dh, dh)],
                        w_send.at[shift - 1, c, 1 + section],
                        w_recv.at[shift - 1, k, 1 + section],
                        target,
                    )
                )

    def w_arrive(shift, c, part):
        source = 2 * lax.rem(z - shift + PLANES, PLANES) + c
        if part == 0:
            dst = up_out.at[source, up_rows]
        else:
            dst = qkv_out.at[source, qkv_rows, pl.ds((part - 1) * dh, dh)]
        remote(dst, dst, w_send.at[shift - 1, c, part], w_recv.at[shift - 1, c, part], core_to).wait_recv()

    def x_rows(flip):
        other = 2 * y + (1 - x if flip else x)
        return pl.ds(pl.multiple_of(other * quarter, 16), quarter)

    def pair_of(shift):
        return pl.ds(2 * lax.rem(z - shift + PLANES, PLANES), 2)

    def share_up(shift):
        for c in range(2):
            w_arrive(shift, c, 0)
        block = up_out.at[pair_of(shift), up_rows]
        start(remote(block, block, wx_send.at[shift - 1], wx_recv.at[shift - 1], x_to))
        start(remote(block, block, wy_send.at[shift - 1, 0], wy_recv.at[shift - 1, 0], y_to))

    def share_qkv(shift):
        for c in range(2):
            for part in range(1, 4):
                w_arrive(shift, c, part)
        block = qkv_out.at[pair_of(shift), qkv_rows]
        start(remote(block, block, wy_send.at[shift - 1, 2], wy_recv.at[shift - 1, 2], y_to))

    def share_side_weights(shift):
        block = up_out.at[pair_of(shift), x_rows(True)]
        remote(block, block, wx_send.at[shift - 1], wx_recv.at[shift - 1], x_to).wait_recv()
        start(remote(block, block, wy_send.at[shift - 1, 1], wy_recv.at[shift - 1, 1], y_to))

    def step_blocks(step):
        blocks = []
        for along in (1, -1):
            plane = z - along * step
            there = jnp.logical_and(plane >= 0, plane < PLANES)
            blocks.append((along, lax.rem(plane + PLANES, PLANES), there))
        return blocks

    def line_step(step):
        for a in range(2):
            for along, plane, there in step_blocks(step):
                arrived(a, plane, there)
                carry(a, plane, there, along)

    def side_step(step):
        for a in range(2):
            for unused, plane, there in step_blocks(step):
                side_on(a, plane, there)

    for a in range(2):
        own_arrived(a)
        carry(a, z, always, 0)
    for copy in core_copies + own_copies:
        copy.start()
    line_step(1)
    for copy in up_copies:
        copy.start()
    for a in range(2):
        side_on(a, z, always)
    line_step(2)
    for copy in qkv_copies:
        copy.start()
    side_step(1)
    share_up(1)
    share_up(2)
    line_step(3)
    side_step(2)
    share_up(3)
    for shift in range(1, PLANES):
        share_side_weights(shift)
    side_step(3)
    for shift in range(1, PLANES):
        share_qkv(shift)

    for shift in range(1, PLANES):
        other_y = 2 * (1 - y)
        for n, other in enumerate((other_y + x, other_y + 1 - x)):
            block = up_out.at[pair_of(shift), pl.ds(pl.multiple_of(other * quarter, 16), quarter)]
            remote(block, block, wy_send.at[shift - 1, n], wy_recv.at[shift - 1, n], y_to).wait_recv()
        block = qkv_out.at[pair_of(shift), pl.ds(pl.multiple_of((1 - y) * half, 16), half)]
        remote(block, block, wy_send.at[shift - 1, 2], wy_recv.at[shift - 1, 2], y_to).wait_recv()
    for a in range(2):
        for plane in range(PLANES):
            for n, side in enumerate((x, 1 - x)):
                block = arrays[a][1].at[plane, 2 * (1 - k) + side]
                remote(
                    block, block, core_send.at[a, n, plane], core_recv.at[a, n, plane], core_to
                ).wait_recv()
    for n, (shift, c) in enumerate([(s, c) for s in range(PLANES) for c in range(2)][1:]):
        source = 2 * lax.rem(z - shift + PLANES, PLANES) + lax.rem(k + c, 2)
        remote(
            small_in, small_out.at[source], small_send.at[n], small_recv.at[n], core_to
        ).wait_recv()
    for copy in core_copies:
        copy.wait()
    for copy in own_copies:
        copy.wait()
    small_local.wait()
    for copy in small_copies + up_copies + qkv_copies:
        copy.wait_send()
    for a, (src, dst) in enumerate(arrays):
        pair = remote(src, dst.at[z, 2 * y + x], pair_send.at[a], line_recv.at[a, z], pair_to)
        pl.when(jnp.logical_not(same))(pair.wait_send)
    for when, copy in sends:
        if when is None:
            copy.wait_send()
        else:
            pl.when(when)(copy.wait_send)


def gather_all(tokens, cotangent, w_up, w_qkv, small):
    rows, width = tokens.shape
    n_dp = 2 * PLANES
    bf16 = jnp.bfloat16
    dma = pltpu.SemaphoreType.DMA
    hbm = pl.BlockSpec(memory_space=pl.ANY)
    block = jax.ShapeDtypeStruct((PLANES, 4, rows, width), bf16)
    return pl.pallas_call(
        gather_kernel,
        out_shape=(
            block,
            block,
            jax.ShapeDtypeStruct((n_dp, w_up.shape[0], w_up.shape[1] // n_dp), bf16),
            jax.ShapeDtypeStruct((n_dp, w_qkv.shape[0], w_qkv.shape[1] // n_dp), bf16),
            jax.ShapeDtypeStruct((n_dp,) + small.shape, bf16),
        ),
        in_specs=[hbm] * 5,
        out_specs=(hbm,) * 5,
        scratch_shapes=[
            dma((2, 2, PLANES)),
            dma((2, PLANES)),
            dma((2, PLANES)),
            dma((2, PLANES)),
            dma((2,)),
            dma((2, 2, PLANES)),
            dma((2, 2, PLANES)),
            dma((3, 2, 4)),
            dma((3, 2, 4)),
            dma((3,)),
            dma((3,)),
            dma((3, 3)),
            dma((3, 3)),
            dma((4,)),
            dma((4,)),
            dma((7,)),
            dma((7,)),
            dma((7,)),
        ],
        compiler_params=pltpu.CompilerParams(collective_id=1, has_side_effects=True),
    )(tokens, cotangent, w_up, w_qkv, small)


def dot_nn(left, right):
    return jnp.dot(left, right, preferred_element_type=jnp.float32)


def half_turn(head, cosine, sine):
    first = head[:, :128]
    lane = lax.broadcasted_iota(jnp.int32, first.shape, 1)
    swapped = jnp.where(
        lane < ROT // 2, pltpu.roll(first, 128 - ROT // 2, 1), pltpu.roll(first, ROT // 2, 1)
    )
    return jnp.concatenate([first * cosine + swapped * sine, head[:, 128:]], axis=1)


def block_kernel(
    x_hbm,
    g_hbm,
    up,
    down,
    qkv,
    out_w,
    gains,
    up_bias,
    qkv_bias,
    cosine,
    sine,
    place_q,
    place_k,
    out_sum,
    back_sum,
    vec_all,
    down_tot,
    up_tot,
    outw_tot,
    qkv_tot,
    na_hbm,
    hp_hbm,
    got_down,
    got_up,
    got_outw,
    got_qkv,
    core_got,
    plane_got,
    xb,
    gb,
    hx,
    half_in,
    hid,
    prg,
    q,
    k,
    v,
    mg,
    mix,
    proj,
    stat,
    kacc,
    vacc,
    acc_down,
    acc_up,
    g_down,
    g_up,
    g_outw,
    g_qkv,
    cb,
    tmp,
    vec,
    vec_got,
    load_sem,
    save_sem,
    tmp_sem,
    core_send,
    core_recv,
    plane_send,
    plane_recv,
    home_send,
    home_recv,
    y_send,
    y_recv,
    x_send,
    x_recv,
    a2a_send,
    a2a_recv,
    vec_send,
    vec_recv,
    local_sem,
):
    f32, bf16 = jnp.float32, jnp.bfloat16
    dp = lax.axis_index("dp")
    rank = lax.axis_index("ctx")
    z, core = dp // 2, dp % 2
    y, x = rank // 2, rank % 2
    core_to = (2 * z + 1 - core, rank)
    x_to = (dp, 2 * y + 1 - x)
    y_to = (dp, 2 * (1 - y) + x)
    pair_to = (2 * z + 1 - core, 2 * (1 - y) + x)
    seqs, length, width = x_hbm.shape
    tok = length // 4
    ff = up.shape[1]
    row_tile = 64
    half_part = width // (4 * PLANES)
    section_cols = qkv_tot.shape[1] // 3
    scale = DH ** (-0.5)
    n_qkv = 3 * DH

    barrier = pltpu.get_barrier_semaphore()
    for target in (core_to, x_to, y_to, pair_to):
        pl.semaphore_signal(barrier, inc=1, device_id=target, device_id_type=MESH_ID)
    for shift in range(1, PLANES):
        for c in range(2):
            target = (2 * lax.rem(z + shift, PLANES) + c, rank)
            pl.semaphore_signal(barrier, inc=1, device_id=target, device_id_type=MESH_ID)
    pl.semaphore_wait(barrier, 4 + 2 * (PLANES - 1))

    def ds(first, size, step=None):
        return pl.ds(pl.multiple_of(first, step or size), size)

    def remote(src, dst, send, recv, target):
        return pltpu.make_async_remote_copy(
            src_ref=src,
            dst_ref=dst,
            send_sem=send,
            recv_sem=recv,
            device_id=target,
            device_id_type=MESH_ID,
        )

    pending = []

    def start(copy, when=None):
        if when is None:
            copy.start()
        else:
            pl.when(when)(copy.start)
        pending.append((when, copy.wait_send))

    def start_local(copy, when=None):
        if when is None:
            copy.start()
        else:
            pl.when(when)(copy.start)
        pending.append((when, copy.wait))

    one, two = ds(x * tok, tok), ds((2 + x) * tok, tok)

    def load(s, slot):
        return (
            pltpu.make_async_copy(x_hbm.at[s], xb.at[slot], load_sem.at[0, slot]),
            pltpu.make_async_copy(g_hbm.at[s], gb.at[slot], load_sem.at[1, slot]),
        )

    def save_norm(s):
        return pltpu.make_async_copy(hx.at[1], na_hbm.at[s], save_sem.at[0])

    def save_rows(s):
        copies = []
        for n, (ref, cols) in enumerate(((hid, pl.ds(0, ff)), (prg, pl.ds(ff, ff)))):
            for h, rows in enumerate((one, two)):
                copies.append(
                    pltpu.make_async_copy(
                        ref.at[rows],
                        hp_hbm.at[s, pl.ds(h * tok, tok), cols],
                        save_sem.at[1 + 2 * n + h],
                    )
                )
        return copies

    for copy in load(0, 0):
        copy.start()

    def clear(ref):
        @pl.loop(0, ref.shape[0] // 64)
        def rows(i):
            ref[ds(i * 64, 64), :] = jnp.zeros((64, ref.shape[1]), f32)

    clear(acc_down)
    clear(acc_up)
    vec[...] = jnp.zeros_like(vec)

    def choose_half(src, slot):
        for d in range(width // 256):
            half_in[:, d * 128 : (d + 1) * 128] = src[slot, :, ds(d * 256 + x * 128, 128)]

    @pl.loop(0, seqs)
    def feed_forward(s):
        slot = lax.rem(s, 2)
        for copy in load(s, slot):
            copy.wait()

        @pl.when(s + 1 < seqs)
        def ahead():
            for copy in load(s + 1, 1 - slot):
                copy.start()

        @pl.when(s > 0)
        def saved():
            save_norm(s - 1).wait()
            for copy in save_rows(s - 1):
                copy.wait()

        @pl.loop(0, length // row_tile)
        def norm(i):
            r = ds(i * row_tile, row_tile)
            value = xb[slot, r, :].astype(f32)
            centre = value - jnp.mean(value, axis=1, keepdims=True)
            inv = lax.rsqrt(jnp.mean(centre * centre, axis=1, keepdims=True) + EPS_NORM)
            hat = centre * inv
            hx[1, r, :] = (hat * gains[0:1, :] + gains[1:2, :]).astype(bf16)
            hx[0, r, :] = (hat * gains[2:3, :] + gains[3:4, :]).astype(bf16)

        save_norm(s).start()
        choose_half(hx, 0)

        @pl.loop(0, ff // 256)
        def feed(n):
            c = ds(n * 256, 256)
            pre = dot_nn(hx[0], up[:, c]) + up_bias[:, c]
            hidden_grad = contract_cols(gb[slot], down[c, :])
            cdf = 0.5 * (1.0 + lax.erf(pre * (0.5**0.5)))
            pdf = jnp.exp(-0.5 * pre * pre) * ((2.0 * 3.141592653589793) ** -0.5)
            hid[:, c] = (pre * cdf).astype(bf16)
            prg[:, c] = (hidden_grad * (cdf + pre * pdf)).astype(bf16)

        for copy in save_rows(s):
            copy.start()

        @pl.loop(0, ff // 512)
        def gdown(m):
            r = ds(m * 256, 256)
            acc_down[r, :] += contract_rows(hid[:, ds(x * (ff // 2) + m * 256, 256)], gb[slot])

        @pl.loop(0, width // 512)
        def gup(m):
            r = ds(m * 256, 256)
            acc_up[r, :] += contract_rows(half_in[:, r], prg[...])

        rows_sum = jnp.sum(prg[one, :].astype(f32), axis=0, keepdims=True)
        rows_sum += jnp.sum(prg[two, :].astype(f32), axis=0, keepdims=True)
        vec[0, 6:7, 0:ff] += rows_sum

    save_norm(seqs - 1).wait()
    for copy in save_rows(seqs - 1):
        copy.wait()

    def add_rows(dst, src, rows):
        @pl.loop(0, rows // 32)
        def tiles(i):
            r = ds(i * 32, 32)
            dst[r, :] = (dst[r, :].astype(f32) + src[r, :].astype(f32)).astype(bf16)

    def add_pieces(pieces):
        copies = []
        first = 0
        for n, (dst, src) in enumerate(pieces):
            rows, cols = dst.shape
            here = tmp.at[first : first + rows, 0:cols]
            copy = pltpu.make_async_copy(src, here, tmp_sem.at[n])
            copy.start()
            copies.append((copy, dst, here, rows))
            first += rows
        for copy, dst, here, rows in copies:
            copy.wait()
            add_rows(dst, here, rows)

    down_pieces = g_down.shape[0] // tok

    def y_copy(kind, piece):
        sems = (y_send.at[kind, piece], y_recv.at[kind, piece])
        if kind == 0:
            rows = pl.ds(piece * tok, tok)
            return remote(g_down.at[rows], got_down.at[rows], *sems, y_to)
        if kind == 1:
            return remote(g_outw, got_outw, *sems, y_to)
        src, got = (g_up, got_up) if kind == 2 else (g_qkv, got_qkv)
        pair = pl.ds(2 * lax.rem(z + piece, PLANES), 2)
        return remote(src.at[pair], got.at[pair], *sems, y_to)

    half_rows = ds(x * half_part, half_part)
    other_half = ds((1 - x) * half_part, half_part)

    def column_parts(kind, index, source):
        if kind == 2:
            return [(g_up.at[index], up_tot.at[half_rows, ds(source * ff, ff)])]
        return [
            (
                g_qkv.at[index, :, pl.ds(n * DH, DH)],
                qkv_tot.at[half_rows, ds(n * section_cols + source * DH, DH)],
            )
            for n in range(3)
        ]

    def side_parts(kind, plane, rows):
        if kind == 2:
            return [up_tot.at[rows, ds(plane * 2 * ff, 2 * ff)]]
        return [qkv_tot.at[rows, ds(n * section_cols + plane * 2 * DH, 2 * DH)] for n in range(3)]

    def reduced(kind, piece):
        y_copy(kind, piece).wait()
        if kind == 0:
            rows = pl.ds(piece * tok, tok)
            add_pieces([(g_down.at[rows], got_down.at[rows])])
            place = down_tot.at[ds(x * g_down.shape[0] + piece * tok, tok)]
            start_local(pltpu.make_async_copy(g_down.at[rows], place, local_sem.at[2 + piece]))
            start(remote(g_down.at[rows], place, x_send.at[0, piece], x_recv.at[0, piece], x_to))
            return
        if kind == 1:
            add_pieces([(g_outw, got_outw)])
            place = outw_tot.at[half_rows]
            start_local(pltpu.make_async_copy(g_outw, place, local_sem.at[6]))
            start(remote(g_outw, place, x_send.at[1, 0], x_recv.at[1, 0], x_to))
            return
        got, own = ((got_up, g_up), (got_qkv, g_qkv))[kind - 2]
        plane = lax.rem(z + piece, PLANES)
        add_pieces([(own.at[2 * plane + c], got.at[2 * plane + c]) for c in range(2)])
        for c in range(2):
            for part, (src, dst) in enumerate(column_parts(kind, 2 * plane + c, dp)):
                send = a2a_send.at[kind - 2, piece, c, part]
                recv = a2a_recv.at[kind - 2, piece, core, part]
                copy = remote(src, dst, send, recv, (2 * plane + c, rank))
                if piece == 0:
                    local = pltpu.make_async_copy(
                        src, dst, local_sem.at[7 + 3 * (kind - 2) + part]
                    )
                    pl.when(core == c)(local.start)
                    start(copy, core != c)
                else:
                    start(copy)

    def share(kind, shift):
        plane = lax.rem(z - shift + PLANES, PLANES)
        for c in range(2):
            for part, (src, dst) in enumerate(column_parts(kind, 2 * plane + c, 2 * plane + c)):
                recv = a2a_recv.at[kind - 2, shift, c, part]
                copy = remote(dst, dst, a2a_send.at[kind - 2, shift, c, part], recv, core_to)
                if shift == 0:
                    pl.when(core != c)(copy.wait_recv)
                    local = pltpu.make_async_copy(
                        src, dst, local_sem.at[7 + 3 * (kind - 2) + part]
                    )
                    pl.when(core == c)(local.wait)
                else:
                    copy.wait_recv()
        for part, block in enumerate(side_parts(kind, plane, half_rows)):
            sems = (x_send.at[kind + part, shift], x_recv.at[kind + part, shift])
            start(remote(block, block, *sems, x_to))

    order = (0, 3, 2, 1)

    def core_copy(i):
        s = order[i]
        return remote(
            cb.at[seqs + i % 2], core_got.at[s], core_send.at[i], core_recv.at[i], core_to
        )

    def chip_sum(i):
        s = order[i]
        core_copy(i).wait_recv()
        add_pieces([(cb.at[i, a], core_got.at[s, a]) for a in range(2)])
        start(flow_copy(i, 0), jnp.logical_and(z == 0, s > 0))
        start(flow_copy(i, 1), jnp.logical_and(z == PLANES - 1, s < PLANES - 1))

    def flow_copy(i, side):
        s = order[i]
        sems = (plane_send.at[i], plane_recv.at[side, s])
        return remote(cb.at[i], plane_got.at[side, s], *sems, (dp + (2, -2)[side], rank))

    def flow_add(i, side):
        flow_copy(i, side).wait_recv()
        add_pieces([(cb.at[i, a], plane_got.at[side, order[i], a]) for a in range(2)])

    def flow_relay(i, hop):
        s = order[i]
        for side, plane in enumerate((hop, PLANES - 1 - hop)):
            if (plane < s) if side == 0 else (plane > s):
                here = z == plane
                pl.when(here)(functools.partial(flow_add, i, side))
                start(flow_copy(i, side), here)

    def flow_end(i):
        s = order[i]

        @pl.when(z == s)
        def both():
            if s > 0:
                flow_add(i, 0)
            if s < PLANES - 1:
                flow_add(i, 1)

        same = core == y
        for a, result in enumerate((out_sum, back_sum)):
            block = cb.at[i, a]
            start_local(
                pltpu.make_async_copy(block, result, local_sem.at[a]),
                jnp.logical_and(z == s, same),
            )
            start(
                remote(block, result, home_send.at[a], home_recv.at[a], pair_to),
                jnp.logical_and(z == s, jnp.logical_not(same)),
            )

    def rounded(dst, src, rows, cols):
        @pl.loop(0, rows // 64)
        def tiles(i):
            r = ds(i * 64, 64)
            dst[r, :] = src[r, 0:cols].astype(bf16)

    def rounded_columns(dst, src, cols):
        @pl.loop(0, dst.shape[0])
        def blocks(d):
            dst[d] = src[ds(d * half_part, half_part), 0:cols].astype(bf16)

    def load_again(i, slot):
        s = order[i]
        copies = [
            pltpu.make_async_copy(na_hbm.at[s], xb.at[slot], load_sem.at[0, slot]),
            pltpu.make_async_copy(g_hbm.at[s], gb.at[slot], load_sem.at[1, slot]),
            pltpu.make_async_copy(
                hp_hbm.at[s], hx.at[slot, pl.ds(2 * tok, 2 * tok)], load_sem.at[2, slot]
            ),
        ]
        for h, rows in enumerate((one, two)):
            copies.append(
                pltpu.make_async_copy(
                    x_hbm.at[s, rows],
                    hx.at[slot, pl.ds(h * tok, tok)],
                    load_sem.at[3 + h, slot],
                )
            )
        return copies

    for copy in load_again(0, 0):
        copy.start()
    rounded(g_down, acc_down, g_down.shape[0], width)
    for piece in (0, 1):
        y_copy(0, piece).start()
    rounded_columns(g_up, acc_up, ff)
    for shift in (1, 0, 2, 3):
        y_copy(2, shift).start()
    for piece in range(2, down_pieces):
        y_copy(0, piece).start()
    clear(acc_up)
    clear(acc_down.at[0 : tok])

    def attention(i, tick):
        slot = i % 2
        for copy in load_again(i, slot):
            copy.wait()
        if i + 1 < seqs:
            for copy in load_again(i + 1, 1 - slot):
                copy.start()
        tick(i, 0)
        choose_half(xb, slot)
        for n, ref in enumerate((q, k, v)):
            c = slice(n * DH, (n + 1) * DH)
            part = dot_nn(xb[slot], qkv[:, c]) + qkv_bias[:, c]
            if n < 2:
                part = half_turn(part, cosine[...], sine[...])
            ref[...] = part.astype(bf16)
        mg[...] = contract_cols(gb[slot], out_w[...]).astype(bf16)
        tick(i, 1)
        kacc[...] = jnp.zeros_like(kacc)
        vacc[...] = jnp.zeros_like(vacc)

        @pl.loop(0, 4)
        def attend(part):
            r = ds(part * tok, tok)
            scores = contract_cols(q[r, :], k[...]) * scale
            scores = jnp.where(place_k[...] <= place_q[r, :], scores, MASK_FILL)
            exponent = jnp.exp(scores - jnp.max(scores, axis=1, keepdims=True))
            prob = exponent / jnp.sum(exponent, axis=1, keepdims=True)
            low = prob.astype(bf16)
            mix[r, :] = dot_nn(low, v[...]).astype(bf16)
            prob_grad = contract_cols(mg[r, :], v[...])
            row_dot = jnp.sum(prob_grad * prob, axis=1, keepdims=True)
            score_grad = (prob * (prob_grad - row_dot)).astype(bf16)
            query_grad = dot_nn(score_grad, k[...]) * scale
            proj[r, 0:DH] = half_turn(query_grad, cosine[r, :], -sine[r, :]).astype(bf16)
            kacc[...] += contract_rows(score_grad, q[r, :])
            vacc[...] += contract_rows(low, mg[r, :])

        proj[:, DH : 2 * DH] = half_turn(kacc[...] * scale, cosine[...], -sine[...]).astype(bf16)
        proj[:, 2 * DH : 3 * DH] = vacc[...].astype(bf16)
        tick(i, 2)
        acc_down[0:tok, :] += contract_rows(mix[:, ds(x * 128, 128)], gb[slot])

        @pl.loop(0, width // 512)
        def gqkv(m):
            r = ds(m * 256, 256)
            acc_up[r, 0:n_qkv] += contract_rows(half_in[:, r], proj[...])

        tick(i, 3)
        value = hx[slot, 0 : 2 * tok, :].astype(f32)
        mean = jnp.mean(value, axis=1, keepdims=True)
        centre = value - mean
        stat[0] = mean
        stat[1] = lax.rsqrt(jnp.mean(centre * centre, axis=1, keepdims=True) + EPS_NORM)
        if i >= 2:
            core_copy(i - 2).wait_send()

        def picked(ref):
            return jnp.concatenate([ref[one, :], ref[two, :]], axis=0)

        place = [jnp.where(core == h, i, seqs + i % 2) for h in range(2)]
        later = slice(2 * tok, 4 * tok)

        @pl.loop(0, width // 256)
        def followers(n):
            c = ds(n * 256, 256)
            out = dot_nn(hx[slot, later, 0:ff], down[:, c]) + dot_nn(picked(mix), out_w[:, c])
            mlp_back = contract_cols(hx[slot, later, ff : 2 * ff], up[c, :])
            attn_back = contract_cols(picked(proj), qkv[c, :])
            back = attn_back * gains[0:1, c] + mlp_back * gains[2:3, c]
            for h in range(2):
                rows = slice(h * tok, (h + 1) * tok)
                cb[place[h], 0, :, c] = out[rows].astype(bf16)
                cb[place[h], 1, :, c] = back[rows].astype(bf16)
            hat = (hx[slot, 0 : 2 * tok, c].astype(f32) - stat[0]) * stat[1]
            grad = jnp.concatenate([gb[slot, one, c], gb[slot, two, c]], axis=0).astype(f32)
            sums = (attn_back * hat, attn_back, mlp_back * hat, mlp_back, grad)
            for n_sum, term in enumerate(sums):
                vec[0, n_sum : n_sum + 1, c] += jnp.sum(term, axis=0, keepdims=True)

        vec[0, 5:6, 0:n_qkv] += jnp.sum(picked(proj).astype(f32), axis=0, keepdims=True)
        core_copy(i).start()
        tick(i, 4)

    plan = {
        (0, 3): [(reduced, 0, 0)],
        (1, 1): [(chip_sum, 0)],
        (1, 2): [(reduced, 0, 1)],
        (1, 4): [(reduced, 2, 1)],
        (2, 1): [(chip_sum, 1)],
        (2, 3): [(reduced, 2, 0), (flow_relay, 0, 1)],
        (2, 4): [(share, 2, 0), (share, 2, 1)],
        (3, 1): [(chip_sum, 2), (reduced, 2, 2)],
        (3, 2): [(flow_relay, 1, 1)],
        (3, 4): [(reduced, 2, 3), (flow_relay, 0, 2)],
    }

    def tick(i, point):
        for step, *which in plan.get((i, point), ()):
            step(*which)

    for i in range(seqs):
        attention(i, tick)

    rounded_columns(g_qkv, acc_up, n_qkv)
    for shift in (1, 2, 3, 0):
        y_copy(3, shift).start()
    rounded(g_outw, acc_down, tok, width)
    y_copy(1, 0).start()

    def vec_copy(n):
        target = (x_to, y_to)[n]
        return remote(vec.at[n], vec_got.at[n], vec_send.at[n], vec_recv.at[n], target)

    vec_copy(0).start()
    chip_sum(3)
    reduced(0, 2)
    flow_relay(2, 1)
    vec_copy(0).wait()
    vec[1] = vec[0] + vec_got[0]
    vec_copy(1).start()
    share(2, 2)
    flow_relay(1, 2)
    reduced(0, 3)
    flow_end(0)
    vec_copy(1).wait()
    vec_all[dp] = vec[1] + vec_got[1]
    peers = [(s, c) for s in range(PLANES) for c in range(2)][1:]
    for n, (shift, c) in enumerate(peers):
        target = (2 * lax.rem(z + shift, PLANES) + lax.rem(core + c, 2), rank)
        start(
            remote(
                vec_all.at[dp], vec_all.at[dp], vec_send.at[2 + n], vec_recv.at[2 + n], target
            )
        )
    share(2, 3)
    flow_relay(3, 1)
    reduced(3, 1)
    flow_end(2)
    reduced(3, 2)
    flow_end(1)
    share(3, 1)
    reduced(3, 3)
    flow_end(3)
    reduced(3, 0)
    share(3, 2)
    share(3, 0)
    reduced(1, 0)
    share(3, 3)

    for n, (shift, c) in enumerate(peers):
        source = 2 * lax.rem(z - shift + PLANES, PLANES) + lax.rem(core + c, 2)
        block = vec_all.at[source]
        remote(block, block, vec_send.at[2 + n], vec_recv.at[2 + n], core_to).wait_recv()
    for piece in range(down_pieces):
        block = down_tot.at[ds((1 - x) * g_down.shape[0] + piece * tok, tok)]
        remote(block, block, x_send.at[0, piece], x_recv.at[0, piece], x_to).wait_recv()
    block = outw_tot.at[other_half]
    remote(block, block, x_send.at[1, 0], x_recv.at[1, 0], x_to).wait_recv()
    for kind in (2, 3):
        for shift in range(PLANES):
            plane = lax.rem(z - shift + PLANES, PLANES)
            for part, block in enumerate(side_parts(kind, plane, other_half)):
                sems = (x_send.at[kind + part, shift], x_recv.at[kind + part, shift])
                remote(block, block, *sems, x_to).wait_recv()
    for a, result in enumerate((out_sum, back_sum)):
        copy = remote(result, result, home_send.at[a], home_recv.at[a], pair_to)
        pl.when(core != y)(copy.wait_recv)
    for i in range(seqs - 2, seqs):
        core_copy(i).wait_send()
    for when, wait in pending:
        if when is None:
            wait()
        else:
            pl.when(when)(wait)


def block_compute(x_all, g_all, up_cols, w_down, qkv_cols, w_out, gains, up_bias, qkv_bias, place):
    f32, bf16 = jnp.float32, jnp.bfloat16
    seqs, length, width = x_all.shape
    ff = up_cols.shape[1]
    tok = length // 4
    n_dp = 2 * PLANES
    half_part = width // (2 * n_dp)
    half_rot = ROT // 2
    frequency = ROPE_BASE ** (-2.0 * jnp.arange(half_rot, dtype=f32) / ROT)
    angles = place.astype(f32)[:, None] * frequency[None, :]
    rest = jnp.zeros((length, 128 - ROT), f32)
    cosine = jnp.concatenate([jnp.cos(angles), jnp.cos(angles), rest + 1.0], axis=1)
    sine = jnp.concatenate([-jnp.sin(angles), jnp.sin(angles), rest], axis=1)
    hbm = pl.BlockSpec(memory_space=pl.ANY)
    vmem = pl.BlockSpec(memory_space=pltpu.VMEM)
    dma = pltpu.SemaphoreType.DMA

    def shape(*dims, dtype=bf16):
        return jax.ShapeDtypeStruct(dims, dtype)

    def buf(*dims, dtype=bf16):
        return pltpu.VMEM(dims, dtype)

    results = pl.pallas_call(
        block_kernel,
        out_shape=(
            shape(tok, width),
            shape(tok, width),
            shape(n_dp, 8, width, dtype=f32),
            shape(ff, width),
            shape(2 * half_part, n_dp * ff),
            shape(DH, width),
            shape(2 * half_part, n_dp * 3 * DH),
            shape(seqs, length, width),
            shape(seqs, 2 * tok, 2 * ff),
            shape(ff // 2, width),
            shape(n_dp, half_part, ff),
            shape(DH // 2, width),
            shape(n_dp, half_part, 3 * DH),
            shape(seqs, 2, tok, width),
            shape(2, seqs, 2, tok, width),
        ),
        in_specs=[hbm, hbm] + [vmem] * 11,
        out_specs=(hbm, hbm, vmem) + (hbm,) * 12,
        scratch_shapes=[
            buf(2, length, width),
            buf(2, length, width),
            buf(2, length, width),
            buf(length, width // 2),
            buf(length, ff),
            buf(length, ff),
            buf(length, DH),
            buf(length, DH),
            buf(length, DH),
            buf(length, DH),
            buf(length, DH),
            buf(length, 3 * DH),
            buf(2, 2 * tok, 1, dtype=f32),
            buf(length, DH, dtype=f32),
            buf(length, DH, dtype=f32),
            buf(ff // 2, width, dtype=f32),
            buf(width // 2, ff, dtype=f32),
            buf(ff // 2, width),
            buf(n_dp, half_part, ff),
            buf(DH // 2, width),
            buf(n_dp, half_part, 3 * DH),
            buf(seqs + 2, 2, tok, width),
            buf(2 * tok, width),
            buf(2, 8, width, dtype=f32),
            buf(2, 8, width, dtype=f32),
            dma((5, 2)),
            dma((5,)),
            dma((2,)),
            dma((seqs,)),
            dma((seqs,)),
            dma((seqs,)),
            dma((2, seqs)),
            dma((2,)),
            dma((2,)),
            dma((4, 4)),
            dma((4, 4)),
            dma((6, 4)),
            dma((6, 4)),
            dma((2, PLANES, 2, 3)),
            dma((2, PLANES, 2, 3)),
            dma((9,)),
            dma((9,)),
            dma((13,)),
        ],
        compiler_params=pltpu.CompilerParams(
            collective_id=2, has_side_effects=True, vmem_limit_bytes=63 * 2**20
        ),
    )(
        x_all,
        g_all,
        up_cols,
        w_down,
        qkv_cols,
        w_out,
        gains,
        up_bias,
        qkv_bias,
        cosine,
        sine,
        place[:, None],
        place[None, :],
    )
    return results[:7]


def column_local(
    tokens,
    cotangent,
    pair_index,
    norm1_gain,
    norm1_bias,
    norm2_gain,
    norm2_bias,
    w_qkv,
    b_qkv,
    w_out,
    b_out,
    w_up,
    b_up,
    w_down,
    b_down,
):
    bf16, f32 = jnp.bfloat16, jnp.float32
    tok_count, width = tokens.shape[1:]
    n_dp = H
    dp_rank = lax.axis_index("dp")
    rank = lax.axis_index("ctx")
    z, core = dp_rank // 2, dp_rank % 2
    y, x = rank // 2, rank % 2
    part = width // n_dp
    ff_part = w_up.shape[1] // n_dp
    qkv_part = 3 * DH
    seq_len = 4 * tok_count
    place = positions(pair_index, tok_count)

    small = jnp.concatenate(
        [norm1_gain, norm1_bias, norm2_gain, norm2_bias, b_out, b_down, b_qkv]
    ).reshape(-1, part)
    small = jnp.pad(small, ((0, -small.shape[0] % 16), (0, 0)))
    x_all, g_all, up_cols, qkv_cols, small_all = gather_all(
        tokens[0], cotangent[0], w_up, w_qkv, small
    )
    up_cols = up_cols.reshape(width, ff_part)
    qkv_cols = qkv_cols.reshape(width, qkv_part)
    vectors = [small_all[:, i].reshape(width).astype(f32) for i in range(6)]
    gain1, shift1, gain2, shift2, out_bias, down_bias = vectors
    qkv_bias_all = small_all[:, 6:9].reshape(3, H, DH).astype(f32)
    qkv_bias = lax.dynamic_index_in_dim(qkv_bias_all, dp_rank, 1, keepdims=False).reshape(qkv_part)

    gains = jnp.stack([gain1, shift1, gain2, shift2] * 2)
    out_sum, back_sum, vec_all, down_total, up_total, out_total, qkv_total = block_compute(
        x_all.reshape(PLANES, seq_len, width),
        g_all.reshape(PLANES, seq_len, width),
        up_cols,
        w_down,
        qkv_cols,
        w_out,
        gains,
        b_up.astype(f32)[None],
        qkv_bias[None],
        place,
    )

    back_sum = back_sum.astype(f32)
    own_rows = tokens[0].astype(f32)
    output = (own_rows + out_sum.astype(f32) + out_bias + down_bias).astype(bf16)[None]

    own_centre = own_rows - jnp.mean(own_rows, axis=-1, keepdims=True)
    own_inv = lax.rsqrt(jnp.mean(own_centre * own_centre, axis=-1, keepdims=True) + EPS_NORM)
    own_hat = own_centre * own_inv
    norm_back = (
        back_sum
        - jnp.mean(back_sum, axis=-1, keepdims=True)
        - own_hat * jnp.mean(back_sum * own_hat, axis=-1, keepdims=True)
    ) * own_inv
    input_grad = (cotangent[0].astype(f32) + norm_back).astype(bf16)[None]

    totals = jnp.sum(vec_all[:, :4], axis=0)
    mine = lax.dynamic_slice_in_dim(totals, dp_rank * part, part, 1)
    gain1_total, shift1_total, gain2_total, shift2_total = mine
    own_vec = lax.dynamic_index_in_dim(vec_all, dp_rank, 0, keepdims=False)
    bias_total = lax.dynamic_slice_in_dim(own_vec[4], dp_rank * part, part)
    up_bias_total = own_vec[6, :ff_part]
    qkv_bias_total = vec_all[:, 5, :qkv_part].reshape(n_dp, 3, DH).swapaxes(0, 1).reshape(-1)
    qkv_bias_total = lax.dynamic_slice_in_dim(
        qkv_bias_total, dp_rank * b_qkv.shape[0], b_qkv.shape[0]
    )
    return (
        output,
        input_grad,
        gain1_total,
        shift1_total,
        gain2_total,
        shift2_total,
        qkv_total.astype(f32),
        qkv_bias_total,
        out_total.astype(f32),
        bias_total,
        up_total.astype(f32),
        up_bias_total,
        down_total.astype(f32),
        bias_total,
    )


def solution(mesh):
    local = column_local if mesh.shape["dp"] == H and mesh.shape["ctx"] == 4 else plain_local
    placed = (
        P("dp", "ctx", None),
        P("dp", "ctx", None),
        P(),
        P("dp"),
        P("dp"),
        P("dp"),
        P("dp"),
        P("dp", None),
        P("dp"),
        P("dp", None),
        P("dp"),
        P("dp", None),
        P("dp"),
        P("dp", None),
        P("dp"),
    )
    return jax.shard_map(
        local,
        mesh=mesh,
        in_specs=placed,
        out_specs=(
            P("dp", "ctx", None),
            P("dp", "ctx", None),
            P("dp"),
            P("dp"),
            P("dp"),
            P("dp"),
            P("dp", None),
            P("dp"),
            P("dp", None),
            P("dp"),
            P("dp", None),
            P("dp"),
            P("dp", None),
            P("dp"),
        ),
        check_vma=False,
    )
```

```python
import functools

import jax
import jax.numpy as jnp
from jax import lax
from jax.experimental import pallas as pl
from jax.experimental.pallas import tpu as pltpu
from jax.sharding import PartitionSpec as P

H = 8
DH = 256
ROT = 64


EPS_NORM = 1e-05
ROPE_BASE = 10000.0
MASK_FILL = -1000000000.0


def shortened(x):

    def short(part):
        return part.astype(jnp.bfloat16) if part.dtype == jnp.float32 else part

    return jax.tree.map(short, x)


def layer_norm(values_in, gain_vec, offset):
    centre = values_in - jnp.mean(values_in, axis=-1, keepdims=True)
    spread = jnp.mean(centre * centre, axis=-1, keepdims=True)
    return centre * lax.rsqrt(spread + EPS_NORM) * gain_vec + offset


def norm_grads(values_in, gain_vec, offset, upstream):
    unused, pullback = jax.vjp(layer_norm, values_in, gain_vec, offset)
    return pullback(upstream)


def positions(pair_index, tok_count):
    ranks_total = pair_index.shape[0]
    half_len = tok_count // 2
    index_all = jnp.arange(ranks_total * tok_count, dtype=jnp.int32)
    owner_rank = index_all // tok_count
    within = index_all % tok_count
    match_table = owner_rank[:, None] == jnp.arange(ranks_total, dtype=jnp.int32)[None, :]
    first_block = jnp.sum(jnp.where(match_table, pair_index[None, :], 0), axis=1)
    block_id = jnp.where(within < half_len, first_block, 2 * ranks_total - 1 - first_block)
    return block_id * half_len + within % half_len


def rotary(head_vals, token_place, turn_sign):
    half_rot = ROT // 2
    frequency = ROPE_BASE ** (-2.0 * jnp.arange(half_rot, dtype=jnp.float32) / ROT)
    angles = token_place.astype(jnp.float32)[:, None] * frequency[None, :]
    cosine = jnp.cos(angles)[:, None, :]
    sine_part = turn_sign * jnp.sin(angles)[:, None, :]
    first_half = head_vals[..., :half_rot]
    second = head_vals[..., half_rot:ROT]
    return jnp.concatenate(
        [
            first_half * cosine - second * sine_part,
            second * cosine + first_half * sine_part,
            head_vals[..., ROT:],
        ],
        axis=-1,
    )


def contract_rows(left, right):
    return lax.dot_general(
        left, right, (((0,), (0,)), ((), ())), preferred_element_type=jnp.float32
    )


def contract_cols(left, right):
    return lax.dot_general(
        left, right, (((1,), (1,)), ((), ())), preferred_element_type=jnp.float32
    )


def plain_local(
    tokens,
    cotangent,
    pair_index,
    norm1_gain,
    norm1_bias,
    norm2_gain,
    norm2_bias,
    w_qkv,
    b_qkv,
    w_out,
    b_out,
    w_up,
    b_up,
    w_down,
    b_down,
):
    seq_dev, tok_count, width = tokens.shape
    row_count = seq_dev * tok_count
    head_shape = (seq_dev, tok_count, H, DH)
    score_scale = DH ** (-0.5)
    device_rank = lax.axis_index("ctx")
    all_place = positions(pair_index, tok_count)
    own_place = lax.dynamic_slice_in_dim(all_place, device_rank * tok_count, tok_count)
    allowed = all_place[None, None, None, :] <= own_place[None, None, :, None]
    gathered = (
        lax.all_gather(norm1_gain, "dp", axis=0, tiled=True),
        lax.all_gather(norm1_bias, "dp", axis=0, tiled=True),
        lax.all_gather(norm2_gain, "dp", axis=0, tiled=True),
        lax.all_gather(norm2_bias, "dp", axis=0, tiled=True),
        lax.all_gather(w_qkv, "dp", axis=0, tiled=True),
        lax.all_gather(b_qkv, "dp", axis=0, tiled=True),
        lax.all_gather(w_out, "dp", axis=0, tiled=True),
        lax.all_gather(b_out, "dp", axis=0, tiled=True),
        lax.all_gather(w_up, "dp", axis=0, tiled=True),
        lax.all_gather(b_up, "dp", axis=0, tiled=True),
        lax.all_gather(w_down, "dp", axis=0, tiled=True),
        lax.all_gather(b_down, "dp", axis=0, tiled=True),
    )
    (
        attn_gain,
        attn_shift,
        mlp_gain,
        mlp_shift,
        qkv_weight,
        qkv_bias,
        out_weight,
        out_bias,
        up_weight,
        up_bias,
        down_weight,
        down_bias,
    ) = gathered
    token_rows = tokens.reshape(row_count, width).astype(jnp.float32)
    normed_attn = layer_norm(
        token_rows, attn_gain.astype(jnp.float32), attn_shift.astype(jnp.float32)
    ).astype(jnp.bfloat16)
    normed_mlp = layer_norm(
        token_rows, mlp_gain.astype(jnp.float32), mlp_shift.astype(jnp.float32)
    ).astype(jnp.bfloat16)
    projected = jnp.dot(
        normed_attn, qkv_weight, preferred_element_type=jnp.float32
    ) + qkv_bias.astype(jnp.float32)
    queries = rotary(projected[:, :width].reshape(head_shape), own_place, 1.0).astype(jnp.bfloat16)
    key_local = (
        rotary(projected[:, width : 2 * width].reshape(head_shape), own_place, 1.0)
        .astype(jnp.bfloat16)
        .reshape(seq_dev, tok_count, width)
    )
    value_local = projected[:, 2 * width :].astype(jnp.bfloat16).reshape(seq_dev, tok_count, width)
    key_all, value_all = (
        lax.all_gather(key_local, "ctx", axis=1, tiled=True),
        lax.all_gather(value_local, "ctx", axis=1, tiled=True),
    )
    seq_len = key_all.shape[1]
    key_heads = key_all.reshape(seq_dev, seq_len, H, DH)
    value_heads = value_all.reshape(seq_dev, seq_len, H, DH)
    raw_scores = (
        jnp.einsum("sqhd,skhd->shqk", queries, key_heads, preferred_element_type=jnp.float32)
        * score_scale
    )
    raw_scores = jnp.where(allowed, raw_scores, MASK_FILL)
    row_max = jnp.max(raw_scores, axis=-1, keepdims=True)
    exponent = jnp.exp(raw_scores - row_max)
    row_total = jnp.sum(exponent, axis=-1, keepdims=True)
    log_norm = row_max + jnp.log(row_total)
    prob_low = (exponent / row_total).astype(jnp.bfloat16)
    attn_mixed = (
        jnp.einsum("shqk,skhd->sqhd", prob_low, value_heads, preferred_element_type=jnp.float32)
        .reshape(row_count, width)
        .astype(jnp.bfloat16)
    )
    attn_branch = jnp.dot(
        attn_mixed, out_weight, preferred_element_type=jnp.float32
    ) + out_bias.astype(jnp.float32)
    hidden_pre = jnp.dot(
        normed_mlp, up_weight, preferred_element_type=jnp.float32
    ) + up_bias.astype(jnp.float32)
    hidden = jax.nn.gelu(hidden_pre, approximate=False).astype(jnp.bfloat16)
    mlp_branch = jnp.dot(
        hidden, down_weight, preferred_element_type=jnp.float32
    ) + down_bias.astype(jnp.float32)
    output = (token_rows + attn_branch + mlp_branch).astype(jnp.bfloat16).reshape(tokens.shape)
    attn_gain, mlp_gain, qkv_weight, out_weight, up_weight, down_weight = (
        lax.all_gather(norm1_gain, "dp", axis=0, tiled=True),
        lax.all_gather(norm2_gain, "dp", axis=0, tiled=True),
        lax.all_gather(w_qkv, "dp", axis=0, tiled=True),
        lax.all_gather(w_out, "dp", axis=0, tiled=True),
        lax.all_gather(w_up, "dp", axis=0, tiled=True),
        lax.all_gather(w_down, "dp", axis=0, tiled=True),
    )
    grad_rows = cotangent.reshape(row_count, width)
    grad_wide = grad_rows.astype(jnp.float32)
    hidden_grad = contract_cols(grad_rows, down_weight)
    unused, gelu_pull = jax.vjp(
        lambda pre_value: jax.nn.gelu(pre_value, approximate=False), hidden_pre
    )
    pre_grad = gelu_pull(hidden_grad)[0].astype(jnp.bfloat16)
    normed_mlp_grad = contract_cols(pre_grad, up_weight)
    mlp_in_grad, mlp_gain_grad, mlp_shift_grad = norm_grads(
        token_rows, mlp_gain.astype(jnp.float32), mlp_shift.astype(jnp.float32), normed_mlp_grad
    )
    mlp_terms = (
        contract_rows(normed_mlp, pre_grad),
        jnp.sum(pre_grad.astype(jnp.float32), axis=0),
        contract_rows(hidden, grad_rows),
        jnp.sum(grad_wide, axis=0),
        mlp_gain_grad,
        mlp_shift_grad,
    )
    mlp_shares = (
        lax.psum_scatter(
            mlp_terms[0].astype(jnp.bfloat16), "dp", scatter_dimension=0, tiled=True
        ).astype(jnp.float32),
        lax.psum_scatter(
            mlp_terms[1].astype(jnp.bfloat16), "dp", scatter_dimension=0, tiled=True
        ).astype(jnp.float32),
        lax.psum_scatter(
            mlp_terms[2].astype(jnp.bfloat16), "dp", scatter_dimension=0, tiled=True
        ).astype(jnp.float32),
        lax.psum_scatter(
            mlp_terms[3].astype(jnp.bfloat16), "dp", scatter_dimension=0, tiled=True
        ).astype(jnp.float32),
        lax.psum_scatter(
            mlp_terms[4].astype(jnp.bfloat16), "dp", scatter_dimension=0, tiled=True
        ).astype(jnp.float32),
        lax.psum_scatter(
            mlp_terms[5].astype(jnp.bfloat16), "dp", scatter_dimension=0, tiled=True
        ).astype(jnp.float32),
    )
    mixed_grad = contract_cols(grad_rows, out_weight).astype(jnp.bfloat16).reshape(head_shape)
    again_scores = (
        jnp.einsum("sqhd,skhd->shqk", queries, key_heads, preferred_element_type=jnp.float32)
        * score_scale
    )
    again_scores = jnp.where(allowed, again_scores, MASK_FILL)
    attn_prob = jnp.exp(again_scores - log_norm)
    prob_again = attn_prob.astype(jnp.bfloat16)
    prob_grad = jnp.einsum(
        "sqhd,skhd->shqk", mixed_grad, value_heads, preferred_element_type=jnp.float32
    )
    row_dot = jnp.sum(prob_grad * attn_prob, axis=-1, keepdims=True)
    score_grad = (attn_prob * (prob_grad - row_dot)).astype(jnp.bfloat16)
    query_grad = (
        jnp.einsum("shqk,skhd->sqhd", score_grad, key_heads, preferred_element_type=jnp.float32)
        * score_scale
    )
    key_part = (
        jnp.einsum("shqk,sqhd->skhd", score_grad, queries, preferred_element_type=jnp.float32)
        * score_scale
    ).reshape(seq_dev, seq_len, width)
    value_part = jnp.einsum(
        "shqk,sqhd->skhd", prob_again, mixed_grad, preferred_element_type=jnp.float32
    ).reshape(seq_dev, seq_len, width)
    key_grad, value_grad = (
        lax.psum_scatter(
            key_part.astype(jnp.bfloat16), "ctx", scatter_dimension=1, tiled=True
        ).astype(jnp.float32),
        lax.psum_scatter(
            value_part.astype(jnp.bfloat16), "ctx", scatter_dimension=1, tiled=True
        ).astype(jnp.float32),
    )
    query_back = rotary(query_grad, own_place, -1.0).reshape(row_count, width)
    key_back = rotary(key_grad.reshape(head_shape), own_place, -1.0).reshape(row_count, width)
    proj_grad = jnp.concatenate(
        [query_back, key_back, value_grad.reshape(row_count, width)], axis=1
    ).astype(jnp.bfloat16)
    normed_attn_grad = contract_cols(proj_grad, qkv_weight)
    attn_in_grad, attn_gain_grad, attn_shift_grad = norm_grads(
        token_rows, attn_gain.astype(jnp.float32), attn_shift.astype(jnp.float32), normed_attn_grad
    )
    input_grad = (grad_wide + mlp_in_grad + attn_in_grad).astype(jnp.bfloat16).reshape(tokens.shape)
    attn_terms = (
        contract_rows(normed_attn, proj_grad),
        jnp.sum(proj_grad.astype(jnp.float32), axis=0),
        contract_rows(attn_mixed, grad_rows),
        attn_gain_grad,
        attn_shift_grad,
    )
    attn_shares = (
        lax.psum_scatter(
            attn_terms[0].astype(jnp.bfloat16), "dp", scatter_dimension=0, tiled=True
        ).astype(jnp.float32),
        lax.psum_scatter(
            attn_terms[1].astype(jnp.bfloat16), "dp", scatter_dimension=0, tiled=True
        ).astype(jnp.float32),
        lax.psum_scatter(
            attn_terms[2].astype(jnp.bfloat16), "dp", scatter_dimension=0, tiled=True
        ).astype(jnp.float32),
        lax.psum_scatter(
            attn_terms[3].astype(jnp.bfloat16), "dp", scatter_dimension=0, tiled=True
        ).astype(jnp.float32),
        lax.psum_scatter(
            attn_terms[4].astype(jnp.bfloat16), "dp", scatter_dimension=0, tiled=True
        ).astype(jnp.float32),
    )
    summed = jax.tree.map(
        lambda part: part.astype(jnp.float32), lax.psum(shortened(mlp_shares + attn_shares), "ctx")
    )
    (
        up_total,
        up_bias_total,
        down_total,
        bias_total,
        mlp_gain_total,
        mlp_shift_total,
        qkv_total,
        qkv_bias_total,
        out_total,
        attn_gain_total,
        attn_shift_total,
    ) = summed
    return (
        output,
        input_grad,
        attn_gain_total,
        attn_shift_total,
        mlp_gain_total,
        mlp_shift_total,
        qkv_total,
        qkv_bias_total,
        out_total,
        bias_total,
        up_total,
        up_bias_total,
        down_total,
        bias_total,
    )


PLANES = 4


MESH_ID = pl.DeviceIdType.MESH


def dot_nn(left, right):
    return jnp.dot(left, right, preferred_element_type=jnp.float32)


def half_turn(head, cosine, sine):
    first = head[:, :128]
    lane = lax.broadcasted_iota(jnp.int32, first.shape, 1)
    swapped = jnp.where(
        lane < ROT // 2, pltpu.roll(first, 128 - ROT // 2, 1), pltpu.roll(first, ROT // 2, 1)
    )
    return jnp.concatenate([first * cosine + swapped * sine, head[:, 128:]], axis=1)


def block_kernel(
    x_in,
    g_in,
    up_in,
    qkv_in,
    small_in,
    down,
    out_w,
    up_bias,
    cosine,
    sine,
    place_q,
    place_k,
    out_sum,
    back_sum,
    vec_all,
    small_out,
    down_tot,
    up_tot,
    outw_tot,
    qkv_tot,
    x_hbm,
    g_hbm,
    na_hbm,
    hp_hbm,
    got_down,
    got_up,
    got_outw,
    got_qkv,
    core_got,
    plane_got,
    up,
    qkv,
    gains,
    qkv_bias,
    xb,
    gb,
    hx,
    half_in,
    hid,
    prg,
    q,
    k,
    v,
    mg,
    mix,
    proj,
    stat,
    kacc,
    vacc,
    acc_down,
    acc_up,
    g_down,
    g_up,
    g_outw,
    g_qkv,
    cb,
    tmp,
    vec,
    vec_got,
    line_send,
    line_recv,
    side_send,
    side_recv,
    pair_send,
    core_tok_send,
    core_tok_recv,
    w_send,
    w_recv,
    wx_send,
    wx_recv,
    wy_send,
    wy_recv,
    wc_send,
    wc_recv,
    small_send,
    small_recv,
    gather_sem,
    load_sem,
    save_sem,
    tmp_sem,
    core_send,
    core_recv,
    plane_send,
    plane_recv,
    home_send,
    home_recv,
    y_send,
    y_recv,
    x_send,
    x_recv,
    a2a_send,
    a2a_recv,
    vec_send,
    vec_recv,
    local_sem,
):
    f32, bf16 = jnp.float32, jnp.bfloat16
    dp = lax.axis_index("dp")
    rank = lax.axis_index("ctx")
    z, core = dp // 2, dp % 2
    y, x = rank // 2, rank % 2
    core_to = (2 * z + 1 - core, rank)
    x_to = (dp, 2 * y + 1 - x)
    y_to = (dp, 2 * (1 - y) + x)
    pair_to = (2 * z + 1 - core, 2 * (1 - y) + x)
    seqs, length, width = x_hbm.shape
    tok = length // 4
    ff = up.shape[2]
    row_tile = 64
    half_part = width // (4 * PLANES)
    n_dp = 2 * PLANES
    part_rows = up_in.shape[0]
    section_cols = qkv_tot.shape[1] // 3
    scale = DH ** (-0.5)
    n_qkv = 3 * DH

    barrier = pltpu.get_barrier_semaphore()
    for target in (core_to, x_to, y_to, pair_to):
        pl.semaphore_signal(barrier, inc=1, device_id=target, device_id_type=MESH_ID)
    for shift in range(1, PLANES):
        for c in range(2):
            target = (2 * lax.rem(z + shift, PLANES) + c, rank)
            pl.semaphore_signal(barrier, inc=1, device_id=target, device_id_type=MESH_ID)
    pl.semaphore_wait(barrier, 4 + 2 * (PLANES - 1))

    def ds(first, size, step=None):
        return pl.ds(pl.multiple_of(first, step or size), size)

    def remote(src, dst, send, recv, target):
        return pltpu.make_async_remote_copy(
            src_ref=src,
            dst_ref=dst,
            send_sem=send,
            recv_sem=recv,
            device_id=target,
            device_id_type=MESH_ID,
        )

    pending = []

    def start(copy, when=None):
        if when is None or when is True:
            when = None
            copy.start()
        else:
            pl.when(when)(copy.start)
        pending.append((when, copy.wait_send))

    def start_local(copy, when=None):
        if when is None:
            copy.start()
        else:
            pl.when(when)(copy.start)
        pending.append((when, copy.wait))

    one, two = ds(x * tok, tok), ds((2 + x) * tok, tok)

    arrays = ((g_in, g_hbm), (x_in, x_hbm))
    mine = 2 * core + x
    theirs = 2 * core + 1 - x
    same_row = core == y

    def block_of(a, plane, ctx):
        return arrays[a][1].at[plane, ds(ctx * tok, tok)]

    def pair_copy(a, ctx):
        return remote(
            arrays[a][0], block_of(a, z, ctx), pair_send.at[a], line_recv.at[a, z], pair_to
        )

    def own_copy(a):
        return pltpu.make_async_copy(arrays[a][0], block_of(a, z, mine), gather_sem.at[a])

    def own_start(a):
        pl.when(jnp.logical_not(same_row))(pair_copy(a, 2 * y + x).start)
        pl.when(same_row)(own_copy(a).start)

    def own_arrived(a):
        pl.when(jnp.logical_not(same_row))(pair_copy(a, mine).wait_recv)
        pl.when(same_row)(own_copy(a).wait)

    quarter = part_rows // 4
    half = part_rows // 2
    up_rows = ds(rank * quarter, quarter)
    qkv_rows = ds(y * half, half)
    peers = [(s, c) for s in range(PLANES) for c in range(2)][1:]

    def small_copy(n):
        shift, c = peers[n]
        target = (2 * lax.rem(z + shift, PLANES) + lax.rem(core + c, 2), rank)
        return remote(small_in, small_out.at[dp], small_send.at[n], small_recv.at[n], target)

    small_own = pltpu.make_async_copy(small_in, small_out.at[dp], gather_sem.at[2])

    def up_cols(target):
        return up_in.at[:, ds(target * ff, ff)]

    def qkv_cols(target, section):
        return qkv_in.at[:, ds(section * section_cols + target * DH, DH)]

    own_weights = [pltpu.make_async_copy(up_cols(dp), up.at[dp], gather_sem.at[3])]
    core_weights = [
        remote(up_cols(core_to[0]), up.at[dp], wc_send.at[0], wc_recv.at[0], core_to)
    ]
    for section in range(3):
        columns = pl.ds(section * DH, DH)
        own_weights.append(
            pltpu.make_async_copy(
                qkv_cols(dp, section), qkv.at[dp, :, columns], gather_sem.at[4 + section]
            )
        )
        core_weights.append(
            remote(
                qkv_cols(core_to[0], section),
                qkv.at[dp, :, columns],
                wc_send.at[1 + section],
                wc_recv.at[1 + section],
                core_to,
            )
        )

    up_copies = []
    qkv_copies = []
    for shift in range(1, PLANES):
        plane = lax.rem(z + shift, PLANES)
        for c in range(2):
            target = (2 * plane + c, rank)
            up_copies.append(
                remote(
                    up_in.at[up_rows, ds(target[0] * ff, ff)],
                    up.at[dp, up_rows],
                    w_send.at[shift - 1, c, 0],
                    w_recv.at[shift - 1, core, 0],
                    target,
                )
            )
            for section in range(3):
                qkv_copies.append(
                    remote(
                        qkv_in.at[qkv_rows, ds(section * section_cols + target[0] * DH, DH)],
                        qkv.at[dp, qkv_rows, pl.ds(section * DH, DH)],
                        w_send.at[shift - 1, c, 1 + section],
                        w_recv.at[shift - 1, core, 1 + section],
                        target,
                    )
                )

    def carry(a, plane, when, along):
        block = block_of(a, plane, mine)
        recv = line_recv.at[a, plane]
        if along in (0, 1):
            start(
                remote(block, block, line_send.at[a, 0, plane], recv, (dp + 2, rank)),
                jnp.logical_and(when, z < PLANES - 1),
            )
        if along in (0, -1):
            start(
                remote(block, block, line_send.at[a, 1, plane], recv, (dp - 2, rank)),
                jnp.logical_and(when, z > 0),
            )
        start(remote(block, block, side_send.at[a, plane], side_recv.at[a, plane], x_to), when)
        sems = (core_tok_send.at[a, 0, plane], core_tok_recv.at[a, 0, plane])
        start(remote(block, block, *sems, core_to), when)

    def step_blocks(step):
        blocks = []
        for along in (1, -1):
            plane = z - along * step
            there = jnp.logical_and(plane >= 0, plane < PLANES)
            blocks.append((along, lax.rem(plane + PLANES, PLANES), there))
        return blocks

    def line_step(step, a):
        for along, plane, there in step_blocks(step):
            block = block_of(a, plane, mine)
            sems = (line_send.at[a, 0, plane], line_recv.at[a, plane])
            pl.when(there)(remote(block, block, *sems, core_to).wait_recv)
            carry(a, plane, there, along)

    def side_on(a, plane, when):
        block = block_of(a, plane, theirs)
        copy = remote(block, block, side_send.at[a, plane], side_recv.at[a, plane], core_to)
        pl.when(when)(copy.wait_recv)
        sems = (core_tok_send.at[a, 1, plane], core_tok_recv.at[a, 1, plane])
        start(remote(block, block, *sems, core_to), when)

    def side_step(step, a):
        for unused, plane, there in step_blocks(step):
            side_on(a, plane, there)

    def w_arrive(shift, c, part):
        source = 2 * lax.rem(z - shift + PLANES, PLANES) + c
        if part == 0:
            dst = up.at[source, up_rows]
        else:
            dst = qkv.at[source, qkv_rows, pl.ds((part - 1) * DH, DH)]
        sems = (w_send.at[shift - 1, c, part], w_recv.at[shift - 1, c, part])
        remote(dst, dst, *sems, core_to).wait_recv()

    def pair_of(shift):
        return pl.ds(2 * lax.rem(z - shift + PLANES, PLANES), 2)

    def quarter_of(ctx):
        return ds(ctx * quarter, quarter)

    def share_up(shift):
        for c in range(2):
            w_arrive(shift, c, 0)
        block = up.at[pair_of(shift), up_rows]
        start(remote(block, block, wx_send.at[shift - 1], wx_recv.at[shift - 1], x_to))
        start(remote(block, block, wy_send.at[shift - 1, 0], wy_recv.at[shift - 1, 0], y_to))

    def share_up_side(shift):
        block = up.at[pair_of(shift), quarter_of(2 * y + 1 - x)]
        remote(block, block, wx_send.at[shift - 1], wx_recv.at[shift - 1], x_to).wait_recv()
        start(remote(block, block, wy_send.at[shift - 1, 1], wy_recv.at[shift - 1, 1], y_to))

    def share_qkv(shift):
        for c in range(2):
            for part in range(1, 4):
                w_arrive(shift, c, part)
        block = qkv.at[pair_of(shift), qkv_rows]
        start(remote(block, block, wy_send.at[shift - 1, 2], wy_recv.at[shift - 1, 2], y_to))

    def qkv_send():
        for copy in qkv_copies:
            copy.start()

    def up_ready():
        for shift in range(1, PLANES):
            for n, side in enumerate((x, 1 - x)):
                block = up.at[pair_of(shift), quarter_of(2 * (1 - y) + side)]
                sems = (wy_send.at[shift - 1, n], wy_recv.at[shift - 1, n])
                remote(block, block, *sems, y_to).wait_recv()
        own_weights[0].wait()
        core_weights[0].wait()

    def qkv_ready():
        for shift in range(1, PLANES):
            block = qkv.at[pair_of(shift), ds((1 - y) * half, half)]
            sems = (wy_send.at[shift - 1, 2], wy_recv.at[shift - 1, 2])
            remote(block, block, *sems, y_to).wait_recv()
        for copy in own_weights[1:] + core_weights[1:]:
            copy.wait()

    def small_ready():
        small_own.wait()
        for n, (shift, c) in enumerate(peers):
            source = 2 * lax.rem(z - shift + PLANES, PLANES) + lax.rem(core + c, 2)
            dst = small_out.at[source]
            remote(small_in, dst, small_send.at[n], small_recv.at[n], core_to).wait()
        for i in range(4):
            for d in range(n_dp):
                gains[i : i + 1, d * part_rows : (d + 1) * part_rows] = small_out[d, i : i + 1, :]
        for section in range(3):
            block = n_dp * section + dp
            source, row = block // 3, 6 + lax.rem(block, 3)
            qkv_bias[:, section * DH : (section + 1) * DH] = small_out[source, pl.ds(row, 1), :]

    toward = jnp.where(z < PLANES // 2, 1, -1)
    far = jnp.where(z < PLANES // 2, PLANES - 1, 0)
    near = z + toward
    feed_order = (z, near, 6 - z - near - far, far)

    def sequence_ready(j):
        for a in range(2):
            for n, side in enumerate((x, 1 - x)):
                block = block_of(a, feed_order[j], 2 * (1 - core) + side)
                sems = (
                    core_tok_send.at[a, n, feed_order[j]],
                    core_tok_recv.at[a, n, feed_order[j]],
                )
                remote(block, block, *sems, core_to).wait_recv()
        for copy in load(feed_order[j], j % 2):
            copy.start()

    own_start(0)
    own_start(1)
    for copy in up_copies:
        copy.start()
    small_own.start()
    for n in range(len(peers)):
        small_copy(n).start()
    for copy in own_weights + core_weights:
        copy.start()

    def load(s, slot):
        return (
            pltpu.make_async_copy(x_hbm.at[s], xb.at[slot], load_sem.at[0, slot]),
            pltpu.make_async_copy(g_hbm.at[s], gb.at[slot], load_sem.at[1, slot]),
        )

    def save_norm(s):
        return pltpu.make_async_copy(hx.at[1], na_hbm.at[s], save_sem.at[0])

    def save_rows(s):
        copies = []
        for n, (ref, cols) in enumerate(((hid, pl.ds(0, ff)), (prg, pl.ds(ff, ff)))):
            for h, rows in enumerate((one, two)):
                copies.append(
                    pltpu.make_async_copy(
                        ref.at[rows],
                        hp_hbm.at[s, pl.ds(h * tok, tok), cols],
                        save_sem.at[1 + 2 * n + h],
                    )
                )
        return copies

    def clear(ref):
        @pl.loop(0, ref.shape[0] // 64)
        def rows(i):
            ref[ds(i * 64, 64), :] = jnp.zeros((64, ref.shape[1]), f32)

    def choose_half(src, slot):
        for d in range(width // 256):
            half_in[:, d * 128 : (d + 1) * 128] = src[slot, :, ds(d * 256 + x * 128, 128)]

    def feed(slot, tile):
        c = ds(tile * 256, 256)
        columns = up[:, :, c].reshape(width, 256)
        pre = dot_nn(hx[0], columns) + up_bias[:, c]
        hidden_grad = contract_cols(gb[slot], down[c, :])
        cdf = 0.5 * (1.0 + lax.erf(pre * (0.5**0.5)))
        pdf = jnp.exp(-0.5 * pre * pre) * ((2.0 * 3.141592653589793) ** -0.5)
        hid[:, c] = (pre * cdf).astype(bf16)
        prg[:, c] = (hidden_grad * (cdf + pre * pdf)).astype(bf16)

    def feed_down(slot, m):
        r = ds(m * 256, 256)
        acc_down[r, :] += contract_rows(hid[:, ds(x * (ff // 2) + m * 256, 256)], gb[slot])

    def feed_forward(j, tick):
        s = feed_order[j]
        slot = j % 2
        for copy in load(s, slot):
            copy.wait()
        if j > 0:
            save_norm(feed_order[j - 1]).wait()
            for copy in save_rows(feed_order[j - 1]):
                copy.wait()

        @pl.loop(0, length // row_tile)
        def norm(i):
            r = ds(i * row_tile, row_tile)
            value = xb[slot, r, :].astype(f32)
            centre = value - jnp.mean(value, axis=1, keepdims=True)
            inv = lax.rsqrt(jnp.mean(centre * centre, axis=1, keepdims=True) + EPS_NORM)
            hat = centre * inv
            hx[1, r, :] = (hat * gains[0:1, :] + gains[1:2, :]).astype(bf16)
            hx[0, r, :] = (hat * gains[2:3, :] + gains[3:4, :]).astype(bf16)

        save_norm(s).start()
        choose_half(hx, 0)
        tick(j, 0)

        @pl.loop(0, 2)
        def first_tiles(m):
            feed(slot, 2 * x + m)
            feed_down(slot, m)

        if j == seqs - 1:
            rounded(g_down, acc_down, g_down.shape[0], width)
            for piece in (0, 1):
                y_copy(0, piece).start()
        tick(j, 1)

        @pl.loop(0, 2)
        def last_tiles(m):
            feed(slot, 2 * (1 - x) + m)

        for copy in save_rows(s):
            copy.start()
        tick(j, 2)

        @pl.loop(0, width // 512)
        def gup(m):
            r = ds(m * 256, 256)
            acc_up[r, :] += contract_rows(half_in[:, r], prg[...])

        rows_sum = jnp.sum(prg[one, :].astype(f32), axis=0, keepdims=True)
        rows_sum += jnp.sum(prg[two, :].astype(f32), axis=0, keepdims=True)
        vec[0, 6:7, 0:ff] += rows_sum
        tick(j, 3)

    def add_rows(dst, src, rows):
        @pl.loop(0, rows // 32)
        def tiles(i):
            r = ds(i * 32, 32)
            dst[r, :] = (dst[r, :].astype(f32) + src[r, :].astype(f32)).astype(bf16)

    def add_pieces(pieces):
        copies = []
        first = 0
        for n, (dst, src) in enumerate(pieces):
            rows, cols = dst.shape
            here = tmp.at[first : first + rows, 0:cols]
            copy = pltpu.make_async_copy(src, here, tmp_sem.at[n])
            copy.start()
            copies.append((copy, dst, here, rows))
            first += rows
        for copy, dst, here, rows in copies:
            copy.wait()
            add_rows(dst, here, rows)

    down_pieces = g_down.shape[0] // tok

    def y_copy(kind, piece):
        sems = (y_send.at[kind, piece], y_recv.at[kind, piece])
        if kind == 0:
            rows = pl.ds(piece * tok, tok)
            return remote(g_down.at[rows], got_down.at[rows], *sems, y_to)
        if kind == 1:
            return remote(g_outw, got_outw, *sems, y_to)
        src, got = (g_up, got_up) if kind == 2 else (g_qkv, got_qkv)
        pair = pl.ds(2 * lax.rem(z + piece, PLANES), 2)
        return remote(src.at[pair], got.at[pair], *sems, y_to)

    half_rows = ds(x * half_part, half_part)
    other_half = ds((1 - x) * half_part, half_part)

    def column_parts(kind, index, source):
        if kind == 2:
            return [(g_up.at[index], up_tot.at[half_rows, ds(source * ff, ff)])]
        return [
            (
                g_qkv.at[index, :, pl.ds(n * DH, DH)],
                qkv_tot.at[half_rows, ds(n * section_cols + source * DH, DH)],
            )
            for n in range(3)
        ]

    def side_parts(kind, plane, rows):
        if kind == 2:
            return [up_tot.at[rows, ds(plane * 2 * ff, 2 * ff)]]
        return [qkv_tot.at[rows, ds(n * section_cols + plane * 2 * DH, 2 * DH)] for n in range(3)]

    def reduced(kind, piece):
        y_copy(kind, piece).wait()
        if kind == 0:
            rows = pl.ds(piece * tok, tok)
            add_pieces([(g_down.at[rows], got_down.at[rows])])
            place = down_tot.at[ds(x * g_down.shape[0] + piece * tok, tok)]
            start_local(pltpu.make_async_copy(g_down.at[rows], place, local_sem.at[2 + piece]))
            start(remote(g_down.at[rows], place, x_send.at[0, piece], x_recv.at[0, piece], x_to))
            return
        if kind == 1:
            add_pieces([(g_outw, got_outw)])
            place = outw_tot.at[half_rows]
            start_local(pltpu.make_async_copy(g_outw, place, local_sem.at[6]))
            start(remote(g_outw, place, x_send.at[1, 0], x_recv.at[1, 0], x_to))
            return
        got, own = ((got_up, g_up), (got_qkv, g_qkv))[kind - 2]
        plane = lax.rem(z + piece, PLANES)
        add_pieces([(own.at[2 * plane + c], got.at[2 * plane + c]) for c in range(2)])
        for c in range(2):
            for part, (src, dst) in enumerate(column_parts(kind, 2 * plane + c, dp)):
                send = a2a_send.at[kind - 2, piece, c, part]
                recv = a2a_recv.at[kind - 2, piece, core, part]
                copy = remote(src, dst, send, recv, (2 * plane + c, rank))
                if piece == 0:
                    local = pltpu.make_async_copy(
                        src, dst, local_sem.at[7 + 3 * (kind - 2) + part]
                    )
                    pl.when(core == c)(local.start)
                    start(copy, core != c)
                else:
                    start(copy)

    def share(kind, shift):
        plane = lax.rem(z - shift + PLANES, PLANES)
        for c in range(2):
            for part, (src, dst) in enumerate(column_parts(kind, 2 * plane + c, 2 * plane + c)):
                recv = a2a_recv.at[kind - 2, shift, c, part]
                copy = remote(dst, dst, a2a_send.at[kind - 2, shift, c, part], recv, core_to)
                if shift == 0:
                    pl.when(core != c)(copy.wait_recv)
                    local = pltpu.make_async_copy(
                        src, dst, local_sem.at[7 + 3 * (kind - 2) + part]
                    )
                    pl.when(core == c)(local.wait)
                else:
                    copy.wait_recv()
        for part, block in enumerate(side_parts(kind, plane, half_rows)):
            sems = (x_send.at[kind + part, shift], x_recv.at[kind + part, shift])
            start(remote(block, block, *sems, x_to))

    order = (0, 3, 2, 1)

    def core_copy(i):
        s = order[i]
        return remote(
            cb.at[seqs + i % 2], core_got.at[s], core_send.at[i], core_recv.at[i], core_to
        )

    def chip_sum(i):
        s = order[i]
        core_copy(i).wait_recv()
        add_pieces([(cb.at[i, a], core_got.at[s, a]) for a in range(2)])
        start(flow_copy(i, 0), jnp.logical_and(z == 0, s > 0))
        start(flow_copy(i, 1), jnp.logical_and(z == PLANES - 1, s < PLANES - 1))

    def flow_copy(i, side):
        s = order[i]
        sems = (plane_send.at[i], plane_recv.at[side, s])
        return remote(cb.at[i], plane_got.at[side, s], *sems, (dp + (2, -2)[side], rank))

    def flow_add(i, side):
        flow_copy(i, side).wait_recv()
        add_pieces([(cb.at[i, a], plane_got.at[side, order[i], a]) for a in range(2)])

    def flow_relay(i, hop):
        s = order[i]
        for side, plane in enumerate((hop, PLANES - 1 - hop)):
            if (plane < s) if side == 0 else (plane > s):
                here = z == plane
                pl.when(here)(functools.partial(flow_add, i, side))
                start(flow_copy(i, side), here)

    def flow_end(i):
        s = order[i]

        @pl.when(z == s)
        def both():
            if s > 0:
                flow_add(i, 0)
            if s < PLANES - 1:
                flow_add(i, 1)

        same = core == y
        for a, result in enumerate((out_sum, back_sum)):
            block = cb.at[i, a]
            start_local(
                pltpu.make_async_copy(block, result, local_sem.at[a]),
                jnp.logical_and(z == s, same),
            )
            start(
                remote(block, result, home_send.at[a], home_recv.at[a], pair_to),
                jnp.logical_and(z == s, jnp.logical_not(same)),
            )

    def rounded(dst, src, rows, cols):
        @pl.loop(0, rows // 64)
        def tiles(i):
            r = ds(i * 64, 64)
            dst[r, :] = src[r, 0:cols].astype(bf16)

    def rounded_columns(dst, src, cols):
        @pl.loop(0, dst.shape[0])
        def blocks(d):
            dst[d] = src[ds(d * half_part, half_part), 0:cols].astype(bf16)

    def load_again(i, slot):
        s = order[i]
        copies = [
            pltpu.make_async_copy(na_hbm.at[s], xb.at[slot], load_sem.at[0, slot]),
            pltpu.make_async_copy(g_hbm.at[s], gb.at[slot], load_sem.at[1, slot]),
            pltpu.make_async_copy(
                hp_hbm.at[s], hx.at[slot, pl.ds(2 * tok, 2 * tok)], load_sem.at[2, slot]
            ),
        ]
        for h, rows in enumerate((one, two)):
            copies.append(
                pltpu.make_async_copy(
                    x_hbm.at[s, rows],
                    hx.at[slot, pl.ds(h * tok, tok)],
                    load_sem.at[3 + h, slot],
                )
            )
        return copies

    feed_plan = {
        (0, 0): [(share_up_side, 1), (share_up_side, 2), (share_up_side, 3), (line_step, 2, 0), (line_step, 2, 1), (up_ready,)],
        (0, 1): [(side_step, 1, 0)],
        (0, 2): [(side_step, 1, 1)],
        (0, 3): [(line_step, 3, 0), (sequence_ready, 1)],
        (1, 0): [(side_step, 2, 0)],
        (1, 1): [(line_step, 3, 1)],
        (1, 3): [(side_step, 2, 1), (sequence_ready, 2)],
        (2, 0): [(share_qkv, 1)],
        (2, 1): [(share_qkv, 2)],
        (2, 2): [(side_step, 3, 0), (share_qkv, 3)],
        (2, 3): [(side_step, 3, 1), (sequence_ready, 3)],
    }

    def feed_tick(j, point):
        for step, *which in feed_plan.get((j, point), ()):
            step(*which)

    clear(acc_down)
    clear(acc_up)
    vec[...] = jnp.zeros_like(vec)
    for a in range(2):
        own_arrived(a)
        carry(a, z, True, 0)
    for a in range(2):
        side_on(a, z, True)
    for shift in range(1, PLANES):
        share_up(shift)
    line_step(1, 0)
    sequence_ready(0)
    small_ready()
    line_step(1, 1)
    qkv_send()
    for j in range(seqs):
        feed_forward(j, feed_tick)
    save_norm(feed_order[-1]).wait()
    for copy in save_rows(feed_order[-1]):
        copy.wait()

    for copy in load_again(0, 0):
        copy.start()
    rounded_columns(g_up, acc_up, ff)
    for shift in (1, 0, 2, 3):
        y_copy(2, shift).start()
    for piece in range(2, down_pieces):
        y_copy(0, piece).start()
    clear(acc_up)
    clear(acc_down.at[0:tok])
    qkv_ready()

    def attention(i, tick):
        slot = i % 2
        for copy in load_again(i, slot):
            copy.wait()
        if i + 1 < seqs:
            for copy in load_again(i + 1, 1 - slot):
                copy.start()
        tick(i, 0)
        choose_half(xb, slot)
        for n, ref in enumerate((q, k, v)):
            c = slice(n * DH, (n + 1) * DH)
            columns = qkv[:, :, c].reshape(width, DH)
            part = dot_nn(xb[slot], columns) + qkv_bias[:, c]
            if n < 2:
                part = half_turn(part, cosine[...], sine[...])
            ref[...] = part.astype(bf16)
        mg[...] = contract_cols(gb[slot], out_w[...]).astype(bf16)
        tick(i, 1)
        kacc[...] = jnp.zeros_like(kacc)
        vacc[...] = jnp.zeros_like(vacc)

        @pl.loop(0, 4)
        def attend(part):
            r = ds(part * tok, tok)
            scores = contract_cols(q[r, :], k[...]) * scale
            scores = jnp.where(place_k[...] <= place_q[r, :], scores, MASK_FILL)
            exponent = jnp.exp(scores - jnp.max(scores, axis=1, keepdims=True))
            prob = exponent / jnp.sum(exponent, axis=1, keepdims=True)
            low = prob.astype(bf16)
            mix[r, :] = dot_nn(low, v[...]).astype(bf16)
            prob_grad = contract_cols(mg[r, :], v[...])
            row_dot = jnp.sum(prob_grad * prob, axis=1, keepdims=True)
            score_grad = (prob * (prob_grad - row_dot)).astype(bf16)
            query_grad = dot_nn(score_grad, k[...]) * scale
            proj[r, 0:DH] = half_turn(query_grad, cosine[r, :], -sine[r, :]).astype(bf16)
            kacc[...] += contract_rows(score_grad, q[r, :])
            vacc[...] += contract_rows(low, mg[r, :])

        proj[:, DH : 2 * DH] = half_turn(kacc[...] * scale, cosine[...], -sine[...]).astype(bf16)
        proj[:, 2 * DH : 3 * DH] = vacc[...].astype(bf16)
        tick(i, 2)
        acc_down[0:tok, :] += contract_rows(mix[:, ds(x * 128, 128)], gb[slot])

        @pl.loop(0, width // 512)
        def gqkv(m):
            r = ds(m * 256, 256)
            acc_up[r, 0:n_qkv] += contract_rows(half_in[:, r], proj[...])

        tick(i, 3)
        value = hx[slot, 0 : 2 * tok, :].astype(f32)
        mean = jnp.mean(value, axis=1, keepdims=True)
        centre = value - mean
        stat[0] = mean
        stat[1] = lax.rsqrt(jnp.mean(centre * centre, axis=1, keepdims=True) + EPS_NORM)
        if i >= 2:
            core_copy(i - 2).wait_send()

        def picked(ref):
            return jnp.concatenate([ref[one, :], ref[two, :]], axis=0)

        place = [jnp.where(core == h, i, seqs + i % 2) for h in range(2)]
        later = slice(2 * tok, 4 * tok)

        @pl.loop(0, width // 256)
        def followers(n):
            c = ds(n * 256, 256)
            out = dot_nn(hx[slot, later, 0:ff], down[:, c]) + dot_nn(picked(mix), out_w[:, c])
            mlp_back = contract_cols(hx[slot, later, ff : 2 * ff], up[n])
            attn_back = contract_cols(picked(proj), qkv[n])
            back = attn_back * gains[0:1, c] + mlp_back * gains[2:3, c]
            for h in range(2):
                rows = slice(h * tok, (h + 1) * tok)
                cb[place[h], 0, :, c] = out[rows].astype(bf16)
                cb[place[h], 1, :, c] = back[rows].astype(bf16)
            hat = (hx[slot, 0 : 2 * tok, c].astype(f32) - stat[0]) * stat[1]
            grad = jnp.concatenate([gb[slot, one, c], gb[slot, two, c]], axis=0).astype(f32)
            sums = (attn_back * hat, attn_back, mlp_back * hat, mlp_back, grad)
            for n_sum, term in enumerate(sums):
                vec[0, n_sum : n_sum + 1, c] += jnp.sum(term, axis=0, keepdims=True)

        vec[0, 5:6, 0:n_qkv] += jnp.sum(picked(proj).astype(f32), axis=0, keepdims=True)
        core_copy(i).start()
        tick(i, 4)

    plan = {
        (0, 1): [(reduced, 0, 0)],
        (0, 3): [(reduced, 0, 1)],
        (1, 1): [(chip_sum, 0)],
        (1, 2): [(reduced, 2, 1)],
        (2, 0): [(reduced, 2, 0)],
        (2, 1): [(chip_sum, 1), (share, 2, 1)],
        (2, 2): [(share, 2, 0)],
        (2, 3): [(reduced, 2, 2), (flow_relay, 0, 1)],
        (3, 1): [(chip_sum, 2), (reduced, 2, 3)],
        (3, 2): [(flow_relay, 1, 1)],
        (3, 4): [(flow_relay, 0, 2), (reduced, 0, 2), (share, 2, 2)],
    }

    def tick(i, point):
        for step, *which in plan.get((i, point), ()):
            step(*which)

    for i in range(seqs):
        attention(i, tick)

    rounded_columns(g_qkv, acc_up, n_qkv)
    for shift in (1, 2, 3, 0):
        y_copy(3, shift).start()
    rounded(g_outw, acc_down, tok, width)
    y_copy(1, 0).start()

    def vec_copy(n):
        target = (x_to, y_to)[n]
        return remote(vec.at[n], vec_got.at[n], vec_send.at[n], vec_recv.at[n], target)

    vec_copy(0).start()
    chip_sum(3)
    flow_relay(2, 1)
    reduced(0, 3)
    vec_copy(0).wait()
    vec[1] = vec[0] + vec_got[0]
    vec_copy(1).start()
    share(2, 3)
    flow_relay(1, 2)
    reduced(3, 1)
    vec_copy(1).wait()
    vec_all[dp] = vec[1] + vec_got[1]
    for n, (shift, c) in enumerate(peers):
        target = (2 * lax.rem(z + shift, PLANES) + lax.rem(core + c, 2), rank)
        start(
            remote(
                vec_all.at[dp], vec_all.at[dp], vec_send.at[2 + n], vec_recv.at[2 + n], target
            )
        )
    flow_end(0)
    reduced(3, 2)
    flow_relay(3, 1)
    share(3, 1)
    flow_end(2)
    reduced(3, 3)
    flow_end(1)
    reduced(3, 0)
    share(3, 2)
    share(3, 0)
    flow_end(3)
    reduced(1, 0)
    share(3, 3)

    for copy in up_copies + qkv_copies:
        copy.wait_send()
    for a in range(2):
        pl.when(jnp.logical_not(same_row))(pair_copy(a, 2 * y + x).wait_send)
    for n, (shift, c) in enumerate(peers):
        source = 2 * lax.rem(z - shift + PLANES, PLANES) + lax.rem(core + c, 2)
        block = vec_all.at[source]
        remote(block, block, vec_send.at[2 + n], vec_recv.at[2 + n], core_to).wait_recv()
    for piece in range(down_pieces):
        block = down_tot.at[ds((1 - x) * g_down.shape[0] + piece * tok, tok)]
        remote(block, block, x_send.at[0, piece], x_recv.at[0, piece], x_to).wait_recv()
    block = outw_tot.at[other_half]
    remote(block, block, x_send.at[1, 0], x_recv.at[1, 0], x_to).wait_recv()
    for kind in (2, 3):
        for shift in range(PLANES):
            plane = lax.rem(z - shift + PLANES, PLANES)
            for part, block in enumerate(side_parts(kind, plane, other_half)):
                sems = (x_send.at[kind + part, shift], x_recv.at[kind + part, shift])
                remote(block, block, *sems, x_to).wait_recv()
    for a, result in enumerate((out_sum, back_sum)):
        copy = remote(result, result, home_send.at[a], home_recv.at[a], pair_to)
        pl.when(core != y)(copy.wait_recv)
    for i in range(seqs - 2, seqs):
        core_copy(i).wait_send()
    for when, wait in pending:
        if when is None:
            wait()
        else:
            pl.when(when)(wait)


def block_compute(tokens, cotangent, w_up, w_qkv, small, w_down, w_out, up_bias, place):
    f32, bf16 = jnp.float32, jnp.bfloat16
    n_dp = 2 * PLANES
    tok, width = tokens.shape
    seqs, length = PLANES, 4 * tok
    part_rows = w_up.shape[0]
    ff = w_up.shape[1] // n_dp
    half_part = width // (2 * n_dp)
    half_rot = ROT // 2
    frequency = ROPE_BASE ** (-2.0 * jnp.arange(half_rot, dtype=f32) / ROT)
    angles = place.astype(f32)[:, None] * frequency[None, :]
    rest = jnp.zeros((length, 128 - ROT), f32)
    cosine = jnp.concatenate([jnp.cos(angles), jnp.cos(angles), rest + 1.0], axis=1)
    sine = jnp.concatenate([-jnp.sin(angles), jnp.sin(angles), rest], axis=1)
    hbm = pl.BlockSpec(memory_space=pl.ANY)
    vmem = pl.BlockSpec(memory_space=pltpu.VMEM)
    dma = pltpu.SemaphoreType.DMA

    def shape(*dims, dtype=bf16):
        return jax.ShapeDtypeStruct(dims, dtype)

    def buf(*dims, dtype=bf16):
        return pltpu.VMEM(dims, dtype)

    results = pl.pallas_call(
        block_kernel,
        out_shape=(
            shape(tok, width),
            shape(tok, width),
            shape(n_dp, 8, width, dtype=f32),
            shape(n_dp, *small.shape, dtype=f32),
            shape(ff, width),
            shape(2 * half_part, n_dp * ff),
            shape(DH, width),
            shape(2 * half_part, n_dp * 3 * DH),
            shape(seqs, length, width),
            shape(seqs, length, width),
            shape(seqs, length, width),
            shape(seqs, 2 * tok, 2 * ff),
            shape(ff // 2, width),
            shape(n_dp, half_part, ff),
            shape(DH // 2, width),
            shape(n_dp, half_part, 3 * DH),
            shape(seqs, 2, tok, width),
            shape(2, seqs, 2, tok, width),
        ),
        in_specs=[hbm] * 5 + [vmem] * 7,
        out_specs=(hbm, hbm, vmem, vmem) + (hbm,) * 14,
        scratch_shapes=[
            buf(n_dp, part_rows, ff),
            buf(n_dp, part_rows, 3 * DH),
            buf(8, width, dtype=f32),
            buf(1, 3 * DH, dtype=f32),
            buf(2, length, width),
            buf(2, length, width),
            buf(2, length, width),
            buf(length, width // 2),
            buf(length, ff),
            buf(length, ff),
            buf(length, DH),
            buf(length, DH),
            buf(length, DH),
            buf(length, DH),
            buf(length, DH),
            buf(length, 3 * DH),
            buf(2, 2 * tok, 1, dtype=f32),
            buf(length, DH, dtype=f32),
            buf(length, DH, dtype=f32),
            buf(ff // 2, width, dtype=f32),
            buf(width // 2, ff, dtype=f32),
            buf(ff // 2, width),
            buf(n_dp, half_part, ff),
            buf(DH // 2, width),
            buf(n_dp, half_part, 3 * DH),
            buf(seqs + 2, 2, tok, width),
            buf(2 * tok, width),
            buf(2, 8, width, dtype=f32),
            buf(2, 8, width, dtype=f32),
            dma((2, 2, PLANES)),
            dma((2, PLANES)),
            dma((2, PLANES)),
            dma((2, PLANES)),
            dma((2,)),
            dma((2, 2, PLANES)),
            dma((2, 2, PLANES)),
            dma((3, 2, 4)),
            dma((3, 2, 4)),
            dma((3,)),
            dma((3,)),
            dma((3, 3)),
            dma((3, 3)),
            dma((4,)),
            dma((4,)),
            dma((7,)),
            dma((7,)),
            dma((7,)),
            dma((5, 2)),
            dma((5,)),
            dma((2,)),
            dma((seqs,)),
            dma((seqs,)),
            dma((seqs,)),
            dma((2, seqs)),
            dma((2,)),
            dma((2,)),
            dma((4, 4)),
            dma((4, 4)),
            dma((6, 4)),
            dma((6, 4)),
            dma((2, PLANES, 2, 3)),
            dma((2, PLANES, 2, 3)),
            dma((9,)),
            dma((9,)),
            dma((13,)),
        ],
        compiler_params=pltpu.CompilerParams(
            collective_id=2, has_side_effects=True, vmem_limit_bytes=63 * 2**20
        ),
    )(
        tokens,
        cotangent,
        w_up,
        w_qkv,
        small,
        w_down,
        w_out,
        up_bias,
        cosine,
        sine,
        place[:, None],
        place[None, :],
    )
    return results[:8]


def column_local(
    tokens,
    cotangent,
    pair_index,
    norm1_gain,
    norm1_bias,
    norm2_gain,
    norm2_bias,
    w_qkv,
    b_qkv,
    w_out,
    b_out,
    w_up,
    b_up,
    w_down,
    b_down,
):
    bf16, f32 = jnp.bfloat16, jnp.float32
    tok_count, width = tokens.shape[1:]
    n_dp = H
    dp_rank = lax.axis_index("dp")
    rank = lax.axis_index("ctx")
    z, core = dp_rank // 2, dp_rank % 2
    y, x = rank // 2, rank % 2
    part = width // n_dp
    ff_part = w_up.shape[1] // n_dp
    qkv_part = 3 * DH
    seq_len = 4 * tok_count
    place = positions(pair_index, tok_count)

    small = jnp.concatenate(
        [norm1_gain, norm1_bias, norm2_gain, norm2_bias, b_out, b_down, b_qkv]
    ).reshape(-1, part)
    small = jnp.pad(small, ((0, -small.shape[0] % 16), (0, 0))).astype(f32)
    out_sum, back_sum, vec_all, small_all, down_total, up_total, out_total, qkv_total = (
        block_compute(
            tokens[0],
            cotangent[0],
            w_up,
            w_qkv,
            small,
            w_down,
            w_out,
            b_up.astype(f32)[None],
            place,
        )
    )
    back_sum = back_sum.astype(f32)
    out_bias, down_bias = (small_all[:, i].reshape(width) for i in (4, 5))
    own_rows = tokens[0].astype(f32)
    output = (own_rows + out_sum.astype(f32) + out_bias + down_bias).astype(bf16)[None]

    own_centre = own_rows - jnp.mean(own_rows, axis=-1, keepdims=True)
    own_inv = lax.rsqrt(jnp.mean(own_centre * own_centre, axis=-1, keepdims=True) + EPS_NORM)
    own_hat = own_centre * own_inv
    norm_back = (
        back_sum
        - jnp.mean(back_sum, axis=-1, keepdims=True)
        - own_hat * jnp.mean(back_sum * own_hat, axis=-1, keepdims=True)
    ) * own_inv
    input_grad = (cotangent[0].astype(f32) + norm_back).astype(bf16)[None]

    totals = jnp.sum(vec_all[:, :4], axis=0)
    mine = lax.dynamic_slice_in_dim(totals, dp_rank * part, part, 1)
    gain1_total, shift1_total, gain2_total, shift2_total = mine
    own_vec = lax.dynamic_index_in_dim(vec_all, dp_rank, 0, keepdims=False)
    bias_total = lax.dynamic_slice_in_dim(own_vec[4], dp_rank * part, part)
    up_bias_total = own_vec[6, :ff_part]
    qkv_bias_total = vec_all[:, 5, :qkv_part].reshape(n_dp, 3, DH).swapaxes(0, 1).reshape(-1)
    qkv_bias_total = lax.dynamic_slice_in_dim(
        qkv_bias_total, dp_rank * b_qkv.shape[0], b_qkv.shape[0]
    )
    return (
        output,
        input_grad,
        gain1_total,
        shift1_total,
        gain2_total,
        shift2_total,
        qkv_total.astype(f32),
        qkv_bias_total,
        out_total.astype(f32),
        bias_total,
        up_total.astype(f32),
        up_bias_total,
        down_total.astype(f32),
        bias_total,
    )


def solution(mesh):
    local = column_local if mesh.shape["dp"] == H and mesh.shape["ctx"] == 4 else plain_local
    placed = (
        P("dp", "ctx", None),
        P("dp", "ctx", None),
        P(),
        P("dp"),
        P("dp"),
        P("dp"),
        P("dp"),
        P("dp", None),
        P("dp"),
        P("dp", None),
        P("dp"),
        P("dp", None),
        P("dp"),
        P("dp", None),
        P("dp"),
    )
    return jax.shard_map(
        local,
        mesh=mesh,
        in_specs=placed,
        out_specs=(
            P("dp", "ctx", None),
            P("dp", "ctx", None),
            P("dp"),
            P("dp"),
            P("dp"),
            P("dp"),
            P("dp", None),
            P("dp"),
            P("dp", None),
            P("dp"),
            P("dp", None),
            P("dp"),
            P("dp", None),
            P("dp"),
        ),
        check_vma=False,
    )
```

```python
import functools

import jax
import jax.numpy as jnp
import numpy as np
from jax import lax
from jax.experimental import pallas as pl
from jax.experimental.pallas import tpu as pltpu
from jax.sharding import PartitionSpec as P

H = 8
DH = 256
ROT = 64


EPS_NORM = 1e-05
ROPE_BASE = 10000.0
MASK_FILL = -1000000000.0


def shortened(x):

    def short(part):
        return part.astype(jnp.bfloat16) if part.dtype == jnp.float32 else part

    return jax.tree.map(short, x)


def layer_norm(values_in, gain_vec, offset):
    centre = values_in - jnp.mean(values_in, axis=-1, keepdims=True)
    spread = jnp.mean(centre * centre, axis=-1, keepdims=True)
    return centre * lax.rsqrt(spread + EPS_NORM) * gain_vec + offset


def norm_grads(values_in, gain_vec, offset, upstream):
    unused, pullback = jax.vjp(layer_norm, values_in, gain_vec, offset)
    return pullback(upstream)


def positions(pair_index, tok_count):
    ranks_total = pair_index.shape[0]
    half_len = tok_count // 2
    index_all = jnp.arange(ranks_total * tok_count, dtype=jnp.int32)
    owner_rank = index_all // tok_count
    within = index_all % tok_count
    match_table = owner_rank[:, None] == jnp.arange(ranks_total, dtype=jnp.int32)[None, :]
    first_block = jnp.sum(jnp.where(match_table, pair_index[None, :], 0), axis=1)
    block_id = jnp.where(within < half_len, first_block, 2 * ranks_total - 1 - first_block)
    return block_id * half_len + within % half_len


def rotary(head_vals, token_place, turn_sign):
    half_rot = ROT // 2
    frequency = ROPE_BASE ** (-2.0 * jnp.arange(half_rot, dtype=jnp.float32) / ROT)
    angles = token_place.astype(jnp.float32)[:, None] * frequency[None, :]
    cosine = jnp.cos(angles)[:, None, :]
    sine_part = turn_sign * jnp.sin(angles)[:, None, :]
    first_half = head_vals[..., :half_rot]
    second = head_vals[..., half_rot:ROT]
    return jnp.concatenate(
        [
            first_half * cosine - second * sine_part,
            second * cosine + first_half * sine_part,
            head_vals[..., ROT:],
        ],
        axis=-1,
    )


def contract_rows(left, right):
    return lax.dot_general(
        left, right, (((0,), (0,)), ((), ())), preferred_element_type=jnp.float32
    )


def contract_cols(left, right):
    return lax.dot_general(
        left, right, (((1,), (1,)), ((), ())), preferred_element_type=jnp.float32
    )


def plain_local(
    tokens,
    cotangent,
    pair_index,
    norm1_gain,
    norm1_bias,
    norm2_gain,
    norm2_bias,
    w_qkv,
    b_qkv,
    w_out,
    b_out,
    w_up,
    b_up,
    w_down,
    b_down,
):
    seq_dev, tok_count, width = tokens.shape
    row_count = seq_dev * tok_count
    head_shape = (seq_dev, tok_count, H, DH)
    score_scale = DH ** (-0.5)
    device_rank = lax.axis_index("ctx")
    all_place = positions(pair_index, tok_count)
    own_place = lax.dynamic_slice_in_dim(all_place, device_rank * tok_count, tok_count)
    allowed = all_place[None, None, None, :] <= own_place[None, None, :, None]
    gathered = (
        lax.all_gather(norm1_gain, "dp", axis=0, tiled=True),
        lax.all_gather(norm1_bias, "dp", axis=0, tiled=True),
        lax.all_gather(norm2_gain, "dp", axis=0, tiled=True),
        lax.all_gather(norm2_bias, "dp", axis=0, tiled=True),
        lax.all_gather(w_qkv, "dp", axis=0, tiled=True),
        lax.all_gather(b_qkv, "dp", axis=0, tiled=True),
        lax.all_gather(w_out, "dp", axis=0, tiled=True),
        lax.all_gather(b_out, "dp", axis=0, tiled=True),
        lax.all_gather(w_up, "dp", axis=0, tiled=True),
        lax.all_gather(b_up, "dp", axis=0, tiled=True),
        lax.all_gather(w_down, "dp", axis=0, tiled=True),
        lax.all_gather(b_down, "dp", axis=0, tiled=True),
    )
    (
        attn_gain,
        attn_shift,
        mlp_gain,
        mlp_shift,
        qkv_weight,
        qkv_bias,
        out_weight,
        out_bias,
        up_weight,
        up_bias,
        down_weight,
        down_bias,
    ) = gathered
    token_rows = tokens.reshape(row_count, width).astype(jnp.float32)
    normed_attn = layer_norm(
        token_rows, attn_gain.astype(jnp.float32), attn_shift.astype(jnp.float32)
    ).astype(jnp.bfloat16)
    normed_mlp = layer_norm(
        token_rows, mlp_gain.astype(jnp.float32), mlp_shift.astype(jnp.float32)
    ).astype(jnp.bfloat16)
    projected = jnp.dot(
        normed_attn, qkv_weight, preferred_element_type=jnp.float32
    ) + qkv_bias.astype(jnp.float32)
    queries = rotary(projected[:, :width].reshape(head_shape), own_place, 1.0).astype(jnp.bfloat16)
    key_local = (
        rotary(projected[:, width : 2 * width].reshape(head_shape), own_place, 1.0)
        .astype(jnp.bfloat16)
        .reshape(seq_dev, tok_count, width)
    )
    value_local = projected[:, 2 * width :].astype(jnp.bfloat16).reshape(seq_dev, tok_count, width)
    key_all, value_all = (
        lax.all_gather(key_local, "ctx", axis=1, tiled=True),
        lax.all_gather(value_local, "ctx", axis=1, tiled=True),
    )
    seq_len = key_all.shape[1]
    key_heads = key_all.reshape(seq_dev, seq_len, H, DH)
    value_heads = value_all.reshape(seq_dev, seq_len, H, DH)
    raw_scores = (
        jnp.einsum("sqhd,skhd->shqk", queries, key_heads, preferred_element_type=jnp.float32)
        * score_scale
    )
    raw_scores = jnp.where(allowed, raw_scores, MASK_FILL)
    row_max = jnp.max(raw_scores, axis=-1, keepdims=True)
    exponent = jnp.exp(raw_scores - row_max)
    row_total = jnp.sum(exponent, axis=-1, keepdims=True)
    log_norm = row_max + jnp.log(row_total)
    prob_low = (exponent / row_total).astype(jnp.bfloat16)
    attn_mixed = (
        jnp.einsum("shqk,skhd->sqhd", prob_low, value_heads, preferred_element_type=jnp.float32)
        .reshape(row_count, width)
        .astype(jnp.bfloat16)
    )
    attn_branch = jnp.dot(
        attn_mixed, out_weight, preferred_element_type=jnp.float32
    ) + out_bias.astype(jnp.float32)
    hidden_pre = jnp.dot(
        normed_mlp, up_weight, preferred_element_type=jnp.float32
    ) + up_bias.astype(jnp.float32)
    hidden = jax.nn.gelu(hidden_pre, approximate=False).astype(jnp.bfloat16)
    mlp_branch = jnp.dot(
        hidden, down_weight, preferred_element_type=jnp.float32
    ) + down_bias.astype(jnp.float32)
    output = (token_rows + attn_branch + mlp_branch).astype(jnp.bfloat16).reshape(tokens.shape)
    attn_gain, mlp_gain, qkv_weight, out_weight, up_weight, down_weight = (
        lax.all_gather(norm1_gain, "dp", axis=0, tiled=True),
        lax.all_gather(norm2_gain, "dp", axis=0, tiled=True),
        lax.all_gather(w_qkv, "dp", axis=0, tiled=True),
        lax.all_gather(w_out, "dp", axis=0, tiled=True),
        lax.all_gather(w_up, "dp", axis=0, tiled=True),
        lax.all_gather(w_down, "dp", axis=0, tiled=True),
    )
    grad_rows = cotangent.reshape(row_count, width)
    grad_wide = grad_rows.astype(jnp.float32)
    hidden_grad = contract_cols(grad_rows, down_weight)
    unused, gelu_pull = jax.vjp(
        lambda pre_value: jax.nn.gelu(pre_value, approximate=False), hidden_pre
    )
    pre_grad = gelu_pull(hidden_grad)[0].astype(jnp.bfloat16)
    normed_mlp_grad = contract_cols(pre_grad, up_weight)
    mlp_in_grad, mlp_gain_grad, mlp_shift_grad = norm_grads(
        token_rows, mlp_gain.astype(jnp.float32), mlp_shift.astype(jnp.float32), normed_mlp_grad
    )
    mlp_terms = (
        contract_rows(normed_mlp, pre_grad),
        jnp.sum(pre_grad.astype(jnp.float32), axis=0),
        contract_rows(hidden, grad_rows),
        jnp.sum(grad_wide, axis=0),
        mlp_gain_grad,
        mlp_shift_grad,
    )
    mlp_shares = (
        lax.psum_scatter(
            mlp_terms[0].astype(jnp.bfloat16), "dp", scatter_dimension=0, tiled=True
        ).astype(jnp.float32),
        lax.psum_scatter(
            mlp_terms[1].astype(jnp.bfloat16), "dp", scatter_dimension=0, tiled=True
        ).astype(jnp.float32),
        lax.psum_scatter(
            mlp_terms[2].astype(jnp.bfloat16), "dp", scatter_dimension=0, tiled=True
        ).astype(jnp.float32),
        lax.psum_scatter(
            mlp_terms[3].astype(jnp.bfloat16), "dp", scatter_dimension=0, tiled=True
        ).astype(jnp.float32),
        lax.psum_scatter(
            mlp_terms[4].astype(jnp.bfloat16), "dp", scatter_dimension=0, tiled=True
        ).astype(jnp.float32),
        lax.psum_scatter(
            mlp_terms[5].astype(jnp.bfloat16), "dp", scatter_dimension=0, tiled=True
        ).astype(jnp.float32),
    )
    mixed_grad = contract_cols(grad_rows, out_weight).astype(jnp.bfloat16).reshape(head_shape)
    again_scores = (
        jnp.einsum("sqhd,skhd->shqk", queries, key_heads, preferred_element_type=jnp.float32)
        * score_scale
    )
    again_scores = jnp.where(allowed, again_scores, MASK_FILL)
    attn_prob = jnp.exp(again_scores - log_norm)
    prob_again = attn_prob.astype(jnp.bfloat16)
    prob_grad = jnp.einsum(
        "sqhd,skhd->shqk", mixed_grad, value_heads, preferred_element_type=jnp.float32
    )
    row_dot = jnp.sum(prob_grad * attn_prob, axis=-1, keepdims=True)
    score_grad = (attn_prob * (prob_grad - row_dot)).astype(jnp.bfloat16)
    query_grad = (
        jnp.einsum("shqk,skhd->sqhd", score_grad, key_heads, preferred_element_type=jnp.float32)
        * score_scale
    )
    key_part = (
        jnp.einsum("shqk,sqhd->skhd", score_grad, queries, preferred_element_type=jnp.float32)
        * score_scale
    ).reshape(seq_dev, seq_len, width)
    value_part = jnp.einsum(
        "shqk,sqhd->skhd", prob_again, mixed_grad, preferred_element_type=jnp.float32
    ).reshape(seq_dev, seq_len, width)
    key_grad, value_grad = (
        lax.psum_scatter(
            key_part.astype(jnp.bfloat16), "ctx", scatter_dimension=1, tiled=True
        ).astype(jnp.float32),
        lax.psum_scatter(
            value_part.astype(jnp.bfloat16), "ctx", scatter_dimension=1, tiled=True
        ).astype(jnp.float32),
    )
    query_back = rotary(query_grad, own_place, -1.0).reshape(row_count, width)
    key_back = rotary(key_grad.reshape(head_shape), own_place, -1.0).reshape(row_count, width)
    proj_grad = jnp.concatenate(
        [query_back, key_back, value_grad.reshape(row_count, width)], axis=1
    ).astype(jnp.bfloat16)
    normed_attn_grad = contract_cols(proj_grad, qkv_weight)
    attn_in_grad, attn_gain_grad, attn_shift_grad = norm_grads(
        token_rows, attn_gain.astype(jnp.float32), attn_shift.astype(jnp.float32), normed_attn_grad
    )
    input_grad = (grad_wide + mlp_in_grad + attn_in_grad).astype(jnp.bfloat16).reshape(tokens.shape)
    attn_terms = (
        contract_rows(normed_attn, proj_grad),
        jnp.sum(proj_grad.astype(jnp.float32), axis=0),
        contract_rows(attn_mixed, grad_rows),
        attn_gain_grad,
        attn_shift_grad,
    )
    attn_shares = (
        lax.psum_scatter(
            attn_terms[0].astype(jnp.bfloat16), "dp", scatter_dimension=0, tiled=True
        ).astype(jnp.float32),
        lax.psum_scatter(
            attn_terms[1].astype(jnp.bfloat16), "dp", scatter_dimension=0, tiled=True
        ).astype(jnp.float32),
        lax.psum_scatter(
            attn_terms[2].astype(jnp.bfloat16), "dp", scatter_dimension=0, tiled=True
        ).astype(jnp.float32),
        lax.psum_scatter(
            attn_terms[3].astype(jnp.bfloat16), "dp", scatter_dimension=0, tiled=True
        ).astype(jnp.float32),
        lax.psum_scatter(
            attn_terms[4].astype(jnp.bfloat16), "dp", scatter_dimension=0, tiled=True
        ).astype(jnp.float32),
    )
    summed = jax.tree.map(
        lambda part: part.astype(jnp.float32), lax.psum(shortened(mlp_shares + attn_shares), "ctx")
    )
    (
        up_total,
        up_bias_total,
        down_total,
        bias_total,
        mlp_gain_total,
        mlp_shift_total,
        qkv_total,
        qkv_bias_total,
        out_total,
        attn_gain_total,
        attn_shift_total,
    ) = summed
    return (
        output,
        input_grad,
        attn_gain_total,
        attn_shift_total,
        mlp_gain_total,
        mlp_shift_total,
        qkv_total,
        qkv_bias_total,
        out_total,
        bias_total,
        up_total,
        up_bias_total,
        down_total,
        bias_total,
    )


PLANES = 4


MESH_ID = pl.DeviceIdType.MESH


def dot_nn(left, right):
    return jnp.dot(left, right, preferred_element_type=jnp.float32)


def half_turn(head, cosine, sine):
    first = head[:, :128]
    lane = lax.broadcasted_iota(jnp.int32, first.shape, 1)
    swapped = jnp.where(
        lane < ROT // 2, pltpu.roll(first, 128 - ROT // 2, 1), pltpu.roll(first, ROT // 2, 1)
    )
    return jnp.concatenate([first * cosine + swapped * sine, head[:, 128:]], axis=1)


def block_kernel(
    x_in,
    g_in,
    up_in,
    qkv_in,
    small_in,
    down,
    out_w,
    up_bias,
    cosine,
    sine,
    pair,
    out_sum,
    back_sum,
    vec_all,
    small_out,
    down_tot,
    up_tot,
    outw_tot,
    qkv_tot,
    x_hbm,
    g_hbm,
    na_hbm,
    hp_hbm,
    got_down,
    got_up,
    got_outw,
    got_qkv,
    core_got,
    plane_got,
    up,
    qkv,
    gains,
    qkv_bias,
    xb,
    gb,
    hx,
    half_in,
    hid,
    prg,
    q,
    k,
    v,
    mg,
    mix,
    proj,
    stat,
    kacc,
    vacc,
    acc_down,
    acc_up,
    g_down,
    g_up,
    g_outw,
    g_qkv,
    cb,
    tmp,
    vec,
    vec_got,
    line_send,
    line_recv,
    side_send,
    side_recv,
    pair_send,
    core_tok_send,
    core_tok_recv,
    w_send,
    w_recv,
    wx_send,
    wx_recv,
    wy_send,
    wy_recv,
    wc_send,
    wc_recv,
    small_send,
    small_recv,
    gather_sem,
    load_sem,
    save_sem,
    tmp_sem,
    core_send,
    core_recv,
    plane_send,
    plane_recv,
    home_send,
    home_recv,
    y_send,
    y_recv,
    x_send,
    x_recv,
    a2a_send,
    a2a_recv,
    vec_send,
    vec_recv,
    local_sem,
):
    f32, bf16 = jnp.float32, jnp.bfloat16
    dp = lax.axis_index("dp")
    rank = lax.axis_index("ctx")
    z, core = dp // 2, dp % 2
    y, x = rank // 2, rank % 2
    core_to = (2 * z + 1 - core, rank)
    x_to = (dp, 2 * y + 1 - x)
    y_to = (dp, 2 * (1 - y) + x)
    pair_to = (2 * z + 1 - core, 2 * (1 - y) + x)
    seqs, length, width = x_hbm.shape
    tok = length // 4
    ff = up.shape[2]
    row_tile = 64
    half_part = width // (4 * PLANES)
    n_dp = 2 * PLANES
    part_rows = up_in.shape[0]
    section_cols = qkv_tot.shape[1] // 3
    scale = DH ** (-0.5)
    n_qkv = 3 * DH

    barrier = pltpu.get_barrier_semaphore()
    for target in (core_to, x_to, y_to, pair_to, (dp, 3 - rank)):
        pl.semaphore_signal(barrier, inc=1, device_id=target, device_id_type=MESH_ID)
    for shift in range(1, PLANES):
        for c in range(2):
            target = (2 * lax.rem(z + shift, PLANES) + c, rank)
            pl.semaphore_signal(barrier, inc=1, device_id=target, device_id_type=MESH_ID)
    pl.semaphore_wait(barrier, 5 + 2 * (PLANES - 1))

    def ds(first, size, step=None):
        return pl.ds(pl.multiple_of(first, step or size), size)

    def remote(src, dst, send, recv, target):
        return pltpu.make_async_remote_copy(
            src_ref=src,
            dst_ref=dst,
            send_sem=send,
            recv_sem=recv,
            device_id=target,
            device_id_type=MESH_ID,
        )

    pending = []

    def start(copy, when=None):
        if when is None or when is True:
            when = None
            copy.start()
        else:
            pl.when(when)(copy.start)
        pending.append((when, copy.wait_send))

    def start_local(copy, when=None):
        if when is None:
            copy.start()
        else:
            pl.when(when)(copy.start)
        pending.append((when, copy.wait))

    one, two = ds(x * tok, tok), ds((2 + x) * tok, tok)

    arrays = ((g_in, g_hbm), (x_in, x_hbm))
    mine = 2 * core + x
    theirs = 2 * core + 1 - x
    same_row = core == y

    def block_of(a, plane, ctx):
        return arrays[a][1].at[plane, ds(ctx * tok, tok)]

    def pair_copy(a, ctx):
        return remote(
            arrays[a][0], block_of(a, z, ctx), pair_send.at[a], line_recv.at[a, z], pair_to
        )

    def own_copy(a):
        return pltpu.make_async_copy(arrays[a][0], block_of(a, z, mine), gather_sem.at[a])

    def own_start(a):
        pl.when(jnp.logical_not(same_row))(pair_copy(a, 2 * y + x).start)
        pl.when(same_row)(own_copy(a).start)

    def own_arrived(a):
        pl.when(jnp.logical_not(same_row))(pair_copy(a, mine).wait_recv)
        pl.when(same_row)(own_copy(a).wait)

    quarter = part_rows // 4
    half = part_rows // 2
    up_rows = ds(rank * quarter, quarter)
    qkv_rows = ds(y * half, half)
    peers = [(s, c) for s in range(PLANES) for c in range(2)][1:]

    def small_copy(n):
        shift, c = peers[n]
        target = (2 * lax.rem(z + shift, PLANES) + lax.rem(core + c, 2), rank)
        return remote(small_in, small_out.at[dp], small_send.at[n], small_recv.at[n], target)

    small_own = pltpu.make_async_copy(small_in, small_out.at[dp], gather_sem.at[2])

    def up_cols(target):
        return up_in.at[:, ds(target * ff, ff)]

    def qkv_cols(target, section):
        return qkv_in.at[:, ds(section * section_cols + target * DH, DH)]

    own_weights = [pltpu.make_async_copy(up_cols(dp), up.at[dp], gather_sem.at[3])]
    core_weights = [
        remote(up_cols(core_to[0]), up.at[dp], wc_send.at[0], wc_recv.at[0], core_to)
    ]
    for section in range(3):
        columns = pl.ds(section * DH, DH)
        own_weights.append(
            pltpu.make_async_copy(
                qkv_cols(dp, section), qkv.at[dp, :, columns], gather_sem.at[4 + section]
            )
        )
        core_weights.append(
            remote(
                qkv_cols(core_to[0], section),
                qkv.at[dp, :, columns],
                wc_send.at[1 + section],
                wc_recv.at[1 + section],
                core_to,
            )
        )

    up_copies = []
    qkv_copies = []
    for shift in range(1, PLANES):
        plane = lax.rem(z + shift, PLANES)
        for c in range(2):
            target = (2 * plane + c, rank)
            up_copies.append(
                remote(
                    up_in.at[up_rows, ds(target[0] * ff, ff)],
                    up.at[dp, up_rows],
                    w_send.at[shift - 1, c, 0],
                    w_recv.at[shift - 1, core, 0],
                    target,
                )
            )
            for section in range(3):
                qkv_copies.append(
                    remote(
                        qkv_in.at[qkv_rows, ds(section * section_cols + target[0] * DH, DH)],
                        qkv.at[dp, qkv_rows, pl.ds(section * DH, DH)],
                        w_send.at[shift - 1, c, 1 + section],
                        w_recv.at[shift - 1, core, 1 + section],
                        target,
                    )
                )

    def carry(a, plane, when, along):
        block = block_of(a, plane, mine)
        recv = line_recv.at[a, plane]
        if along in (0, 1):
            start(
                remote(block, block, line_send.at[a, 0, plane], recv, (dp + 2, rank)),
                jnp.logical_and(when, z < PLANES - 1),
            )
        if along in (0, -1):
            start(
                remote(block, block, line_send.at[a, 1, plane], recv, (dp - 2, rank)),
                jnp.logical_and(when, z > 0),
            )
        start(remote(block, block, side_send.at[a, plane], side_recv.at[a, plane], x_to), when)
        sems = (core_tok_send.at[a, 0, plane], core_tok_recv.at[a, 0, plane])
        start(remote(block, block, *sems, core_to), when)

    def step_blocks(step):
        blocks = []
        for along in (1, -1):
            plane = z - along * step
            there = jnp.logical_and(plane >= 0, plane < PLANES)
            blocks.append((along, lax.rem(plane + PLANES, PLANES), there))
        return blocks

    def line_step(step, a):
        for along, plane, there in step_blocks(step):
            block = block_of(a, plane, mine)
            sems = (line_send.at[a, 0, plane], line_recv.at[a, plane])
            pl.when(there)(remote(block, block, *sems, core_to).wait_recv)
            carry(a, plane, there, along)

    def side_on(a, plane, when):
        block = block_of(a, plane, theirs)
        copy = remote(block, block, side_send.at[a, plane], side_recv.at[a, plane], core_to)
        pl.when(when)(copy.wait_recv)
        sems = (core_tok_send.at[a, 1, plane], core_tok_recv.at[a, 1, plane])
        start(remote(block, block, *sems, core_to), when)

    def side_step(step, a):
        for unused, plane, there in step_blocks(step):
            side_on(a, plane, there)

    def w_arrive(shift, c, part):
        source = 2 * lax.rem(z - shift + PLANES, PLANES) + c
        if part == 0:
            dst = up.at[source, up_rows]
        else:
            dst = qkv.at[source, qkv_rows, pl.ds((part - 1) * DH, DH)]
        sems = (w_send.at[shift - 1, c, part], w_recv.at[shift - 1, c, part])
        remote(dst, dst, *sems, core_to).wait_recv()

    def pair_of(shift):
        return pl.ds(2 * lax.rem(z - shift + PLANES, PLANES), 2)

    def quarter_of(ctx):
        return ds(ctx * quarter, quarter)

    def share_up(shift):
        for c in range(2):
            w_arrive(shift, c, 0)
        block = up.at[pair_of(shift), up_rows]
        start(remote(block, block, wx_send.at[shift - 1], wx_recv.at[shift - 1], x_to))
        start(remote(block, block, wy_send.at[shift - 1, 0], wy_recv.at[shift - 1, 0], y_to))

    def share_up_side(shift):
        block = up.at[pair_of(shift), quarter_of(2 * y + 1 - x)]
        remote(block, block, wx_send.at[shift - 1], wx_recv.at[shift - 1], x_to).wait_recv()
        start(remote(block, block, wy_send.at[shift - 1, 1], wy_recv.at[shift - 1, 1], y_to))

    def share_qkv(shift):
        for c in range(2):
            for part in range(1, 4):
                w_arrive(shift, c, part)
        block = qkv.at[pair_of(shift), qkv_rows]
        start(remote(block, block, wy_send.at[shift - 1, 2], wy_recv.at[shift - 1, 2], y_to))

    def qkv_send():
        for copy in qkv_copies:
            copy.start()

    def own_in(a):
        own_arrived(a)
        carry(a, z, True, 0)

    def up_send():
        for copy in up_copies:
            copy.start()

    def up_ready():
        for shift in range(1, PLANES):
            for n, side in enumerate((x, 1 - x)):
                block = up.at[pair_of(shift), quarter_of(2 * (1 - y) + side)]
                sems = (wy_send.at[shift - 1, n], wy_recv.at[shift - 1, n])
                remote(block, block, *sems, y_to).wait_recv()
        own_weights[0].wait()
        core_weights[0].wait()

    def qkv_ready():
        for shift in range(1, PLANES):
            block = qkv.at[pair_of(shift), ds((1 - y) * half, half)]
            sems = (wy_send.at[shift - 1, 2], wy_recv.at[shift - 1, 2])
            remote(block, block, *sems, y_to).wait_recv()
        for copy in own_weights[1:] + core_weights[1:]:
            copy.wait()

    def small_ready():
        small_own.wait()
        for n, (shift, c) in enumerate(peers):
            source = 2 * lax.rem(z - shift + PLANES, PLANES) + lax.rem(core + c, 2)
            dst = small_out.at[source]
            remote(small_in, dst, small_send.at[n], small_recv.at[n], core_to).wait()
        for i in range(4):
            for d in range(n_dp):
                gains[i : i + 1, d * part_rows : (d + 1) * part_rows] = small_out[d, i : i + 1, :]
        for section in range(3):
            block = n_dp * section + dp
            source, row = block // 3, 6 + lax.rem(block, 3)
            qkv_bias[:, section * DH : (section + 1) * DH] = small_out[source, pl.ds(row, 1), :]

    toward = jnp.where(z < PLANES // 2, 1, -1)
    far = jnp.where(z < PLANES // 2, PLANES - 1, 0)
    near = z + toward
    feed_order = (z, near, 6 - z - near - far, far)

    def sequence_ready(j):
        for a in range(2):
            for n, side in enumerate((x, 1 - x)):
                block = block_of(a, feed_order[j], 2 * (1 - core) + side)
                sems = (
                    core_tok_send.at[a, n, feed_order[j]],
                    core_tok_recv.at[a, n, feed_order[j]],
                )
                remote(block, block, *sems, core_to).wait_recv()
        for copy in load(feed_order[j], j % 2):
            copy.start()

    own_start(0)
    own_start(1)
    small_own.start()
    for n in range(len(peers)):
        small_copy(n).start()
    for copy in own_weights + core_weights:
        copy.start()

    def load(s, slot):
        return (
            pltpu.make_async_copy(x_hbm.at[s], xb.at[slot], load_sem.at[0, slot]),
            pltpu.make_async_copy(g_hbm.at[s], gb.at[slot], load_sem.at[1, slot]),
        )

    def save_norm(s):
        return pltpu.make_async_copy(hx.at[1], na_hbm.at[s], save_sem.at[0])

    def save_rows(s):
        copies = []
        for n, (ref, cols) in enumerate(((hid, pl.ds(0, ff)), (prg, pl.ds(ff, ff)))):
            for h, rows in enumerate((one, two)):
                copies.append(
                    pltpu.make_async_copy(
                        ref.at[rows],
                        hp_hbm.at[s, pl.ds(h * tok, tok), cols],
                        save_sem.at[1 + 2 * n + h],
                    )
                )
        return copies

    def clear(ref):
        @pl.loop(0, ref.shape[0] // 64)
        def rows(i):
            ref[ds(i * 64, 64), :] = jnp.zeros((64, ref.shape[1]), f32)

    def choose_half(src, slot):
        for d in range(width // 256):
            half_in[:, d * 128 : (d + 1) * 128] = src[slot, :, ds(d * 256 + x * 128, 128)]

    def feed(slot, tile):
        c = ds(tile * 256, 256)
        columns = up[:, :, c].reshape(width, 256)
        pre = dot_nn(hx[0], columns) + up_bias[:, c]
        hidden_grad = contract_cols(gb[slot], down[c, :])
        cdf = 0.5 * (1.0 + lax.erf(pre * (0.5**0.5)))
        pdf = jnp.exp(-0.5 * pre * pre) * ((2.0 * 3.141592653589793) ** -0.5)
        hid[:, c] = (pre * cdf).astype(bf16)
        prg[:, c] = (hidden_grad * (cdf + pre * pdf)).astype(bf16)

    def feed_down(slot, m):
        r = ds(m * 256, 256)
        acc_down[r, :] += contract_rows(hid[:, ds(x * (ff // 2) + m * 256, 256)], gb[slot])

    def feed_forward(j, tick):
        s = feed_order[j]
        slot = j % 2
        for copy in load(s, slot):
            copy.wait()
        if j > 0:
            save_norm(feed_order[j - 1]).wait()
            for copy in save_rows(feed_order[j - 1]):
                copy.wait()

        @pl.loop(0, length // row_tile)
        def norm(i):
            r = ds(i * row_tile, row_tile)
            value = xb[slot, r, :].astype(f32)
            centre = value - jnp.mean(value, axis=1, keepdims=True)
            inv = lax.rsqrt(jnp.mean(centre * centre, axis=1, keepdims=True) + EPS_NORM)
            hat = centre * inv
            hx[1, r, :] = (hat * gains[0:1, :] + gains[1:2, :]).astype(bf16)
            hx[0, r, :] = (hat * gains[2:3, :] + gains[3:4, :]).astype(bf16)

        save_norm(s).start()
        choose_half(hx, 0)
        tick(j, 0)

        @pl.loop(0, 2)
        def first_tiles(m):
            feed(slot, 2 * x + m)
            feed_down(slot, m)

        if j == seqs - 1:
            rounded(g_down, acc_down, g_down.shape[0], width)
            y_copy(0, 0).start()
        tick(j, 1)

        @pl.loop(0, 2)
        def last_tiles(m):
            feed(slot, 2 * (1 - x) + m)

        for copy in save_rows(s):
            copy.start()
        tick(j, 2)

        @pl.loop(0, width // 512)
        def gup(m):
            r = ds(m * 256, 256)
            acc_up[r, :] += contract_rows(half_in[:, r], prg[...])

        rows_sum = jnp.sum(prg[one, :].astype(f32), axis=0, keepdims=True)
        rows_sum += jnp.sum(prg[two, :].astype(f32), axis=0, keepdims=True)
        vec[6:7, 0:ff] += rows_sum
        tick(j, 3)

    def add_rows(dst, src, rows):
        @pl.loop(0, rows // 32)
        def tiles(i):
            r = ds(i * 32, 32)
            dst[r, :] = (dst[r, :].astype(f32) + src[r, :].astype(f32)).astype(bf16)

    def add_pieces(pieces):
        copies = []
        first = 0
        for n, (dst, src) in enumerate(pieces):
            rows, cols = dst.shape
            here = tmp.at[first : first + rows, 0:cols]
            copy = pltpu.make_async_copy(src, here, tmp_sem.at[n])
            copy.start()
            copies.append((copy, dst, here, rows))
            first += rows
        for copy, dst, here, rows in copies:
            copy.wait()
            add_rows(dst, here, rows)

    down_pieces = g_down.shape[0] // tok

    def y_copy(kind, piece):
        sems = (y_send.at[kind, piece], y_recv.at[kind, piece])
        if kind == 0:
            rows = pl.ds(piece * tok, tok)
            return remote(g_down.at[rows], got_down.at[rows], *sems, y_to)
        if kind == 1:
            return remote(g_outw, got_outw, *sems, y_to)
        src, got = (g_up, got_up) if kind == 2 else (g_qkv, got_qkv)
        pair = pl.ds(2 * lax.rem(z + piece, PLANES), 2)
        return remote(src.at[pair], got.at[pair], *sems, y_to)

    half_rows = ds(x * half_part, half_part)
    other_half = ds((1 - x) * half_part, half_part)

    def column_parts(kind, index, source):
        if kind == 2:
            return [(g_up.at[index], up_tot.at[half_rows, ds(source * ff, ff)])]
        return [
            (
                g_qkv.at[index, :, pl.ds(n * DH, DH)],
                qkv_tot.at[half_rows, ds(n * section_cols + source * DH, DH)],
            )
            for n in range(3)
        ]

    def side_parts(kind, plane, rows):
        if kind == 2:
            return [up_tot.at[rows, ds(plane * 2 * ff, 2 * ff)]]
        return [qkv_tot.at[rows, ds(n * section_cols + plane * 2 * DH, 2 * DH)] for n in range(3)]

    def reduced(kind, piece):
        y_copy(kind, piece).wait()
        if kind == 0:
            rows = pl.ds(piece * tok, tok)
            add_pieces([(g_down.at[rows], got_down.at[rows])])
            place = down_tot.at[ds(x * g_down.shape[0] + piece * tok, tok)]
            start_local(pltpu.make_async_copy(g_down.at[rows], place, local_sem.at[2 + piece]))
            start(remote(g_down.at[rows], place, x_send.at[0, piece], x_recv.at[0, piece], x_to))
            return
        if kind == 1:
            add_pieces([(g_outw, got_outw)])
            place = outw_tot.at[half_rows]
            start_local(pltpu.make_async_copy(g_outw, place, local_sem.at[6]))
            start(remote(g_outw, place, x_send.at[1, 0], x_recv.at[1, 0], x_to))
            return
        got, own = ((got_up, g_up), (got_qkv, g_qkv))[kind - 2]
        plane = lax.rem(z + piece, PLANES)
        add_pieces([(own.at[2 * plane + c], got.at[2 * plane + c]) for c in range(2)])
        for c in range(2):
            for part, (src, dst) in enumerate(column_parts(kind, 2 * plane + c, dp)):
                send = a2a_send.at[kind - 2, piece, c, part]
                recv = a2a_recv.at[kind - 2, piece, core, part]
                copy = remote(src, dst, send, recv, (2 * plane + c, rank))
                if piece == 0:
                    local = pltpu.make_async_copy(
                        src, dst, local_sem.at[7 + 3 * (kind - 2) + part]
                    )
                    pl.when(core == c)(local.start)
                    start(copy, core != c)
                else:
                    start(copy)

    def share(kind, shift):
        plane = lax.rem(z - shift + PLANES, PLANES)
        for c in range(2):
            for part, (src, dst) in enumerate(column_parts(kind, 2 * plane + c, 2 * plane + c)):
                recv = a2a_recv.at[kind - 2, shift, c, part]
                copy = remote(dst, dst, a2a_send.at[kind - 2, shift, c, part], recv, core_to)
                if shift == 0:
                    pl.when(core != c)(copy.wait_recv)
                    local = pltpu.make_async_copy(
                        src, dst, local_sem.at[7 + 3 * (kind - 2) + part]
                    )
                    pl.when(core == c)(local.wait)
                else:
                    copy.wait_recv()
        for part, block in enumerate(side_parts(kind, plane, half_rows)):
            sems = (x_send.at[kind + part, shift], x_recv.at[kind + part, shift])
            start(remote(block, block, *sems, x_to))

    order = (0, 3, 1, 2)

    def core_copy(i):
        s = order[i]
        return remote(
            cb.at[seqs + i % 2], core_got.at[s], core_send.at[i], core_recv.at[i], core_to
        )

    def chip_sum(i):
        s = order[i]
        core_copy(i).wait_recv()
        add_pieces([(cb.at[i, a], core_got.at[s, a]) for a in range(2)])
        start(flow_copy(i, 0), jnp.logical_and(z == 0, s > 0))
        start(flow_copy(i, 1), jnp.logical_and(z == PLANES - 1, s < PLANES - 1))

    def flow_copy(i, side):
        s = order[i]
        sems = (plane_send.at[i], plane_recv.at[side, s])
        return remote(cb.at[i], plane_got.at[side, s], *sems, (dp + (2, -2)[side], rank))

    def flow_add(i, side):
        flow_copy(i, side).wait_recv()
        add_pieces([(cb.at[i, a], plane_got.at[side, order[i], a]) for a in range(2)])

    def flow_relay(i, hop):
        s = order[i]
        for side, plane in enumerate((hop, PLANES - 1 - hop)):
            if (plane < s) if side == 0 else (plane > s):
                here = z == plane
                pl.when(here)(functools.partial(flow_add, i, side))
                start(flow_copy(i, side), here)

    def flow_end(i):
        s = order[i]

        @pl.when(z == s)
        def both():
            if s > 0:
                flow_add(i, 0)
            if s < PLANES - 1:
                flow_add(i, 1)

        same = core == y
        for a, result in enumerate((out_sum, back_sum)):
            block = cb.at[i, a]
            start_local(
                pltpu.make_async_copy(block, result, local_sem.at[a]),
                jnp.logical_and(z == s, same),
            )
            start(
                remote(block, result, home_send.at[a], home_recv.at[a], pair_to),
                jnp.logical_and(z == s, jnp.logical_not(same)),
            )

    def rounded(dst, src, rows, cols):
        @pl.loop(0, rows // 64)
        def tiles(i):
            r = ds(i * 64, 64)
            dst[r, :] = src[r, 0:cols].astype(bf16)

    def rounded_columns(dst, src, cols):
        @pl.loop(0, dst.shape[0])
        def blocks(d):
            dst[d] = src[ds(d * half_part, half_part), 0:cols].astype(bf16)

    def place_of(first, within):
        block = jnp.where(within < tok // 2, first, 2 * 4 - 1 - first)
        return block * (tok // 2) + lax.bitwise_and(within, tok // 2 - 1)

    def place_q(part):
        return place_of(pair[part], lax.broadcasted_iota(jnp.int32, (tok, 1), 0))

    column = lax.broadcasted_iota(jnp.int32, (1, length), 1)
    firsts = jnp.where(column < tok, pair[0], pair[1])
    firsts = jnp.where(column < 2 * tok, firsts, jnp.where(column < 3 * tok, pair[2], pair[3]))
    place_k = place_of(firsts, lax.bitwise_and(column, tok - 1))

    def load_again(i, slot):
        s = order[i]
        copies = [
            pltpu.make_async_copy(na_hbm.at[s], xb.at[slot], load_sem.at[0, slot]),
            pltpu.make_async_copy(g_hbm.at[s], gb.at[slot], load_sem.at[1, slot]),
            pltpu.make_async_copy(
                hp_hbm.at[s], hx.at[slot, pl.ds(2 * tok, 2 * tok)], load_sem.at[2, slot]
            ),
        ]
        for h, rows in enumerate((one, two)):
            copies.append(
                pltpu.make_async_copy(
                    x_hbm.at[s, rows],
                    hx.at[slot, pl.ds(h * tok, tok)],
                    load_sem.at[3 + h, slot],
                )
            )
        return copies

    feed_plan = {
        (0, 0): [(up_ready,), (line_step, 2, 0)],
        (0, 2): [(line_step, 2, 1), (side_step, 1, 0)],
        (0, 3): [(qkv_send,), (side_step, 1, 1), (line_step, 3, 0), (sequence_ready, 1)],
        (1, 3): [(side_step, 2, 0), (line_step, 3, 1), (side_step, 3, 0), (share_qkv, 3), (side_step, 2, 1), (sequence_ready, 2)],
        (2, 2): [(side_step, 3, 1)],
        (2, 3): [(share_qkv, 1), (sequence_ready, 3)],
        (3, 1): [(share_qkv, 2)],
    }

    def feed_tick(j, point):
        for step, *which in feed_plan.get((j, point), ()):
            step(*which)

    clear(acc_down)
    clear(acc_up)
    vec[...] = jnp.zeros_like(vec)
    for step, *which in (
        (up_send,),
        (own_in, 0),
        (own_in, 1),
        (share_up, 3),
        (side_on, 1, z, True),
        (share_up, 1),
        (side_on, 0, z, True),
        (share_up, 2),
        (sequence_ready, 0),
        (line_step, 1, 0),
        (share_up_side, 2),
        (line_step, 1, 1),
        (share_up_side, 3),
        (share_up_side, 1),
    ):
        step(*which)
    small_ready()
    for j in range(seqs):
        feed_forward(j, feed_tick)
    save_norm(feed_order[-1]).wait()
    for copy in save_rows(feed_order[-1]):
        copy.wait()

    for copy in load_again(0, 0):
        copy.start()
    rounded_columns(g_up, acc_up, ff)
    for kind, piece in ((2, 3), (2, 2), (2, 1), (0, 1), (0, 2), (2, 0), (0, 3)):
        y_copy(kind, piece).start()
    clear(acc_up)
    clear(acc_down.at[0:tok])
    qkv_ready()

    def attention(i, tick):
        slot = i % 2
        for copy in load_again(i, slot):
            copy.wait()
        if i + 1 < seqs:
            for copy in load_again(i + 1, 1 - slot):
                copy.start()
        tick(i, 0)
        choose_half(xb, slot)
        for n, ref in enumerate((q, k, v)):
            c = slice(n * DH, (n + 1) * DH)
            columns = qkv[:, :, c].reshape(width, DH)
            part = dot_nn(xb[slot], columns) + qkv_bias[:, c]
            if n < 2:
                part = half_turn(part, cosine[...], sine[...])
            ref[...] = part.astype(bf16)
        mg[...] = contract_cols(gb[slot], out_w[...]).astype(bf16)
        tick(i, 1)
        kacc[...] = jnp.zeros_like(kacc)
        vacc[...] = jnp.zeros_like(vacc)

        @pl.loop(0, 4)
        def attend(part):
            r = ds(part * tok, tok)
            scores = contract_cols(q[r, :], k[...]) * scale
            scores = jnp.where(place_k <= place_q(part), scores, MASK_FILL)
            exponent = jnp.exp(scores - jnp.max(scores, axis=1, keepdims=True))
            prob = exponent / jnp.sum(exponent, axis=1, keepdims=True)
            low = prob.astype(bf16)
            mix[r, :] = dot_nn(low, v[...]).astype(bf16)
            prob_grad = contract_cols(mg[r, :], v[...])
            row_dot = jnp.sum(prob_grad * prob, axis=1, keepdims=True)
            score_grad = (prob * (prob_grad - row_dot)).astype(bf16)
            query_grad = dot_nn(score_grad, k[...]) * scale
            proj[r, 0:DH] = half_turn(query_grad, cosine[r, :], -sine[r, :]).astype(bf16)
            kacc[...] += contract_rows(score_grad, q[r, :])
            vacc[...] += contract_rows(low, mg[r, :])

        proj[:, DH : 2 * DH] = half_turn(kacc[...] * scale, cosine[...], -sine[...]).astype(bf16)
        proj[:, 2 * DH : 3 * DH] = vacc[...].astype(bf16)
        tick(i, 2)
        acc_down[0:tok, :] += contract_rows(mix[:, ds(x * 128, 128)], gb[slot])

        @pl.loop(0, width // 512)
        def gqkv(m):
            r = ds(m * 256, 256)
            acc_up[r, 0:n_qkv] += contract_rows(half_in[:, r], proj[...])

        tick(i, 3)
        value = hx[slot, 0 : 2 * tok, :].astype(f32)
        mean = jnp.mean(value, axis=1, keepdims=True)
        centre = value - mean
        stat[0] = mean
        stat[1] = lax.rsqrt(jnp.mean(centre * centre, axis=1, keepdims=True) + EPS_NORM)
        if i >= 2:
            core_copy(i - 2).wait_send()

        def picked(ref):
            return jnp.concatenate([ref[one, :], ref[two, :]], axis=0)

        place = [jnp.where(core == h, i, seqs + i % 2) for h in range(2)]
        later = slice(2 * tok, 4 * tok)

        @pl.loop(0, width // 256)
        def followers(n):
            c = ds(n * 256, 256)
            out = dot_nn(hx[slot, later, 0:ff], down[:, c]) + dot_nn(picked(mix), out_w[:, c])
            mlp_back = contract_cols(hx[slot, later, ff : 2 * ff], up[n])
            attn_back = contract_cols(picked(proj), qkv[n])
            back = attn_back * gains[0:1, c] + mlp_back * gains[2:3, c]
            for h in range(2):
                rows = slice(h * tok, (h + 1) * tok)
                cb[place[h], 0, :, c] = out[rows].astype(bf16)
                cb[place[h], 1, :, c] = back[rows].astype(bf16)
            hat = (hx[slot, 0 : 2 * tok, c].astype(f32) - stat[0]) * stat[1]
            grad = jnp.concatenate([gb[slot, one, c], gb[slot, two, c]], axis=0).astype(f32)
            sums = (attn_back * hat, attn_back, mlp_back * hat, mlp_back, grad)
            for n_sum, term in enumerate(sums):
                vec[n_sum : n_sum + 1, c] += jnp.sum(term, axis=0, keepdims=True)

        vec[5:6, 0:n_qkv] += jnp.sum(picked(proj).astype(f32), axis=0, keepdims=True)
        core_copy(i).start()
        tick(i, 4)

    plan = {
        (0, 3): [(reduced, 0, 0), (reduced, 2, 3)],
        (1, 1): [(reduced, 2, 2)],
        (1, 4): [(reduced, 2, 1), (share, 2, 3)],
        (2, 1): [(chip_sum, 1), (chip_sum, 0)],
        (2, 2): [(share, 2, 2)],
        (3, 0): [(share, 2, 1)],
        (3, 2): [(chip_sum, 2), (flow_relay, 1, 1)],
        (3, 3): [(flow_relay, 0, 1), (reduced, 0, 1)],
    }

    def tick(i, point):
        for step, *which in plan.get((i, point), ()):
            step(*which)

    for i in range(seqs):
        attention(i, tick)

    def vec_copy(n):
        target = (dp, rank + 1 - 2 * x) if n == 0 else (dp, lax.rem(rank + 2, 4))
        if n == 2:
            target = (dp, 3 - rank)
        return remote(vec, vec_got.at[n], vec_send.at[n], vec_recv.at[n], target)

    def vec_gather():
        for n in range(3):
            vec_copy(n).wait()
        pair_sum = (vec[...] + vec_got[0], vec_got[1] + vec_got[2])
        vec_all[dp] = pair_sum[0] + pair_sum[1]
        for n, (shift, c) in enumerate(peers):
            target = (2 * lax.rem(z + shift, PLANES) + lax.rem(core + c, 2), rank)
            sems = (vec_send.at[3 + n], vec_recv.at[3 + n])
            start(remote(vec_all.at[dp], vec_all.at[dp], *sems, target))

    def send(kind, piece):
        y_copy(kind, piece).start()

    for n in range(3):
        vec_copy(n).start()
    rounded_columns(g_qkv, acc_up, n_qkv)
    rounded(g_outw, acc_down, tok, width)
    for step, *which in (
        (send, 3, 2),
        (reduced, 0, 2),
        (reduced, 0, 3),
        (reduced, 2, 0),
        (send, 3, 3),
        (send, 3, 1),
        (reduced, 3, 2),
        (share, 2, 0),
        (chip_sum, 3),
        (send, 3, 0),
        (flow_relay, 1, 2),
        (flow_relay, 0, 2),
        (share, 3, 2),
        (flow_relay, 2, 1),
        (reduced, 3, 1),
        (send, 1, 0),
        (reduced, 3, 0),
        (flow_relay, 3, 1),
        (share, 3, 0),
        (reduced, 1, 0),
        (reduced, 3, 3),
        (share, 3, 1),
        (flow_end, 3),
        (vec_gather,),
        (flow_end, 1),
        (flow_end, 2),
        (flow_end, 0),
        (share, 3, 3),
    ):
        step(*which)

    for copy in up_copies + qkv_copies:
        copy.wait_send()
    for a in range(2):
        pl.when(jnp.logical_not(same_row))(pair_copy(a, 2 * y + x).wait_send)
    for n, (shift, c) in enumerate(peers):
        source = 2 * lax.rem(z - shift + PLANES, PLANES) + lax.rem(core + c, 2)
        block = vec_all.at[source]
        remote(block, block, vec_send.at[3 + n], vec_recv.at[3 + n], core_to).wait_recv()
    for piece in range(down_pieces):
        block = down_tot.at[ds((1 - x) * g_down.shape[0] + piece * tok, tok)]
        remote(block, block, x_send.at[0, piece], x_recv.at[0, piece], x_to).wait_recv()
    block = outw_tot.at[other_half]
    remote(block, block, x_send.at[1, 0], x_recv.at[1, 0], x_to).wait_recv()
    for kind in (2, 3):
        for shift in range(PLANES):
            plane = lax.rem(z - shift + PLANES, PLANES)
            for part, block in enumerate(side_parts(kind, plane, other_half)):
                sems = (x_send.at[kind + part, shift], x_recv.at[kind + part, shift])
                remote(block, block, *sems, x_to).wait_recv()
    for a, result in enumerate((out_sum, back_sum)):
        copy = remote(result, result, home_send.at[a], home_recv.at[a], pair_to)
        pl.when(core != y)(copy.wait_recv)
    for i in range(seqs - 2, seqs):
        core_copy(i).wait_send()
    for when, wait in pending:
        if when is None:
            wait()
        else:
            pl.when(when)(wait)


def block_compute(tokens, cotangent, w_up, w_qkv, small, w_down, w_out, up_bias, pair_index):
    f32, bf16 = jnp.float32, jnp.bfloat16
    n_dp = 2 * PLANES
    tok, width = tokens.shape
    seqs, length = PLANES, 4 * tok
    part_rows = w_up.shape[0]
    ff = w_up.shape[1] // n_dp
    half_part = width // (2 * n_dp)
    lane = lax.broadcasted_iota(jnp.int32, (length, 128), 1)
    frequency = ROPE_BASE ** (-2.0 * np.arange(ROT // 2, dtype=np.float32) / ROT)
    frequency = np.tile(frequency.astype(np.float32), 128 // (ROT // 2))[None, :]
    angles = positions(pair_index, tok).astype(f32)[:, None] * frequency
    cosine = jnp.where(lane < ROT, jnp.cos(angles), 1.0)
    sine = jnp.where(lane < ROT, jnp.sin(angles), 0.0) * jnp.where(lane < ROT // 2, -1.0, 1.0)
    hbm = pl.BlockSpec(memory_space=pl.ANY)
    vmem = pl.BlockSpec(memory_space=pltpu.VMEM)
    dma = pltpu.SemaphoreType.DMA

    def shape(*dims, dtype=bf16):
        return jax.ShapeDtypeStruct(dims, dtype)

    def buf(*dims, dtype=bf16):
        return pltpu.VMEM(dims, dtype)

    results = pl.pallas_call(
        block_kernel,
        out_shape=(
            shape(tok, width),
            shape(tok, width),
            shape(n_dp, 8, width, dtype=f32),
            shape(n_dp, *small.shape, dtype=f32),
            shape(ff, width),
            shape(2 * half_part, n_dp * ff),
            shape(DH, width),
            shape(2 * half_part, n_dp * 3 * DH),
            shape(seqs, length, width),
            shape(seqs, length, width),
            shape(seqs, length, width),
            shape(seqs, 2 * tok, 2 * ff),
            shape(ff // 2, width),
            shape(n_dp, half_part, ff),
            shape(DH // 2, width),
            shape(n_dp, half_part, 3 * DH),
            shape(seqs, 2, tok, width),
            shape(2, seqs, 2, tok, width),
        ),
        in_specs=[hbm] * 5 + [vmem] * 5 + [pl.BlockSpec(memory_space=pltpu.SMEM)],
        out_specs=(hbm, hbm, vmem, vmem) + (hbm,) * 14,
        scratch_shapes=[
            buf(n_dp, part_rows, ff),
            buf(n_dp, part_rows, 3 * DH),
            buf(8, width, dtype=f32),
            buf(1, 3 * DH, dtype=f32),
            buf(2, length, width),
            buf(2, length, width),
            buf(2, length, width),
            buf(length, width // 2),
            buf(length, ff),
            buf(length, ff),
            buf(length, DH),
            buf(length, DH),
            buf(length, DH),
            buf(length, DH),
            buf(length, DH),
            buf(length, 3 * DH),
            buf(2, 2 * tok, 1, dtype=f32),
            buf(length, DH, dtype=f32),
            buf(length, DH, dtype=f32),
            buf(ff // 2, width, dtype=f32),
            buf(width // 2, ff, dtype=f32),
            buf(ff // 2, width),
            buf(n_dp, half_part, ff),
            buf(DH // 2, width),
            buf(n_dp, half_part, 3 * DH),
            buf(seqs + 2, 2, tok, width),
            buf(2 * tok, width),
            buf(8, width, dtype=f32),
            buf(3, 8, width, dtype=f32),
            dma((2, 2, PLANES)),
            dma((2, PLANES)),
            dma((2, PLANES)),
            dma((2, PLANES)),
            dma((2,)),
            dma((2, 2, PLANES)),
            dma((2, 2, PLANES)),
            dma((3, 2, 4)),
            dma((3, 2, 4)),
            dma((3,)),
            dma((3,)),
            dma((3, 3)),
            dma((3, 3)),
            dma((4,)),
            dma((4,)),
            dma((7,)),
            dma((7,)),
            dma((7,)),
            dma((5, 2)),
            dma((5,)),
            dma((2,)),
            dma((seqs,)),
            dma((seqs,)),
            dma((seqs,)),
            dma((2, seqs)),
            dma((2,)),
            dma((2,)),
            dma((4, 4)),
            dma((4, 4)),
            dma((6, 4)),
            dma((6, 4)),
            dma((2, PLANES, 2, 3)),
            dma((2, PLANES, 2, 3)),
            dma((10,)),
            dma((10,)),
            dma((13,)),
        ],
        compiler_params=pltpu.CompilerParams(
            collective_id=2, has_side_effects=True, vmem_limit_bytes=63 * 2**20
        ),
    )(
        tokens,
        cotangent,
        w_up,
        w_qkv,
        small,
        w_down,
        w_out,
        up_bias,
        cosine,
        sine,
        pair_index,
    )
    return results[:8]


def finish_kernel(
    tokens,
    cotangent,
    out_sum,
    back_sum,
    small,
    down_in,
    up_in,
    outw_in,
    qkv_in,
    output,
    input_grad,
    down_out,
    up_out,
    outw_out,
    qkv_out,
):
    f32 = jnp.float32
    for src, dst in (
        (down_in, down_out),
        (up_in, up_out),
        (outw_in, outw_out),
        (qkv_in, qkv_out),
    ):
        dst[...] = src[...].astype(f32)
    bias = jnp.concatenate(
        [small[d, 4:5, :] + small[d, 5:6, :] for d in range(small.shape[0])], axis=1
    )
    value = tokens[...].astype(f32)
    output[...] = (value + out_sum[...].astype(f32) + bias).astype(output.dtype)
    centre = value - jnp.mean(value, axis=-1, keepdims=True)
    inv = lax.rsqrt(jnp.mean(centre * centre, axis=-1, keepdims=True) + EPS_NORM)
    hat = centre * inv
    back = back_sum[...].astype(f32)
    norm_back = (
        back
        - jnp.mean(back, axis=-1, keepdims=True)
        - hat * jnp.mean(back * hat, axis=-1, keepdims=True)
    ) * inv
    input_grad[...] = (cotangent[...].astype(f32) + norm_back).astype(input_grad.dtype)


def finish(tokens, cotangent, out_sum, back_sum, small, totals):
    steps = tokens.shape[0] // 16

    def rows(array):
        return pl.BlockSpec((array.shape[0] // steps, array.shape[1]), lambda i: (i, 0))

    narrow = [tokens, cotangent, out_sum, back_sum]
    whole = pl.BlockSpec(small.shape, lambda i: (0, 0, 0))
    return pl.pallas_call(
        finish_kernel,
        grid=(steps,),
        out_shape=[jax.ShapeDtypeStruct(tokens.shape, tokens.dtype)] * 2
        + [jax.ShapeDtypeStruct(total.shape, jnp.float32) for total in totals],
        in_specs=[rows(a) for a in narrow] + [whole] + [rows(a) for a in totals],
        out_specs=[rows(tokens)] * 2 + [rows(a) for a in totals],
        compiler_params=pltpu.CompilerParams(vmem_limit_bytes=62 * 2**20),
    )(*narrow, small, *totals)


def column_local(
    tokens,
    cotangent,
    pair_index,
    norm1_gain,
    norm1_bias,
    norm2_gain,
    norm2_bias,
    w_qkv,
    b_qkv,
    w_out,
    b_out,
    w_up,
    b_up,
    w_down,
    b_down,
):
    bf16, f32 = jnp.bfloat16, jnp.float32
    tok_count, width = tokens.shape[1:]
    n_dp = H
    dp_rank = lax.axis_index("dp")
    rank = lax.axis_index("ctx")
    z, core = dp_rank // 2, dp_rank % 2
    y, x = rank // 2, rank % 2
    part = width // n_dp
    ff_part = w_up.shape[1] // n_dp
    qkv_part = 3 * DH
    seq_len = 4 * tok_count

    small_row = lax.broadcasted_iota(jnp.int32, (16, part), 0)
    small = jnp.zeros((16, part), bf16)
    pieces = [norm1_gain, norm1_bias, norm2_gain, norm2_bias, b_out, b_down]
    pieces += [b_qkv[n * part : (n + 1) * part] for n in range(b_qkv.shape[0] // part)]
    for n, piece in enumerate(pieces):
        small = jnp.where(small_row == n, piece[None, :], small)
    out_sum, back_sum, vec_all, small_all, down_total, up_total, out_total, qkv_total = (
        block_compute(
            tokens[0],
            cotangent[0],
            w_up,
            w_qkv,
            small.astype(f32),
            w_down,
            w_out,
            b_up.astype(f32)[None],
            pair_index,
        )
    )
    output, input_grad, down_total, up_total, out_total, qkv_total = finish(
        tokens[0],
        cotangent[0],
        out_sum,
        back_sum,
        small_all,
        (down_total, up_total, out_total, qkv_total),
    )
    totals = jnp.sum(vec_all[:, :4], axis=0)
    mine = lax.dynamic_slice_in_dim(totals, dp_rank * part, part, 1)
    gain1_total, shift1_total, gain2_total, shift2_total = mine
    own_vec = lax.dynamic_index_in_dim(vec_all, dp_rank, 0, keepdims=False)
    bias_total = lax.dynamic_slice_in_dim(own_vec[4], dp_rank * part, part)
    up_bias_total = own_vec[6, :ff_part]
    qkv_bias_total = vec_all[:, 5, :qkv_part].reshape(n_dp, 3, DH).swapaxes(0, 1).reshape(-1)
    qkv_bias_total = lax.dynamic_slice_in_dim(
        qkv_bias_total, dp_rank * b_qkv.shape[0], b_qkv.shape[0]
    )
    return (
        output[None],
        input_grad[None],
        gain1_total,
        shift1_total,
        gain2_total,
        shift2_total,
        qkv_total,
        qkv_bias_total,
        out_total,
        bias_total,
        up_total,
        up_bias_total,
        down_total,
        bias_total,
    )


def solution(mesh):
    local = column_local if mesh.shape["dp"] == H and mesh.shape["ctx"] == 4 else plain_local
    placed = (
        P("dp", "ctx", None),
        P("dp", "ctx", None),
        P(),
        P("dp"),
        P("dp"),
        P("dp"),
        P("dp"),
        P("dp", None),
        P("dp"),
        P("dp", None),
        P("dp"),
        P("dp", None),
        P("dp"),
        P("dp", None),
        P("dp"),
    )
    return jax.shard_map(
        local,
        mesh=mesh,
        in_specs=placed,
        out_specs=(
            P("dp", "ctx", None),
            P("dp", "ctx", None),
            P("dp"),
            P("dp"),
            P("dp"),
            P("dp"),
            P("dp", None),
            P("dp"),
            P("dp", None),
            P("dp"),
            P("dp", None),
            P("dp"),
            P("dp", None),
            P("dp"),
        ),
        check_vma=False,
    )
```

```python
import functools

import jax
import jax.numpy as jnp
import numpy as np
from jax import lax
from jax.experimental import pallas as pl
from jax.experimental.pallas import tpu as pltpu
from jax.sharding import PartitionSpec as P

H = 8
DH = 256
ROT = 64


EPS_NORM = 1e-05
ROPE_BASE = 10000.0
MASK_FILL = -1000000000.0


def shortened(x):

    def short(part):
        return part.astype(jnp.bfloat16) if part.dtype == jnp.float32 else part

    return jax.tree.map(short, x)


def layer_norm(values_in, gain_vec, offset):
    centre = values_in - jnp.mean(values_in, axis=-1, keepdims=True)
    spread = jnp.mean(centre * centre, axis=-1, keepdims=True)
    return centre * lax.rsqrt(spread + EPS_NORM) * gain_vec + offset


def norm_grads(values_in, gain_vec, offset, upstream):
    unused, pullback = jax.vjp(layer_norm, values_in, gain_vec, offset)
    return pullback(upstream)


def positions(pair_index, tok_count):
    ranks_total = pair_index.shape[0]
    half_len = tok_count // 2
    index_all = jnp.arange(ranks_total * tok_count, dtype=jnp.int32)
    owner_rank = index_all // tok_count
    within = index_all % tok_count
    match_table = owner_rank[:, None] == jnp.arange(ranks_total, dtype=jnp.int32)[None, :]
    first_block = jnp.sum(jnp.where(match_table, pair_index[None, :], 0), axis=1)
    block_id = jnp.where(within < half_len, first_block, 2 * ranks_total - 1 - first_block)
    return block_id * half_len + within % half_len


def rotary(head_vals, token_place, turn_sign):
    half_rot = ROT // 2
    frequency = ROPE_BASE ** (-2.0 * jnp.arange(half_rot, dtype=jnp.float32) / ROT)
    angles = token_place.astype(jnp.float32)[:, None] * frequency[None, :]
    cosine = jnp.cos(angles)[:, None, :]
    sine_part = turn_sign * jnp.sin(angles)[:, None, :]
    first_half = head_vals[..., :half_rot]
    second = head_vals[..., half_rot:ROT]
    return jnp.concatenate(
        [
            first_half * cosine - second * sine_part,
            second * cosine + first_half * sine_part,
            head_vals[..., ROT:],
        ],
        axis=-1,
    )


def contract_rows(left, right):
    return lax.dot_general(
        left, right, (((0,), (0,)), ((), ())), preferred_element_type=jnp.float32
    )


def contract_cols(left, right):
    return lax.dot_general(
        left, right, (((1,), (1,)), ((), ())), preferred_element_type=jnp.float32
    )


def plain_local(
    tokens,
    cotangent,
    pair_index,
    norm1_gain,
    norm1_bias,
    norm2_gain,
    norm2_bias,
    w_qkv,
    b_qkv,
    w_out,
    b_out,
    w_up,
    b_up,
    w_down,
    b_down,
):
    seq_dev, tok_count, width = tokens.shape
    row_count = seq_dev * tok_count
    head_shape = (seq_dev, tok_count, H, DH)
    score_scale = DH ** (-0.5)
    device_rank = lax.axis_index("ctx")
    all_place = positions(pair_index, tok_count)
    own_place = lax.dynamic_slice_in_dim(all_place, device_rank * tok_count, tok_count)
    allowed = all_place[None, None, None, :] <= own_place[None, None, :, None]
    gathered = (
        lax.all_gather(norm1_gain, "dp", axis=0, tiled=True),
        lax.all_gather(norm1_bias, "dp", axis=0, tiled=True),
        lax.all_gather(norm2_gain, "dp", axis=0, tiled=True),
        lax.all_gather(norm2_bias, "dp", axis=0, tiled=True),
        lax.all_gather(w_qkv, "dp", axis=0, tiled=True),
        lax.all_gather(b_qkv, "dp", axis=0, tiled=True),
        lax.all_gather(w_out, "dp", axis=0, tiled=True),
        lax.all_gather(b_out, "dp", axis=0, tiled=True),
        lax.all_gather(w_up, "dp", axis=0, tiled=True),
        lax.all_gather(b_up, "dp", axis=0, tiled=True),
        lax.all_gather(w_down, "dp", axis=0, tiled=True),
        lax.all_gather(b_down, "dp", axis=0, tiled=True),
    )
    (
        attn_gain,
        attn_shift,
        mlp_gain,
        mlp_shift,
        qkv_weight,
        qkv_bias,
        out_weight,
        out_bias,
        up_weight,
        up_bias,
        down_weight,
        down_bias,
    ) = gathered
    token_rows = tokens.reshape(row_count, width).astype(jnp.float32)
    normed_attn = layer_norm(
        token_rows, attn_gain.astype(jnp.float32), attn_shift.astype(jnp.float32)
    ).astype(jnp.bfloat16)
    normed_mlp = layer_norm(
        token_rows, mlp_gain.astype(jnp.float32), mlp_shift.astype(jnp.float32)
    ).astype(jnp.bfloat16)
    projected = jnp.dot(
        normed_attn, qkv_weight, preferred_element_type=jnp.float32
    ) + qkv_bias.astype(jnp.float32)
    queries = rotary(projected[:, :width].reshape(head_shape), own_place, 1.0).astype(jnp.bfloat16)
    key_local = (
        rotary(projected[:, width : 2 * width].reshape(head_shape), own_place, 1.0)
        .astype(jnp.bfloat16)
        .reshape(seq_dev, tok_count, width)
    )
    value_local = projected[:, 2 * width :].astype(jnp.bfloat16).reshape(seq_dev, tok_count, width)
    key_all, value_all = (
        lax.all_gather(key_local, "ctx", axis=1, tiled=True),
        lax.all_gather(value_local, "ctx", axis=1, tiled=True),
    )
    seq_len = key_all.shape[1]
    key_heads = key_all.reshape(seq_dev, seq_len, H, DH)
    value_heads = value_all.reshape(seq_dev, seq_len, H, DH)
    raw_scores = (
        jnp.einsum("sqhd,skhd->shqk", queries, key_heads, preferred_element_type=jnp.float32)
        * score_scale
    )
    raw_scores = jnp.where(allowed, raw_scores, MASK_FILL)
    row_max = jnp.max(raw_scores, axis=-1, keepdims=True)
    exponent = jnp.exp(raw_scores - row_max)
    row_total = jnp.sum(exponent, axis=-1, keepdims=True)
    log_norm = row_max + jnp.log(row_total)
    prob_low = (exponent / row_total).astype(jnp.bfloat16)
    attn_mixed = (
        jnp.einsum("shqk,skhd->sqhd", prob_low, value_heads, preferred_element_type=jnp.float32)
        .reshape(row_count, width)
        .astype(jnp.bfloat16)
    )
    attn_branch = jnp.dot(
        attn_mixed, out_weight, preferred_element_type=jnp.float32
    ) + out_bias.astype(jnp.float32)
    hidden_pre = jnp.dot(
        normed_mlp, up_weight, preferred_element_type=jnp.float32
    ) + up_bias.astype(jnp.float32)
    hidden = jax.nn.gelu(hidden_pre, approximate=False).astype(jnp.bfloat16)
    mlp_branch = jnp.dot(
        hidden, down_weight, preferred_element_type=jnp.float32
    ) + down_bias.astype(jnp.float32)
    output = (token_rows + attn_branch + mlp_branch).astype(jnp.bfloat16).reshape(tokens.shape)
    attn_gain, mlp_gain, qkv_weight, out_weight, up_weight, down_weight = (
        lax.all_gather(norm1_gain, "dp", axis=0, tiled=True),
        lax.all_gather(norm2_gain, "dp", axis=0, tiled=True),
        lax.all_gather(w_qkv, "dp", axis=0, tiled=True),
        lax.all_gather(w_out, "dp", axis=0, tiled=True),
        lax.all_gather(w_up, "dp", axis=0, tiled=True),
        lax.all_gather(w_down, "dp", axis=0, tiled=True),
    )
    grad_rows = cotangent.reshape(row_count, width)
    grad_wide = grad_rows.astype(jnp.float32)
    hidden_grad = contract_cols(grad_rows, down_weight)
    unused, gelu_pull = jax.vjp(
        lambda pre_value: jax.nn.gelu(pre_value, approximate=False), hidden_pre
    )
    pre_grad = gelu_pull(hidden_grad)[0].astype(jnp.bfloat16)
    normed_mlp_grad = contract_cols(pre_grad, up_weight)
    mlp_in_grad, mlp_gain_grad, mlp_shift_grad = norm_grads(
        token_rows, mlp_gain.astype(jnp.float32), mlp_shift.astype(jnp.float32), normed_mlp_grad
    )
    mlp_terms = (
        contract_rows(normed_mlp, pre_grad),
        jnp.sum(pre_grad.astype(jnp.float32), axis=0),
        contract_rows(hidden, grad_rows),
        jnp.sum(grad_wide, axis=0),
        mlp_gain_grad,
        mlp_shift_grad,
    )
    mlp_shares = (
        lax.psum_scatter(
            mlp_terms[0].astype(jnp.bfloat16), "dp", scatter_dimension=0, tiled=True
        ).astype(jnp.float32),
        lax.psum_scatter(
            mlp_terms[1].astype(jnp.bfloat16), "dp", scatter_dimension=0, tiled=True
        ).astype(jnp.float32),
        lax.psum_scatter(
            mlp_terms[2].astype(jnp.bfloat16), "dp", scatter_dimension=0, tiled=True
        ).astype(jnp.float32),
        lax.psum_scatter(
            mlp_terms[3].astype(jnp.bfloat16), "dp", scatter_dimension=0, tiled=True
        ).astype(jnp.float32),
        lax.psum_scatter(
            mlp_terms[4].astype(jnp.bfloat16), "dp", scatter_dimension=0, tiled=True
        ).astype(jnp.float32),
        lax.psum_scatter(
            mlp_terms[5].astype(jnp.bfloat16), "dp", scatter_dimension=0, tiled=True
        ).astype(jnp.float32),
    )
    mixed_grad = contract_cols(grad_rows, out_weight).astype(jnp.bfloat16).reshape(head_shape)
    again_scores = (
        jnp.einsum("sqhd,skhd->shqk", queries, key_heads, preferred_element_type=jnp.float32)
        * score_scale
    )
    again_scores = jnp.where(allowed, again_scores, MASK_FILL)
    attn_prob = jnp.exp(again_scores - log_norm)
    prob_again = attn_prob.astype(jnp.bfloat16)
    prob_grad = jnp.einsum(
        "sqhd,skhd->shqk", mixed_grad, value_heads, preferred_element_type=jnp.float32
    )
    row_dot = jnp.sum(prob_grad * attn_prob, axis=-1, keepdims=True)
    score_grad = (attn_prob * (prob_grad - row_dot)).astype(jnp.bfloat16)
    query_grad = (
        jnp.einsum("shqk,skhd->sqhd", score_grad, key_heads, preferred_element_type=jnp.float32)
        * score_scale
    )
    key_part = (
        jnp.einsum("shqk,sqhd->skhd", score_grad, queries, preferred_element_type=jnp.float32)
        * score_scale
    ).reshape(seq_dev, seq_len, width)
    value_part = jnp.einsum(
        "shqk,sqhd->skhd", prob_again, mixed_grad, preferred_element_type=jnp.float32
    ).reshape(seq_dev, seq_len, width)
    key_grad, value_grad = (
        lax.psum_scatter(
            key_part.astype(jnp.bfloat16), "ctx", scatter_dimension=1, tiled=True
        ).astype(jnp.float32),
        lax.psum_scatter(
            value_part.astype(jnp.bfloat16), "ctx", scatter_dimension=1, tiled=True
        ).astype(jnp.float32),
    )
    query_back = rotary(query_grad, own_place, -1.0).reshape(row_count, width)
    key_back = rotary(key_grad.reshape(head_shape), own_place, -1.0).reshape(row_count, width)
    proj_grad = jnp.concatenate(
        [query_back, key_back, value_grad.reshape(row_count, width)], axis=1
    ).astype(jnp.bfloat16)
    normed_attn_grad = contract_cols(proj_grad, qkv_weight)
    attn_in_grad, attn_gain_grad, attn_shift_grad = norm_grads(
        token_rows, attn_gain.astype(jnp.float32), attn_shift.astype(jnp.float32), normed_attn_grad
    )
    input_grad = (grad_wide + mlp_in_grad + attn_in_grad).astype(jnp.bfloat16).reshape(tokens.shape)
    attn_terms = (
        contract_rows(normed_attn, proj_grad),
        jnp.sum(proj_grad.astype(jnp.float32), axis=0),
        contract_rows(attn_mixed, grad_rows),
        attn_gain_grad,
        attn_shift_grad,
    )
    attn_shares = (
        lax.psum_scatter(
            attn_terms[0].astype(jnp.bfloat16), "dp", scatter_dimension=0, tiled=True
        ).astype(jnp.float32),
        lax.psum_scatter(
            attn_terms[1].astype(jnp.bfloat16), "dp", scatter_dimension=0, tiled=True
        ).astype(jnp.float32),
        lax.psum_scatter(
            attn_terms[2].astype(jnp.bfloat16), "dp", scatter_dimension=0, tiled=True
        ).astype(jnp.float32),
        lax.psum_scatter(
            attn_terms[3].astype(jnp.bfloat16), "dp", scatter_dimension=0, tiled=True
        ).astype(jnp.float32),
        lax.psum_scatter(
            attn_terms[4].astype(jnp.bfloat16), "dp", scatter_dimension=0, tiled=True
        ).astype(jnp.float32),
    )
    summed = jax.tree.map(
        lambda part: part.astype(jnp.float32), lax.psum(shortened(mlp_shares + attn_shares), "ctx")
    )
    (
        up_total,
        up_bias_total,
        down_total,
        bias_total,
        mlp_gain_total,
        mlp_shift_total,
        qkv_total,
        qkv_bias_total,
        out_total,
        attn_gain_total,
        attn_shift_total,
    ) = summed
    return (
        output,
        input_grad,
        attn_gain_total,
        attn_shift_total,
        mlp_gain_total,
        mlp_shift_total,
        qkv_total,
        qkv_bias_total,
        out_total,
        bias_total,
        up_total,
        up_bias_total,
        down_total,
        bias_total,
    )


PLANES = 4


MESH_ID = pl.DeviceIdType.MESH


def dot_nn(left, right):
    return jnp.dot(left, right, preferred_element_type=jnp.float32)


def half_turn(head, cosine, sine):
    first = head[:, :128]
    lane = lax.broadcasted_iota(jnp.int32, first.shape, 1)
    swapped = jnp.where(
        lane < ROT // 2, pltpu.roll(first, 128 - ROT // 2, 1), pltpu.roll(first, ROT // 2, 1)
    )
    return jnp.concatenate([first * cosine + swapped * sine, head[:, 128:]], axis=1)


def block_kernel(
    x_in,
    g_in,
    up_in,
    qkv_in,
    small_in,
    down,
    out_w,
    up_bias,
    frequency,
    pair,
    out_sum,
    back_sum,
    vec_all,
    small_out,
    down_tot,
    up_tot,
    outw_tot,
    qkv_tot,
    x_hbm,
    g_hbm,
    na_hbm,
    hp_hbm,
    got_down,
    got_up,
    got_outw,
    got_qkv,
    core_got,
    plane_got,
    up,
    qkv,
    gains,
    qkv_bias,
    cosine,
    sine,
    xb,
    gb,
    hx,
    half_in,
    hid,
    prg,
    q,
    k,
    v,
    mg,
    mix,
    proj,
    stat,
    kacc,
    vacc,
    acc_down,
    acc_up,
    g_down,
    g_up,
    g_outw,
    g_qkv,
    cb,
    tmp,
    vec,
    vec_got,
    line_send,
    line_recv,
    side_send,
    side_recv,
    pair_send,
    core_tok_send,
    core_tok_recv,
    w_send,
    w_recv,
    wx_send,
    wx_recv,
    wy_send,
    wy_recv,
    wc_send,
    wc_recv,
    small_send,
    small_recv,
    gather_sem,
    load_sem,
    save_sem,
    tmp_sem,
    core_send,
    core_recv,
    plane_send,
    plane_recv,
    home_send,
    home_recv,
    y_send,
    y_recv,
    x_send,
    x_recv,
    a2a_send,
    a2a_recv,
    vec_send,
    vec_recv,
    local_sem,
):
    f32, bf16 = jnp.float32, jnp.bfloat16
    dp = lax.axis_index("dp")
    rank = lax.axis_index("ctx")
    z, core = dp // 2, dp % 2
    y, x = rank // 2, rank % 2
    core_to = (2 * z + 1 - core, rank)
    x_to = (dp, 2 * y + 1 - x)
    y_to = (dp, 2 * (1 - y) + x)
    pair_to = (2 * z + 1 - core, 2 * (1 - y) + x)
    seqs, length, width = x_hbm.shape
    tok = length // 4
    ff = up.shape[2]
    row_tile = 64
    half_part = width // (4 * PLANES)
    n_dp = 2 * PLANES
    part_rows = up_in.shape[0]
    section_cols = qkv_tot.shape[1] // 3
    scale = DH ** (-0.5)
    n_qkv = 3 * DH

    barrier = pltpu.get_barrier_semaphore()
    for target in (core_to, x_to, y_to, pair_to, (dp, 3 - rank)):
        pl.semaphore_signal(barrier, inc=1, device_id=target, device_id_type=MESH_ID)
    for shift in range(1, PLANES):
        for c in range(2):
            target = (2 * lax.rem(z + shift, PLANES) + c, rank)
            pl.semaphore_signal(barrier, inc=1, device_id=target, device_id_type=MESH_ID)
    pl.semaphore_wait(barrier, 5 + 2 * (PLANES - 1))

    def ds(first, size, step=None):
        return pl.ds(pl.multiple_of(first, step or size), size)

    def remote(src, dst, send, recv, target):
        return pltpu.make_async_remote_copy(
            src_ref=src,
            dst_ref=dst,
            send_sem=send,
            recv_sem=recv,
            device_id=target,
            device_id_type=MESH_ID,
        )

    pending = []

    def start(copy, when=None):
        if when is None or when is True:
            when = None
            copy.start()
        else:
            pl.when(when)(copy.start)
        pending.append((when, copy.wait_send))

    def start_local(copy, when=None):
        if when is None:
            copy.start()
        else:
            pl.when(when)(copy.start)
        pending.append((when, copy.wait))

    one, two = ds(x * tok, tok), ds((2 + x) * tok, tok)

    arrays = ((x_in, x_hbm), (g_in, g_hbm))
    mine = 2 * core + x
    theirs = 2 * core + 1 - x
    same_row = core == y

    def block_of(a, plane, ctx):
        return arrays[a][1].at[plane, ds(ctx * tok, tok)]

    def pair_copy(a, ctx):
        return remote(
            arrays[a][0], block_of(a, z, ctx), pair_send.at[a], line_recv.at[a, z], pair_to
        )

    def own_copy(a):
        return pltpu.make_async_copy(arrays[a][0], block_of(a, z, mine), gather_sem.at[a])

    def own_start(a):
        pl.when(jnp.logical_not(same_row))(pair_copy(a, 2 * y + x).start)
        pl.when(same_row)(own_copy(a).start)

    def own_arrived(a):
        pl.when(jnp.logical_not(same_row))(pair_copy(a, mine).wait_recv)
        pl.when(same_row)(own_copy(a).wait)

    quarter = part_rows // 4
    half = part_rows // 2
    up_rows = ds(rank * quarter, quarter)
    qkv_rows = ds(y * half, half)
    peers = [(s, c) for s in range(PLANES) for c in range(2)][1:]

    def small_copy(n):
        shift, c = peers[n]
        target = (2 * lax.rem(z + shift, PLANES) + lax.rem(core + c, 2), rank)
        return remote(small_in, small_out.at[dp], small_send.at[n], small_recv.at[n], target)

    small_own = pltpu.make_async_copy(small_in, small_out.at[dp], gather_sem.at[2])

    def up_cols(target):
        return up_in.at[:, ds(target * ff, ff)]

    def qkv_cols(target, section):
        return qkv_in.at[:, ds(section * section_cols + target * DH, DH)]

    own_weights = [pltpu.make_async_copy(up_cols(dp), up.at[dp], gather_sem.at[3])]
    core_weights = [
        remote(up_cols(core_to[0]), up.at[dp], wc_send.at[0], wc_recv.at[0], core_to)
    ]
    for section in range(3):
        columns = pl.ds(section * DH, DH)
        own_weights.append(
            pltpu.make_async_copy(
                qkv_cols(dp, section), qkv.at[dp, :, columns], gather_sem.at[4 + section]
            )
        )
        core_weights.append(
            remote(
                qkv_cols(core_to[0], section),
                qkv.at[dp, :, columns],
                wc_send.at[1 + section],
                wc_recv.at[1 + section],
                core_to,
            )
        )

    up_copies = []
    qkv_copies = []
    for shift in range(1, PLANES):
        plane = lax.rem(z + shift, PLANES)
        for c in range(2):
            target = (2 * plane + c, rank)
            up_copies.append(
                remote(
                    up_in.at[up_rows, ds(target[0] * ff, ff)],
                    up.at[dp, up_rows],
                    w_send.at[shift - 1, c, 0],
                    w_recv.at[shift - 1, core, 0],
                    target,
                )
            )
            for section in range(3):
                qkv_copies.append(
                    remote(
                        qkv_in.at[qkv_rows, ds(section * section_cols + target[0] * DH, DH)],
                        qkv.at[dp, qkv_rows, pl.ds(section * DH, DH)],
                        w_send.at[shift - 1, c, 1 + section],
                        w_recv.at[shift - 1, core, 1 + section],
                        target,
                    )
                )

    def carry(a, plane, when, along):
        block = block_of(a, plane, mine)
        recv = line_recv.at[a, plane]
        if along in (0, 1):
            start(
                remote(block, block, line_send.at[a, 0, plane], recv, (dp + 2, rank)),
                jnp.logical_and(when, z < PLANES - 1),
            )
        if along in (0, -1):
            start(
                remote(block, block, line_send.at[a, 1, plane], recv, (dp - 2, rank)),
                jnp.logical_and(when, z > 0),
            )
        start(remote(block, block, side_send.at[a, plane], side_recv.at[a, plane], x_to), when)
        sems = (core_tok_send.at[a, 0, plane], core_tok_recv.at[a, 0, plane])
        start(remote(block, block, *sems, core_to), when)

    def step_blocks(step):
        blocks = []
        for along in (1, -1):
            plane = z - along * step
            there = jnp.logical_and(plane >= 0, plane < PLANES)
            blocks.append((along, lax.rem(plane + PLANES, PLANES), there))
        return blocks

    def line_step(step, a):
        for along, plane, there in step_blocks(step):
            block = block_of(a, plane, mine)
            sems = (line_send.at[a, 0, plane], line_recv.at[a, plane])
            pl.when(there)(remote(block, block, *sems, core_to).wait_recv)
            carry(a, plane, there, along)

    def side_on(a, plane, when):
        block = block_of(a, plane, theirs)
        copy = remote(block, block, side_send.at[a, plane], side_recv.at[a, plane], core_to)
        pl.when(when)(copy.wait_recv)
        sems = (core_tok_send.at[a, 1, plane], core_tok_recv.at[a, 1, plane])
        start(remote(block, block, *sems, core_to), when)

    def side_step(step, a):
        for unused, plane, there in step_blocks(step):
            side_on(a, plane, there)

    def w_arrive(shift, c, part):
        source = 2 * lax.rem(z - shift + PLANES, PLANES) + c
        if part == 0:
            dst = up.at[source, up_rows]
        else:
            dst = qkv.at[source, qkv_rows, pl.ds((part - 1) * DH, DH)]
        sems = (w_send.at[shift - 1, c, part], w_recv.at[shift - 1, c, part])
        remote(dst, dst, *sems, core_to).wait_recv()

    def pair_of(shift):
        return pl.ds(2 * lax.rem(z - shift + PLANES, PLANES), 2)

    def quarter_of(ctx):
        return ds(ctx * quarter, quarter)

    def share_up(shift):
        for c in range(2):
            w_arrive(shift, c, 0)
        block = up.at[pair_of(shift), up_rows]
        start(remote(block, block, wx_send.at[shift - 1], wx_recv.at[shift - 1], x_to))
        start(remote(block, block, wy_send.at[shift - 1, 0], wy_recv.at[shift - 1, 0], y_to))

    def share_up_side(shift):
        block = up.at[pair_of(shift), quarter_of(2 * y + 1 - x)]
        remote(block, block, wx_send.at[shift - 1], wx_recv.at[shift - 1], x_to).wait_recv()
        start(remote(block, block, wy_send.at[shift - 1, 1], wy_recv.at[shift - 1, 1], y_to))

    def share_qkv(shift):
        for c in range(2):
            for part in range(1, 4):
                w_arrive(shift, c, part)
        block = qkv.at[pair_of(shift), qkv_rows]
        start(remote(block, block, wy_send.at[shift - 1, 2], wy_recv.at[shift - 1, 2], y_to))

    def qkv_send():
        for copy in qkv_copies:
            copy.start()

    def own_in(a):
        own_arrived(a)
        carry(a, z, True, 0)

    def up_send():
        for copy in up_copies:
            copy.start()

    def up_ready():
        for shift in range(1, PLANES):
            for n, side in enumerate((x, 1 - x)):
                block = up.at[pair_of(shift), quarter_of(2 * (1 - y) + side)]
                sems = (wy_send.at[shift - 1, n], wy_recv.at[shift - 1, n])
                remote(block, block, *sems, y_to).wait_recv()
        own_weights[0].wait()
        core_weights[0].wait()

    def qkv_ready():
        for shift in range(1, PLANES):
            block = qkv.at[pair_of(shift), ds((1 - y) * half, half)]
            sems = (wy_send.at[shift - 1, 2], wy_recv.at[shift - 1, 2])
            remote(block, block, *sems, y_to).wait_recv()
        for copy in own_weights[1:] + core_weights[1:]:
            copy.wait()

    def small_ready():
        small_own.wait()
        for n, (shift, c) in enumerate(peers):
            source = 2 * lax.rem(z - shift + PLANES, PLANES) + lax.rem(core + c, 2)
            dst = small_out.at[source]
            remote(small_in, dst, small_send.at[n], small_recv.at[n], core_to).wait()
        for i in range(4):
            for d in range(n_dp):
                gains[i : i + 1, d * part_rows : (d + 1) * part_rows] = small_out[d, i : i + 1, :]
        for section in range(3):
            block = n_dp * section + dp
            source, row = block // 3, 6 + lax.rem(block, 3)
            qkv_bias[:, section * DH : (section + 1) * DH] = small_out[source, pl.ds(row, 1), :]

    toward = jnp.where(z < PLANES // 2, 1, -1)
    far = jnp.where(z < PLANES // 2, PLANES - 1, 0)
    near = z + toward
    feed_order = (z, near, 6 - z - near - far, far)

    def array_ready(a, j):
        for n, side in enumerate((x, 1 - x)):
            block = block_of(a, feed_order[j], 2 * (1 - core) + side)
            sems = (
                core_tok_send.at[a, n, feed_order[j]],
                core_tok_recv.at[a, n, feed_order[j]],
            )
            remote(block, block, *sems, core_to).wait_recv()
        load(feed_order[j], j % 2)[a].start()

    own_start(0)
    own_start(1)
    small_own.start()
    for n in range(len(peers)):
        small_copy(n).start()
    for copy in own_weights + core_weights:
        copy.start()

    def load(s, slot):
        return (
            pltpu.make_async_copy(x_hbm.at[s], xb.at[slot], load_sem.at[0, slot]),
            pltpu.make_async_copy(g_hbm.at[s], gb.at[slot], load_sem.at[1, slot]),
        )

    def save_norm(s):
        return pltpu.make_async_copy(hx.at[1], na_hbm.at[s], save_sem.at[0])

    def save_rows(s):
        copies = []
        for n, (ref, cols) in enumerate(((hid, pl.ds(0, ff)), (prg, pl.ds(ff, ff)))):
            for h, rows in enumerate((one, two)):
                copies.append(
                    pltpu.make_async_copy(
                        ref.at[rows],
                        hp_hbm.at[s, pl.ds(h * tok, tok), cols],
                        save_sem.at[1 + 2 * n + h],
                    )
                )
        return copies

    def clear(ref):
        @pl.loop(0, ref.shape[0] // 64)
        def rows(i):
            ref[ds(i * 64, 64), :] = jnp.zeros((64, ref.shape[1]), f32)

    def choose_half(src, slot):
        for d in range(width // 256):
            half_in[:, d * 128 : (d + 1) * 128] = src[slot, :, ds(d * 256 + x * 128, 128)]

    def feed(slot, tile):
        c = ds(tile * 256, 256)
        columns = up[:, :, c].reshape(width, 256)
        pre = dot_nn(hx[0], columns) + up_bias[:, c].astype(f32)
        hidden_grad = contract_cols(gb[slot], down[c, :])
        cdf = 0.5 * (1.0 + lax.erf(pre * (0.5**0.5)))
        pdf = jnp.exp(-0.5 * pre * pre) * ((2.0 * 3.141592653589793) ** -0.5)
        hid[:, c] = (pre * cdf).astype(bf16)
        prg[:, c] = (hidden_grad * (cdf + pre * pdf)).astype(bf16)

    def feed_down(slot, m):
        r = ds(m * 256, 256)
        acc_down[r, :] += contract_rows(hid[:, ds(x * (ff // 2) + m * 256, 256)], gb[slot])

    def feed_forward(j, tick):
        s = feed_order[j]
        slot = j % 2
        load(s, slot)[0].wait()
        if j > 0:
            save_norm(feed_order[j - 1]).wait()
            for copy in save_rows(feed_order[j - 1]):
                copy.wait()

        @pl.loop(0, length // row_tile)
        def norm(i):
            r = ds(i * row_tile, row_tile)
            value = xb[slot, r, :].astype(f32)
            centre = value - jnp.mean(value, axis=1, keepdims=True)
            inv = lax.rsqrt(jnp.mean(centre * centre, axis=1, keepdims=True) + EPS_NORM)
            hat = centre * inv
            hx[1, r, :] = (hat * gains[0:1, :] + gains[1:2, :]).astype(bf16)
            hx[0, r, :] = (hat * gains[2:3, :] + gains[3:4, :]).astype(bf16)

        save_norm(s).start()
        choose_half(hx, 0)
        tick(j, 0)
        load(s, slot)[1].wait()

        @pl.loop(0, 2)
        def first_tiles(m):
            feed(slot, 2 * x + m)
            feed_down(slot, m)

        if j == seqs - 1:
            rounded(g_down, acc_down, g_down.shape[0], width)
            y_copy(0, 0).start()
        tick(j, 1)

        @pl.loop(0, 2)
        def last_tiles(m):
            feed(slot, 2 * (1 - x) + m)

        for copy in save_rows(s):
            copy.start()
        tick(j, 2)

        @pl.loop(0, width // 512)
        def gup(m):
            r = ds(m * 256, 256)
            acc_up[r, :] += contract_rows(half_in[:, r], prg[...])

        rows_sum = jnp.sum(prg[one, :].astype(f32), axis=0, keepdims=True)
        rows_sum += jnp.sum(prg[two, :].astype(f32), axis=0, keepdims=True)
        vec[6:7, 0:ff] += rows_sum
        tick(j, 3)

    def add_rows(dst, src, rows):
        @pl.loop(0, rows // 32)
        def tiles(i):
            r = ds(i * 32, 32)
            dst[r, :] = (dst[r, :].astype(f32) + src[r, :].astype(f32)).astype(bf16)

    def add_pieces(pieces):
        copies = []
        first = 0
        for n, (dst, src) in enumerate(pieces):
            rows, cols = dst.shape
            here = tmp.at[first : first + rows, 0:cols]
            copy = pltpu.make_async_copy(src, here, tmp_sem.at[n])
            copy.start()
            copies.append((copy, dst, here, rows))
            first += rows
        for copy, dst, here, rows in copies:
            copy.wait()
            add_rows(dst, here, rows)

    down_pieces = g_down.shape[0] // tok

    def y_copy(kind, piece):
        sems = (y_send.at[kind, piece], y_recv.at[kind, piece])
        if kind == 0:
            rows = pl.ds(piece * tok, tok)
            return remote(g_down.at[rows], got_down.at[rows], *sems, y_to)
        if kind == 1:
            return remote(g_outw, got_outw, *sems, y_to)
        src, got = (g_up, got_up) if kind == 2 else (g_qkv, got_qkv)
        pair = pl.ds(2 * lax.rem(z + piece, PLANES), 2)
        return remote(src.at[pair], got.at[pair], *sems, y_to)

    half_rows = ds(x * half_part, half_part)
    other_half = ds((1 - x) * half_part, half_part)

    def column_parts(kind, index, source):
        if kind == 2:
            return [(g_up.at[index], up_tot.at[half_rows, ds(source * ff, ff)])]
        return [
            (
                g_qkv.at[index, :, pl.ds(n * DH, DH)],
                qkv_tot.at[half_rows, ds(n * section_cols + source * DH, DH)],
            )
            for n in range(3)
        ]

    def side_parts(kind, plane, rows):
        if kind == 2:
            return [up_tot.at[rows, ds(plane * 2 * ff, 2 * ff)]]
        return [qkv_tot.at[rows, ds(n * section_cols + plane * 2 * DH, 2 * DH)] for n in range(3)]

    def reduced(kind, piece):
        y_copy(kind, piece).wait()
        if kind == 0:
            rows = pl.ds(piece * tok, tok)
            add_pieces([(g_down.at[rows], got_down.at[rows])])
            place = down_tot.at[ds(x * g_down.shape[0] + piece * tok, tok)]
            start_local(pltpu.make_async_copy(g_down.at[rows], place, local_sem.at[2 + piece]))
            start(remote(g_down.at[rows], place, x_send.at[0, piece], x_recv.at[0, piece], x_to))
            return
        if kind == 1:
            add_pieces([(g_outw, got_outw)])
            place = outw_tot.at[half_rows]
            start_local(pltpu.make_async_copy(g_outw, place, local_sem.at[6]))
            start(remote(g_outw, place, x_send.at[1, 0], x_recv.at[1, 0], x_to))
            return
        got, own = ((got_up, g_up), (got_qkv, g_qkv))[kind - 2]
        plane = lax.rem(z + piece, PLANES)
        add_pieces([(own.at[2 * plane + c], got.at[2 * plane + c]) for c in range(2)])
        for c in range(2):
            for part, (src, dst) in enumerate(column_parts(kind, 2 * plane + c, dp)):
                send = a2a_send.at[kind - 2, piece, c, part]
                recv = a2a_recv.at[kind - 2, piece, core, part]
                copy = remote(src, dst, send, recv, (2 * plane + c, rank))
                if piece == 0:
                    local = pltpu.make_async_copy(
                        src, dst, local_sem.at[7 + 3 * (kind - 2) + part]
                    )
                    pl.when(core == c)(local.start)
                    start(copy, core != c)
                else:
                    start(copy)

    def share(kind, shift):
        plane = lax.rem(z - shift + PLANES, PLANES)
        for c in range(2):
            for part, (src, dst) in enumerate(column_parts(kind, 2 * plane + c, 2 * plane + c)):
                recv = a2a_recv.at[kind - 2, shift, c, part]
                copy = remote(dst, dst, a2a_send.at[kind - 2, shift, c, part], recv, core_to)
                if shift == 0:
                    pl.when(core != c)(copy.wait_recv)
                    local = pltpu.make_async_copy(
                        src, dst, local_sem.at[7 + 3 * (kind - 2) + part]
                    )
                    pl.when(core == c)(local.wait)
                else:
                    copy.wait_recv()
        for part, block in enumerate(side_parts(kind, plane, half_rows)):
            sems = (x_send.at[kind + part, shift], x_recv.at[kind + part, shift])
            start(remote(block, block, *sems, x_to))

    order = (0, 3, 1, 2)

    def core_copy(i):
        s = order[i]
        return remote(
            cb.at[seqs + i % 2], core_got.at[s], core_send.at[i], core_recv.at[i], core_to
        )

    def chip_sum(i):
        s = order[i]
        core_copy(i).wait_recv()
        add_pieces([(cb.at[i, a], core_got.at[s, a]) for a in range(2)])
        start(flow_copy(i, 0), jnp.logical_and(z == 0, s > 0))
        start(flow_copy(i, 1), jnp.logical_and(z == PLANES - 1, s < PLANES - 1))

    def flow_copy(i, side):
        s = order[i]
        sems = (plane_send.at[i], plane_recv.at[side, s])
        return remote(cb.at[i], plane_got.at[side, s], *sems, (dp + (2, -2)[side], rank))

    def flow_add(i, side):
        flow_copy(i, side).wait_recv()
        add_pieces([(cb.at[i, a], plane_got.at[side, order[i], a]) for a in range(2)])

    def flow_relay(i, hop):
        s = order[i]
        for side, plane in enumerate((hop, PLANES - 1 - hop)):
            if (plane < s) if side == 0 else (plane > s):
                here = z == plane
                pl.when(here)(functools.partial(flow_add, i, side))
                start(flow_copy(i, side), here)

    def flow_end(i):
        s = order[i]

        @pl.when(z == s)
        def both():
            if s > 0:
                flow_add(i, 0)
            if s < PLANES - 1:
                flow_add(i, 1)

        same = core == y
        for a, result in enumerate((out_sum, back_sum)):
            block = cb.at[i, a]
            start_local(
                pltpu.make_async_copy(block, result, local_sem.at[a]),
                jnp.logical_and(z == s, same),
            )
            start(
                remote(block, result, home_send.at[a], home_recv.at[a], pair_to),
                jnp.logical_and(z == s, jnp.logical_not(same)),
            )

    def rounded(dst, src, rows, cols):
        @pl.loop(0, rows // 64)
        def tiles(i):
            r = ds(i * 64, 64)
            dst[r, :] = src[r, 0:cols].astype(bf16)

    def rounded_columns(dst, src, cols):
        @pl.loop(0, dst.shape[0])
        def blocks(d):
            dst[d] = src[ds(d * half_part, half_part), 0:cols].astype(bf16)

    def place_of(first, within):
        block = jnp.where(within < tok // 2, first, 2 * 4 - 1 - first)
        return block * (tok // 2) + lax.bitwise_and(within, tok // 2 - 1)

    def place_q(part):
        return place_of(pair[part], lax.broadcasted_iota(jnp.int32, (tok, 1), 0))

    column = lax.broadcasted_iota(jnp.int32, (1, length), 1)
    firsts = jnp.where(column < tok, pair[0], pair[1])
    firsts = jnp.where(column < 2 * tok, firsts, jnp.where(column < 3 * tok, pair[2], pair[3]))
    place_k = place_of(firsts, lax.bitwise_and(column, tok - 1))

    def load_again(i, slot):
        s = order[i]
        copies = [
            pltpu.make_async_copy(na_hbm.at[s], xb.at[slot], load_sem.at[0, slot]),
            pltpu.make_async_copy(g_hbm.at[s], gb.at[slot], load_sem.at[1, slot]),
            pltpu.make_async_copy(
                hp_hbm.at[s], hx.at[slot, pl.ds(2 * tok, 2 * tok)], load_sem.at[2, slot]
            ),
        ]
        for h, rows in enumerate((one, two)):
            copies.append(
                pltpu.make_async_copy(
                    x_hbm.at[s, rows],
                    hx.at[slot, pl.ds(h * tok, tok)],
                    load_sem.at[3 + h, slot],
                )
            )
        return copies

    def rotary_tables():
        lane = lax.broadcasted_iota(jnp.int32, (tok, 128), 1)

        @pl.loop(0, 4)
        def tables(part):
            r = ds(part * tok, tok)
            angle = place_q(part).astype(f32) * frequency[...]
            turns = jnp.floor(angle * (0.5 / 3.141592653589793) + 0.5)
            angle = (angle - turns * 6.28125) - turns * 0.0019353071795864769
            cosine[r, :] = jnp.where(lane < ROT, jnp.cos(angle), 1.0)
            sine_part = jnp.where(lane < ROT // 2, -jnp.sin(angle), jnp.sin(angle))
            sine[r, :] = jnp.where(lane < ROT, sine_part, 0.0)

    feed_plan = {
        (0, 0): [(share_up_side, 2), (side_on, 1, z, True), (share_up_side, 1), (line_step, 2, 0), (array_ready, 1, 0), (side_step, 1, 0), (rotary_tables,), (up_ready,), (array_ready, 0, 1)],
        (0, 1): [(line_step, 2, 1), (qkv_send,)],
        (0, 3): [(side_step, 1, 1)],
        (1, 0): [(array_ready, 1, 1), (line_step, 3, 0)],
        (1, 2): [(side_step, 2, 0)],
        (1, 3): [(array_ready, 0, 2)],
        (2, 0): [(side_step, 3, 0), (share_qkv, 3), (array_ready, 0, 3), (line_step, 3, 1), (side_step, 2, 1), (array_ready, 1, 2)],
        (2, 2): [(share_qkv, 1)],
        (2, 3): [(side_step, 3, 1)],
        (3, 0): [(array_ready, 1, 3)],
        (3, 1): [(share_qkv, 2)],
    }

    def feed_tick(j, point):
        for step, *which in feed_plan.get((j, point), ()):
            step(*which)

    clear(acc_down)
    clear(acc_up)
    vec[...] = jnp.zeros_like(vec)
    for step, *which in (
        (up_send,),
        (own_in, 0),
        (own_in, 1),
        (side_on, 0, z, True),
        (share_up, 3),
        (array_ready, 0, 0),
        (share_up, 2),
        (share_up_side, 3),
        (share_up, 1),
        (line_step, 1, 0),
        (line_step, 1, 1),
    ):
        step(*which)
    small_ready()
    for j in range(seqs):
        feed_forward(j, feed_tick)
    save_norm(feed_order[-1]).wait()
    for copy in save_rows(feed_order[-1]):
        copy.wait()

    for copy in load_again(0, 0):
        copy.start()
    rounded_columns(g_up, acc_up, ff)
    for kind, piece in ((2, 3), (2, 2), (2, 1), (0, 1), (0, 2), (2, 0), (0, 3)):
        y_copy(kind, piece).start()
    clear(acc_up)
    clear(acc_down.at[0:tok])
    qkv_ready()

    def attention(i, tick):
        slot = i % 2
        for copy in load_again(i, slot):
            copy.wait()
        if i + 1 < seqs:
            for copy in load_again(i + 1, 1 - slot):
                copy.start()
        tick(i, 0)
        choose_half(xb, slot)
        for n, ref in enumerate((q, k, v)):
            c = slice(n * DH, (n + 1) * DH)
            columns = qkv[:, :, c].reshape(width, DH)
            part = dot_nn(xb[slot], columns) + qkv_bias[:, c]
            if n < 2:
                part = half_turn(part, cosine[...], sine[...])
            ref[...] = part.astype(bf16)
        mg[...] = contract_cols(gb[slot], out_w[...]).astype(bf16)
        tick(i, 1)
        kacc[...] = jnp.zeros_like(kacc)
        vacc[...] = jnp.zeros_like(vacc)

        @pl.loop(0, 4)
        def attend(part):
            r = ds(part * tok, tok)
            scores = contract_cols(q[r, :], k[...]) * scale
            scores = jnp.where(place_k <= place_q(part), scores, MASK_FILL)
            exponent = jnp.exp(scores - jnp.max(scores, axis=1, keepdims=True))
            prob = exponent / jnp.sum(exponent, axis=1, keepdims=True)
            low = prob.astype(bf16)
            mix[r, :] = dot_nn(low, v[...]).astype(bf16)
            prob_grad = contract_cols(mg[r, :], v[...])
            row_dot = jnp.sum(prob_grad * prob, axis=1, keepdims=True)
            score_grad = (prob * (prob_grad - row_dot)).astype(bf16)
            query_grad = dot_nn(score_grad, k[...]) * scale
            proj[r, 0:DH] = half_turn(query_grad, cosine[r, :], -sine[r, :]).astype(bf16)
            kacc[...] += contract_rows(score_grad, q[r, :])
            vacc[...] += contract_rows(low, mg[r, :])

        proj[:, DH : 2 * DH] = half_turn(kacc[...] * scale, cosine[...], -sine[...]).astype(bf16)
        proj[:, 2 * DH : 3 * DH] = vacc[...].astype(bf16)
        tick(i, 2)
        acc_down[0:tok, :] += contract_rows(mix[:, ds(x * 128, 128)], gb[slot])

        @pl.loop(0, width // 512)
        def gqkv(m):
            r = ds(m * 256, 256)
            acc_up[r, 0:n_qkv] += contract_rows(half_in[:, r], proj[...])

        tick(i, 3)
        value = hx[slot, 0 : 2 * tok, :].astype(f32)
        mean = jnp.mean(value, axis=1, keepdims=True)
        centre = value - mean
        stat[0] = mean
        stat[1] = lax.rsqrt(jnp.mean(centre * centre, axis=1, keepdims=True) + EPS_NORM)
        if i >= 2:
            core_copy(i - 2).wait_send()

        def picked(ref):
            return jnp.concatenate([ref[one, :], ref[two, :]], axis=0)

        place = [jnp.where(core == h, i, seqs + i % 2) for h in range(2)]
        later = slice(2 * tok, 4 * tok)

        @pl.loop(0, width // 256)
        def followers(n):
            c = ds(n * 256, 256)
            out = dot_nn(hx[slot, later, 0:ff], down[:, c]) + dot_nn(picked(mix), out_w[:, c])
            mlp_back = contract_cols(hx[slot, later, ff : 2 * ff], up[n])
            attn_back = contract_cols(picked(proj), qkv[n])
            back = attn_back * gains[0:1, c] + mlp_back * gains[2:3, c]
            for h in range(2):
                rows = slice(h * tok, (h + 1) * tok)
                cb[place[h], 0, :, c] = out[rows].astype(bf16)
                cb[place[h], 1, :, c] = back[rows].astype(bf16)
            hat = (hx[slot, 0 : 2 * tok, c].astype(f32) - stat[0]) * stat[1]
            grad = jnp.concatenate([gb[slot, one, c], gb[slot, two, c]], axis=0).astype(f32)
            sums = (attn_back * hat, attn_back, mlp_back * hat, mlp_back, grad)
            for n_sum, term in enumerate(sums):
                vec[n_sum : n_sum + 1, c] += jnp.sum(term, axis=0, keepdims=True)

        vec[5:6, 0:n_qkv] += jnp.sum(picked(proj).astype(f32), axis=0, keepdims=True)
        core_copy(i).start()
        tick(i, 4)

    plan = {
        (0, 3): [(reduced, 0, 0), (reduced, 2, 3)],
        (1, 1): [(reduced, 2, 2)],
        (1, 4): [(reduced, 2, 1), (share, 2, 3)],
        (2, 1): [(chip_sum, 1), (chip_sum, 0)],
        (2, 2): [(share, 2, 2)],
        (3, 0): [(share, 2, 1)],
        (3, 2): [(chip_sum, 2), (flow_relay, 1, 1)],
        (3, 3): [(flow_relay, 0, 1), (reduced, 0, 1)],
    }

    def tick(i, point):
        for step, *which in plan.get((i, point), ()):
            step(*which)

    for i in range(seqs):
        attention(i, tick)

    def vec_copy(n):
        target = (dp, rank + 1 - 2 * x) if n == 0 else (dp, lax.rem(rank + 2, 4))
        if n == 2:
            target = (dp, 3 - rank)
        return remote(vec, vec_got.at[n], vec_send.at[n], vec_recv.at[n], target)

    def vec_gather():
        for n in range(3):
            vec_copy(n).wait()
        pair_sum = (vec[...] + vec_got[0], vec_got[1] + vec_got[2])
        vec_all[dp] = pair_sum[0] + pair_sum[1]
        for n, (shift, c) in enumerate(peers):
            target = (2 * lax.rem(z + shift, PLANES) + lax.rem(core + c, 2), rank)
            sems = (vec_send.at[3 + n], vec_recv.at[3 + n])
            start(remote(vec_all.at[dp], vec_all.at[dp], *sems, target))

    def send(kind, piece):
        y_copy(kind, piece).start()

    for n in range(3):
        vec_copy(n).start()
    rounded_columns(g_qkv, acc_up, n_qkv)
    rounded(g_outw, acc_down, tok, width)
    for step, *which in (
        (send, 3, 2),
        (reduced, 0, 2),
        (reduced, 0, 3),
        (reduced, 2, 0),
        (send, 3, 3),
        (send, 3, 1),
        (reduced, 3, 2),
        (share, 2, 0),
        (chip_sum, 3),
        (vec_gather,),
        (send, 3, 0),
        (flow_relay, 1, 2),
        (flow_relay, 0, 2),
        (share, 3, 2),
        (flow_relay, 2, 1),
        (reduced, 3, 1),
        (send, 1, 0),
        (reduced, 3, 0),
        (flow_relay, 3, 1),
        (share, 3, 0),
        (reduced, 1, 0),
        (reduced, 3, 3),
        (share, 3, 1),
        (flow_end, 3),
        (flow_end, 1),
        (flow_end, 2),
        (flow_end, 0),
        (share, 3, 3),
    ):
        step(*which)

    for copy in up_copies + qkv_copies:
        copy.wait_send()
    for a in range(2):
        pl.when(jnp.logical_not(same_row))(pair_copy(a, 2 * y + x).wait_send)
    for n, (shift, c) in enumerate(peers):
        source = 2 * lax.rem(z - shift + PLANES, PLANES) + lax.rem(core + c, 2)
        block = vec_all.at[source]
        remote(block, block, vec_send.at[3 + n], vec_recv.at[3 + n], core_to).wait_recv()
    for piece in range(down_pieces):
        block = down_tot.at[ds((1 - x) * g_down.shape[0] + piece * tok, tok)]
        remote(block, block, x_send.at[0, piece], x_recv.at[0, piece], x_to).wait_recv()
    block = outw_tot.at[other_half]
    remote(block, block, x_send.at[1, 0], x_recv.at[1, 0], x_to).wait_recv()
    for kind in (2, 3):
        for shift in range(PLANES):
            plane = lax.rem(z - shift + PLANES, PLANES)
            for part, block in enumerate(side_parts(kind, plane, other_half)):
                sems = (x_send.at[kind + part, shift], x_recv.at[kind + part, shift])
                remote(block, block, *sems, x_to).wait_recv()
    for a, result in enumerate((out_sum, back_sum)):
        copy = remote(result, result, home_send.at[a], home_recv.at[a], pair_to)
        pl.when(core != y)(copy.wait_recv)
    for i in range(seqs - 2, seqs):
        core_copy(i).wait_send()
    for when, wait in pending:
        if when is None:
            wait()
        else:
            pl.when(when)(wait)


def block_compute(tokens, cotangent, w_up, w_qkv, small, w_down, w_out, up_bias, pair_index):
    f32, bf16 = jnp.float32, jnp.bfloat16
    n_dp = 2 * PLANES
    tok, width = tokens.shape
    seqs, length = PLANES, 4 * tok
    part_rows = w_up.shape[0]
    ff = w_up.shape[1] // n_dp
    half_part = width // (2 * n_dp)
    frequency = ROPE_BASE ** (-2.0 * np.arange(ROT // 2, dtype=np.float32) / ROT)
    frequency = jnp.asarray(np.tile(frequency.astype(np.float32), 128 // (ROT // 2))[None, :])
    hbm = pl.BlockSpec(memory_space=pl.ANY)
    vmem = pl.BlockSpec(memory_space=pltpu.VMEM)
    dma = pltpu.SemaphoreType.DMA

    def shape(*dims, dtype=bf16):
        return jax.ShapeDtypeStruct(dims, dtype)

    def buf(*dims, dtype=bf16):
        return pltpu.VMEM(dims, dtype)

    results = pl.pallas_call(
        block_kernel,
        out_shape=(
            shape(tok, width),
            shape(tok, width),
            shape(n_dp, 8, width, dtype=f32),
            shape(n_dp, *small.shape, dtype=f32),
            shape(ff, width),
            shape(2 * half_part, n_dp * ff),
            shape(DH, width),
            shape(2 * half_part, n_dp * 3 * DH),
            shape(seqs, length, width),
            shape(seqs, length, width),
            shape(seqs, length, width),
            shape(seqs, 2 * tok, 2 * ff),
            shape(ff // 2, width),
            shape(n_dp, half_part, ff),
            shape(DH // 2, width),
            shape(n_dp, half_part, 3 * DH),
            shape(seqs, 2, tok, width),
            shape(2, seqs, 2, tok, width),
        ),
        in_specs=[hbm] * 5 + [vmem] * 4 + [pl.BlockSpec(memory_space=pltpu.SMEM)],
        out_specs=(hbm, hbm, vmem, vmem) + (hbm,) * 14,
        scratch_shapes=[
            buf(n_dp, part_rows, ff),
            buf(n_dp, part_rows, 3 * DH),
            buf(8, width, dtype=f32),
            buf(1, 3 * DH, dtype=f32),
            buf(length, 128, dtype=f32),
            buf(length, 128, dtype=f32),
            buf(2, length, width),
            buf(2, length, width),
            buf(2, length, width),
            buf(length, width // 2),
            buf(length, ff),
            buf(length, ff),
            buf(length, DH),
            buf(length, DH),
            buf(length, DH),
            buf(length, DH),
            buf(length, DH),
            buf(length, 3 * DH),
            buf(2, 2 * tok, 1, dtype=f32),
            buf(length, DH, dtype=f32),
            buf(length, DH, dtype=f32),
            buf(ff // 2, width, dtype=f32),
            buf(width // 2, ff, dtype=f32),
            buf(ff // 2, width),
            buf(n_dp, half_part, ff),
            buf(DH // 2, width),
            buf(n_dp, half_part, 3 * DH),
            buf(seqs + 2, 2, tok, width),
            buf(2 * tok, width),
            buf(8, width, dtype=f32),
            buf(3, 8, width, dtype=f32),
            dma((2, 2, PLANES)),
            dma((2, PLANES)),
            dma((2, PLANES)),
            dma((2, PLANES)),
            dma((2,)),
            dma((2, 2, PLANES)),
            dma((2, 2, PLANES)),
            dma((3, 2, 4)),
            dma((3, 2, 4)),
            dma((3,)),
            dma((3,)),
            dma((3, 3)),
            dma((3, 3)),
            dma((4,)),
            dma((4,)),
            dma((7,)),
            dma((7,)),
            dma((7,)),
            dma((5, 2)),
            dma((5,)),
            dma((2,)),
            dma((seqs,)),
            dma((seqs,)),
            dma((seqs,)),
            dma((2, seqs)),
            dma((2,)),
            dma((2,)),
            dma((4, 4)),
            dma((4, 4)),
            dma((6, 4)),
            dma((6, 4)),
            dma((2, PLANES, 2, 3)),
            dma((2, PLANES, 2, 3)),
            dma((10,)),
            dma((10,)),
            dma((13,)),
        ],
        compiler_params=pltpu.CompilerParams(
            collective_id=2, has_side_effects=True, vmem_limit_bytes=63 * 2**20
        ),
    )(
        tokens,
        cotangent,
        w_up,
        w_qkv,
        small,
        w_down,
        w_out,
        up_bias,
        frequency,
        pair_index,
    )
    return results[:8]


def finish_kernel(
    tokens,
    cotangent,
    out_sum,
    back_sum,
    small,
    down_in,
    up_in,
    outw_in,
    qkv_in,
    output,
    input_grad,
    down_out,
    up_out,
    outw_out,
    qkv_out,
):
    f32 = jnp.float32
    for src, dst in (
        (down_in, down_out),
        (up_in, up_out),
        (outw_in, outw_out),
        (qkv_in, qkv_out),
    ):
        dst[...] = src[...].astype(f32)
    bias = jnp.concatenate(
        [small[d, 4:5, :] + small[d, 5:6, :] for d in range(small.shape[0])], axis=1
    )
    value = tokens[...].astype(f32)
    output[...] = (value + out_sum[...].astype(f32) + bias).astype(output.dtype)
    centre = value - jnp.mean(value, axis=-1, keepdims=True)
    inv = lax.rsqrt(jnp.mean(centre * centre, axis=-1, keepdims=True) + EPS_NORM)
    hat = centre * inv
    back = back_sum[...].astype(f32)
    norm_back = (
        back
        - jnp.mean(back, axis=-1, keepdims=True)
        - hat * jnp.mean(back * hat, axis=-1, keepdims=True)
    ) * inv
    input_grad[...] = (cotangent[...].astype(f32) + norm_back).astype(input_grad.dtype)


def finish(tokens, cotangent, out_sum, back_sum, small, totals):
    steps = tokens.shape[0] // 16

    def rows(array):
        return pl.BlockSpec((array.shape[0] // steps, array.shape[1]), lambda i: (i, 0))

    narrow = [tokens, cotangent, out_sum, back_sum]
    whole = pl.BlockSpec(small.shape, lambda i: (0, 0, 0))
    return pl.pallas_call(
        finish_kernel,
        grid=(steps,),
        out_shape=[jax.ShapeDtypeStruct(tokens.shape, tokens.dtype)] * 2
        + [jax.ShapeDtypeStruct(total.shape, jnp.float32) for total in totals],
        in_specs=[rows(a) for a in narrow] + [whole] + [rows(a) for a in totals],
        out_specs=[rows(tokens)] * 2 + [rows(a) for a in totals],
        compiler_params=pltpu.CompilerParams(vmem_limit_bytes=62 * 2**20),
    )(*narrow, small, *totals)


def column_local(
    tokens,
    cotangent,
    pair_index,
    norm1_gain,
    norm1_bias,
    norm2_gain,
    norm2_bias,
    w_qkv,
    b_qkv,
    w_out,
    b_out,
    w_up,
    b_up,
    w_down,
    b_down,
):
    bf16, f32 = jnp.bfloat16, jnp.float32
    tok_count, width = tokens.shape[1:]
    n_dp = H
    dp_rank = lax.axis_index("dp")
    rank = lax.axis_index("ctx")
    z, core = dp_rank // 2, dp_rank % 2
    y, x = rank // 2, rank % 2
    part = width // n_dp
    ff_part = w_up.shape[1] // n_dp
    qkv_part = 3 * DH
    seq_len = 4 * tok_count

    small_row = lax.broadcasted_iota(jnp.int32, (16, part), 0)
    small = jnp.zeros((16, part), bf16)
    pieces = [norm1_gain, norm1_bias, norm2_gain, norm2_bias, b_out, b_down]
    pieces += [b_qkv[n * part : (n + 1) * part] for n in range(b_qkv.shape[0] // part)]
    for n, piece in enumerate(pieces):
        small = jnp.where(small_row == n, piece[None, :], small)
    out_sum, back_sum, vec_all, small_all, down_total, up_total, out_total, qkv_total = (
        block_compute(
            tokens[0],
            cotangent[0],
            w_up,
            w_qkv,
            small.astype(f32),
            w_down,
            w_out,
            b_up[None],
            pair_index,
        )
    )
    output, input_grad, down_total, up_total, out_total, qkv_total = finish(
        tokens[0],
        cotangent[0],
        out_sum,
        back_sum,
        small_all,
        (down_total, up_total, out_total, qkv_total),
    )
    totals = jnp.sum(vec_all[:, :4], axis=0)
    mine = lax.dynamic_slice_in_dim(totals, dp_rank * part, part, 1)
    gain1_total, shift1_total, gain2_total, shift2_total = mine
    own_vec = lax.dynamic_index_in_dim(vec_all, dp_rank, 0, keepdims=False)
    bias_total = lax.dynamic_slice_in_dim(own_vec[4], dp_rank * part, part)
    up_bias_total = own_vec[6, :ff_part]
    qkv_bias_total = vec_all[:, 5, :qkv_part].reshape(n_dp, 3, DH).swapaxes(0, 1).reshape(-1)
    qkv_bias_total = lax.dynamic_slice_in_dim(
        qkv_bias_total, dp_rank * b_qkv.shape[0], b_qkv.shape[0]
    )
    return (
        output[None],
        input_grad[None],
        gain1_total,
        shift1_total,
        gain2_total,
        shift2_total,
        qkv_total,
        qkv_bias_total,
        out_total,
        bias_total,
        up_total,
        up_bias_total,
        down_total,
        bias_total,
    )


def solution(mesh):
    local = column_local if mesh.shape["dp"] == H and mesh.shape["ctx"] == 4 else plain_local
    placed = (
        P("dp", "ctx", None),
        P("dp", "ctx", None),
        P(),
        P("dp"),
        P("dp"),
        P("dp"),
        P("dp"),
        P("dp", None),
        P("dp"),
        P("dp", None),
        P("dp"),
        P("dp", None),
        P("dp"),
        P("dp", None),
        P("dp"),
    )
    return jax.shard_map(
        local,
        mesh=mesh,
        in_specs=placed,
        out_specs=(
            P("dp", "ctx", None),
            P("dp", "ctx", None),
            P("dp"),
            P("dp"),
            P("dp"),
            P("dp"),
            P("dp", None),
            P("dp"),
            P("dp", None),
            P("dp"),
            P("dp", None),
            P("dp"),
            P("dp", None),
            P("dp"),
        ),
        check_vma=False,
    )
```
